32 devices in a mesh: ctx: 4 (over z), fsdp: 8 (over y, x, core).
Axes of the slice: x: 2, y: 2, z: 4, core: 2. Of those that a mesh axis runs over, the one named last changes fastest.
Arguments:
- tokens: bfloat16 [8, 1024, 2048], P('fsdp', 'ctx'), may hold values from -6 to 6
- cotangent: bfloat16 [8, 1024, 2048], P('fsdp', 'ctx'), may hold values from -6 to 6
- block_table: int32 [8], replicated, may hold values from 0 to 7, as said below
- gain_attn: float32 [2048], replicated, may hold values from 0.5 to 1.5
- w_query: bfloat16 [2048, 2048], P('fsdp'), may hold values from -0.125 to 0.125
- w_key: bfloat16 [2048, 256], P('fsdp'), may hold values from -0.125 to 0.125
- w_value: bfloat16 [2048, 256], P('fsdp'), may hold values from -0.125 to 0.125
- w_output: bfloat16 [2048, 2048], P(None, 'fsdp'), may hold values from -0.75 to 0.75
- gain_mlp: float32 [2048], replicated, may hold values from 0.5 to 1.5
- w_gate: bfloat16 [2048, 5632], P(None, 'fsdp'), may hold values from -0.125 to 0.125
- w_up: bfloat16 [2048, 5632], P(None, 'fsdp'), may hold values from -0.125 to 0.125
- w_down: bfloat16 [5632, 2048], P('fsdp'), may hold values from -0.078125 to 0.078125
Outputs:
- result: bfloat16 [8, 1024, 2048], P('fsdp', 'ctx')
- grad_tokens: bfloat16 [8, 1024, 2048], P('fsdp', 'ctx')
- grad_query: float32 [2048, 2048], P('fsdp')
- grad_key: float32 [2048, 256], P('fsdp')
- grad_value: float32 [2048, 256], P('fsdp')
- grad_output: float32 [2048, 2048], P(None, 'fsdp')
- grad_gate: float32 [2048, 5632], P(None, 'fsdp')
- grad_up: float32 [2048, 5632], P(None, 'fsdp')
- grad_down: float32 [5632, 2048], P('fsdp')
- grad_gain_attn: float32 [2048], replicated
- grad_gain_mlp: float32 [2048], replicated
The draws below stay inside these ranges and needn't reach their ends.
Inputs may be any that keep to these rules, and one draw needn't show every extreme that they name: `block_table`: each block number 0 to 7 stands in one slot, and the two slots 2 c and 2 c + 1 hold blocks whose numbers add up to 7.
All inputs are finite; a program needn't handle non-finite values.
Results may differ from the reference program's by a relative error of at most 0.023.
Values may be sent and summed in bfloat16 or wider, within the bound.
A program may use at most 704 MiB of HBM per device.

```python
import jax
import jax.numpy as jnp
from jax import lax

D = 2048
H = 32
KV = 4
HD = 64
FF = 5632
BLK = 128
SLOTS = 8
SEQ_LEN = 1024
SEQS = 8


def draw_block_table(key, part):
    key = jax.random.fold_in(key, 3)
    half = SLOTS // 2
    first = jax.random.permutation(key, half).astype(jnp.int32)
    flips = jax.random.randint(jax.random.fold_in(key, 11), (half,), 0, 2).astype(jnp.int32)
    mirror = (SLOTS - 1 - first).astype(jnp.int32)
    lower = jnp.where(flips == 1, mirror, first)
    upper = jnp.where(flips == 1, first, mirror)
    return jnp.stack([lower, upper], 1).reshape(-1).astype(jnp.int32)


def shard_levels(key, extent, split, low, high):
    level, own = 1.0, jax.random.fold_in(key, 6)
    for axis_at, blocks in split:
        steps = jnp.exp(jax.random.uniform(jax.random.fold_in(own, axis_at), (blocks,), jnp.float32, low / len(split), high / len(split)))
        level = level * jnp.repeat(steps, extent[axis_at] // blocks).reshape([-1 if axis == axis_at else 1 for axis in range(len(extent))])
    return level


def normal_values(key, shape, spread, bound, pieces=(), kind=jnp.bfloat16):
    entries = jax.random.normal(key, shape, jnp.float32) * spread
    if len(pieces) > 0:
        entries = shard_levels(key, shape, pieces, -0.22, 0.18) * entries
    return jnp.clip(entries, min=-bound, max=bound).astype(kind)


def setup_inputs(seed: int = 0) -> dict:
    splits = jax.random.split(jax.random.key(seed), 13)
    tokens = normal_values(splits[0], (SEQS, SEQ_LEN, D), 1.0, 6.0, ((0, 8), (1, 4)))
    cotangent = normal_values(splits[1], (SEQS, SEQ_LEN, D), 1.0, 6.0, ((0, 8), (1, 4)))
    block_table = draw_block_table(jax.random.fold_in(splits[12], 71), 0)
    gain_attn = jnp.clip(1.0 + 0.1 * jax.random.normal(splits[3], (D,), jnp.float32), 0.5, 1.5)
    w_query = normal_values(splits[4], (D, H * HD), D ** -0.5, 0.125, ((0, 8),))
    w_key = normal_values(splits[5], (D, KV * HD), D ** -0.5, 0.125, ((0, 8),))
    w_value = normal_values(splits[6], (D, KV * HD), D ** -0.5, 0.125, ((0, 8),))
    w_output = normal_values(splits[7], (H * HD, D), HD ** -0.5, 0.75, ((1, 8),))
    gain_mlp = jnp.clip(1.0 + 0.1 * jax.random.normal(splits[8], (D,), jnp.float32), 0.5, 1.5)
    w_gate = normal_values(splits[9], (D, FF), D ** -0.5, 0.125, ((1, 8),))
    w_up = normal_values(splits[10], (D, FF), D ** -0.5, 0.125, ((1, 8),))
    w_down = normal_values(splits[11], (FF, D), FF ** -0.5, 0.078125, ((0, 8),))
    return dict(tokens=tokens, cotangent=cotangent, block_table=block_table, gain_attn=gain_attn, w_query=w_query, w_key=w_key, w_value=w_value, w_output=w_output, gain_mlp=gain_mlp, w_gate=w_gate, w_up=w_up, w_down=w_down)


EPSILON = 1e-05
NEGATIVE = -1e+30

def matmul(left, right):
    return jnp.dot(left, right, preferred_element_type=jnp.float32)

def angles(positions, width):
    freqs = 10000.0 ** (-jnp.arange(width // 2, dtype=jnp.float32) / (width // 2))
    turns = positions.astype(jnp.float32)[:, None] * freqs[None, :]
    turns = jnp.concatenate([turns, turns], -1)
    return (jnp.cos(turns)[:, None, :], jnp.sin(turns)[:, None, :])

def rotary(values, cosine, sine):
    middle = values.shape[-1] // 2
    turned = jnp.concatenate([-values[..., middle:], values[..., :middle]], -1)
    return values * cosine + turned * sine

def normed(hidden, gain):
    factor = lax.rsqrt(lax.optimization_barrier(jnp.mean(hidden * hidden, -1, keepdims=True)) + EPSILON)
    unit = hidden * factor
    return (unit, factor, (unit * gain).astype(jnp.bfloat16))

def normed_back(unit, factor, grad_in, gain):
    scaled = grad_in * gain
    return factor * (scaled - unit * lax.optimization_barrier(jnp.mean(scaled * unit, -1, keepdims=True)))

def split_heads(array, groups):
    count, heads, width = array.shape
    return array.reshape(count, groups, heads // groups, width).transpose(1, 0, 2, 3)

def join_heads(array):
    groups, count, inner, width = array.shape
    return array.transpose(1, 0, 2, 3).reshape(count, groups * inner, width)

def attend(queries, keys_all, values_all, positions):
    scale = queries.shape[-1] ** (-0.5)
    allowed = positions[:, None] >= positions[None, :]
    q_split = split_heads(queries, KV)
    k_split = keys_all.transpose(1, 0, 2)
    v_split = values_all.transpose(1, 0, 2)

    def single(item):
        q_part, k_part, v_part = item
        scores = jnp.einsum('rgd,ld->grl', q_part.astype(jnp.float32), k_part.astype(jnp.float32)) * scale
        scores = jnp.where(allowed[None], scores, NEGATIVE)
        peak = lax.optimization_barrier(jnp.max(scores, -1, keepdims=True))
        logsum = peak + jnp.log(lax.optimization_barrier(jnp.sum(jnp.exp(scores - peak), -1, keepdims=True)))
        probs = jnp.exp(scores - logsum).astype(jnp.bfloat16)
        mixed = jnp.einsum('grl,ld->rgd', probs.astype(jnp.float32), v_part.astype(jnp.float32))
        return (mixed.astype(jnp.bfloat16), logsum)
    mixed, logsum = lax.map(single, (q_split, k_split, v_split))
    return (join_heads(mixed), logsum)

def attend_back(queries, keys_all, values_all, mixed, grad_mixed, logsum, positions):
    scale = queries.shape[-1] ** (-0.5)
    allowed = positions[:, None] >= positions[None, :]
    q_split = split_heads(queries, KV)
    o_split = split_heads(mixed, KV)
    g_split = split_heads(grad_mixed, KV)
    k_split = keys_all.transpose(1, 0, 2)
    v_split = values_all.transpose(1, 0, 2)

    def single(item):
        q_part, k_part, v_part, o_part, g_part, l_part = item
        q_wide = q_part.astype(jnp.float32)
        k_wide = k_part.astype(jnp.float32)
        g_wide = g_part.astype(jnp.float32)
        scores = jnp.einsum('rgd,ld->grl', q_wide, k_wide) * scale
        scores = jnp.where(allowed[None], scores, NEGATIVE)
        probs = jnp.exp(scores - l_part)
        rounded = probs.astype(jnp.bfloat16).astype(jnp.float32)
        dprob = jnp.einsum('rgd,ld->grl', g_wide, v_part.astype(jnp.float32))
        delta = lax.optimization_barrier(jnp.sum(g_wide * o_part.astype(jnp.float32), -1)).T[:, :, None]
        dscore = (probs * (dprob - delta) * scale).astype(jnp.bfloat16).astype(jnp.float32)
        grad_q = jnp.einsum('grl,ld->rgd', dscore, k_wide)
        grad_k = jnp.einsum('grl,rgd->ld', dscore, q_wide)
        grad_v = jnp.einsum('grl,rgd->ld', rounded, g_wide)
        return (grad_q, grad_k, grad_v)
    grad_q, grad_k, grad_v = lax.map(single, (q_split, k_split, v_split, o_split, g_split, logsum))
    return (join_heads(grad_q), grad_k.transpose(1, 0, 2), grad_v.transpose(1, 0, 2))

def one_sequence(rows_in, grad_out, positions, gain_attn, w_query, w_key, w_value, w_output, gain_mlp, w_gate, w_up, w_down):
    count = rows_in.shape[0]
    cosine, sine = angles(positions, HD)
    inputs = rows_in.astype(jnp.float32)
    unit_one, factor_one, normal_one = normed(inputs, gain_attn)
    queries = rotary(matmul(normal_one, w_query).reshape(count, H, HD), cosine, sine).astype(jnp.bfloat16)
    keys_all = rotary(matmul(normal_one, w_key).reshape(count, KV, HD), cosine, sine).astype(jnp.bfloat16)
    values_all = matmul(normal_one, w_value).astype(jnp.bfloat16).reshape(count, KV, HD)
    mixed, logsum = attend(queries, keys_all, values_all, positions)
    mixed_flat = mixed.reshape(count, H * HD)
    hidden_one = inputs + matmul(mixed_flat, w_output)
    unit_two, factor_two, normal_two = normed(hidden_one, gain_mlp)
    gate = matmul(normal_two, w_gate)
    up = matmul(normal_two, w_up)
    sigma = jax.nn.sigmoid(gate)
    activated = gate * sigma
    hidden = (activated * up).astype(jnp.bfloat16)
    result = (hidden_one + matmul(hidden, w_down)).astype(jnp.bfloat16)
    grad_down = matmul(hidden.T, grad_out)
    grad_hidden = matmul(grad_out, w_down.T)
    grad_gate_in = (grad_hidden * up * sigma * (1.0 + gate * (1.0 - sigma))).astype(jnp.bfloat16)
    grad_up_in = (grad_hidden * activated).astype(jnp.bfloat16)
    grad_gate = matmul(normal_two.T, grad_gate_in)
    grad_up = matmul(normal_two.T, grad_up_in)
    grad_normal_two = matmul(grad_gate_in, w_gate.T) + matmul(grad_up_in, w_up.T)
    grad_gain_mlp = lax.optimization_barrier(jnp.sum(grad_normal_two * unit_two, 0))
    grad_hidden_one = grad_out.astype(jnp.float32) + normed_back(unit_two, factor_two, grad_normal_two, gain_mlp)
    grad_mixed_in = grad_hidden_one.astype(jnp.bfloat16)
    grad_output = matmul(mixed_flat.T, grad_mixed_in)
    grad_mixed = matmul(grad_mixed_in, w_output.T).astype(jnp.bfloat16).reshape(count, H, HD)
    grad_q, grad_k, grad_v = attend_back(queries, keys_all, values_all, mixed, grad_mixed, logsum, positions)
    grad_queries = rotary(grad_q, cosine, -sine).astype(jnp.bfloat16).reshape(count, H * HD)
    grad_keys = rotary(grad_k, cosine, -sine).astype(jnp.bfloat16).reshape(count, KV * HD)
    grad_values = grad_v.astype(jnp.bfloat16).reshape(count, KV * HD)
    grad_query = matmul(normal_one.T, grad_queries)
    grad_key = matmul(normal_one.T, grad_keys)
    grad_value = matmul(normal_one.T, grad_values)
    grad_normal_one = matmul(grad_queries, w_query.T) + matmul(grad_keys, w_key.T) + matmul(grad_values, w_value.T)
    grad_gain_attn = lax.optimization_barrier(jnp.sum(grad_normal_one * unit_one, 0))
    grad_tokens = (grad_hidden_one + normed_back(unit_one, factor_one, grad_normal_one, gain_attn)).astype(jnp.bfloat16)
    sums = (grad_query, grad_key, grad_value, grad_output, grad_gate, grad_up, grad_down, grad_gain_attn, grad_gain_mlp)
    return (result, grad_tokens, sums)

def reference(tokens, cotangent, block_table, gain_attn, w_query, w_key, w_value, w_output, gain_mlp, w_gate, w_up, w_down):
    offsets = jnp.arange(BLK, dtype=jnp.int32)
    positions = (block_table[:, None] * BLK + offsets[None, :]).reshape(-1).astype(jnp.int32)
    start = (jnp.zeros((D, H * HD), jnp.float32), jnp.zeros((D, KV * HD), jnp.float32), jnp.zeros((D, KV * HD), jnp.float32), jnp.zeros((H * HD, D), jnp.float32), jnp.zeros((D, FF), jnp.float32), jnp.zeros((D, FF), jnp.float32), jnp.zeros((FF, D), jnp.float32), jnp.zeros((D,), jnp.float32), jnp.zeros((D,), jnp.float32))

    def step(carry, item):
        rows_in, grad_out = item
        result, grad_tokens, sums = one_sequence(rows_in, grad_out, positions, gain_attn, w_query, w_key, w_value, w_output, gain_mlp, w_gate, w_up, w_down)
        carry = tuple((total + part for total, part in zip(carry, sums)))
        return (carry, (result, grad_tokens))
    totals, outputs = lax.scan(step, start, (tokens, cotangent))
    return (outputs[0], outputs[1], totals[0], totals[1], totals[2], totals[3], totals[4], totals[5], totals[6], totals[7], totals[8])
```

```python
import jax
import jax.numpy as jnp
from jax import lax
from jax.sharding import PartitionSpec as P

H = 32
KV = 4
HD = 64


EPSILON = 1e-05
NEGATIVE = -1e30


def matmul(left, right):
    return jnp.dot(left, right, preferred_element_type=jnp.float32)


def across(left, right):
    return lax.dot_general(
        left, right, (((0,), (0,)), ((), ())), preferred_element_type=jnp.float32
    )


def through(left, right):
    return lax.dot_general(
        left, right, (((1,), (1,)), ((), ())), preferred_element_type=jnp.float32
    )


def angles(positions, width):
    freqs = 10000.0 ** (-jnp.arange(width // 2, dtype=jnp.float32) / (width // 2))
    turns = positions.astype(jnp.float32)[:, None] * freqs[None, :]
    turns = jnp.concatenate([turns, turns], -1)
    return (jnp.cos(turns)[:, None, :], jnp.sin(turns)[:, None, :])


def rotary(values, cosine, sine):
    middle = values.shape[-1] // 2
    turned = jnp.concatenate([-values[..., middle:], values[..., :middle]], -1)
    return values * cosine + turned * sine


def normed(hidden, gain):
    factor = lax.rsqrt(jnp.mean(hidden * hidden, -1, keepdims=True) + EPSILON)
    unit = hidden * factor
    return (unit, factor, (unit * gain).astype(jnp.bfloat16))


def normed_back(unit, factor, grad_in, gain):
    scaled = grad_in * gain
    return factor * (scaled - unit * jnp.mean(scaled * unit, -1, keepdims=True))


def split_heads(array, groups):
    count, heads, width = array.shape
    return array.reshape(count, groups, heads // groups, width).transpose(1, 0, 2, 3)


def join_heads(array):
    groups, count, inner, width = array.shape
    return array.transpose(1, 0, 2, 3).reshape(count, groups * inner, width)


def attend(queries, keys_all, values_all, pos_rows, pos_keys):
    scale = queries.shape[-1] ** (-0.5)
    allowed = pos_rows[:, None] >= pos_keys[None, :]
    q_split = split_heads(queries, KV)
    k_split = keys_all.transpose(1, 0, 2)
    v_split = values_all.transpose(1, 0, 2)

    def single(item):
        q_part, k_part, v_part = item
        scores = (
            jnp.einsum("rgd,ld->grl", q_part, k_part, preferred_element_type=jnp.float32) * scale
        )
        scores = jnp.where(allowed[None], scores, NEGATIVE)
        peak = jnp.max(scores, -1, keepdims=True)
        logsum = peak + jnp.log(jnp.sum(jnp.exp(scores - peak), -1, keepdims=True))
        probs = jnp.exp(scores - logsum).astype(jnp.bfloat16)
        mixed = jnp.einsum("grl,ld->rgd", probs, v_part, preferred_element_type=jnp.float32)
        return (mixed.astype(jnp.bfloat16), logsum)

    mixed, logsum = lax.map(single, (q_split, k_split, v_split))
    return (join_heads(mixed), logsum)


def attend_back(queries, keys_all, values_all, mixed, grad_mixed, logsum, pos_rows, pos_keys):
    scale = queries.shape[-1] ** (-0.5)
    allowed = pos_rows[:, None] >= pos_keys[None, :]
    q_split = split_heads(queries, KV)
    o_split = split_heads(mixed, KV)
    g_split = split_heads(grad_mixed, KV)
    k_split = keys_all.transpose(1, 0, 2)
    v_split = values_all.transpose(1, 0, 2)

    def single(item):
        q_part, k_part, v_part, o_part, g_part, l_part = item
        scores = (
            jnp.einsum("rgd,ld->grl", q_part, k_part, preferred_element_type=jnp.float32) * scale
        )
        scores = jnp.where(allowed[None], scores, NEGATIVE)
        probs = jnp.exp(scores - l_part)
        rounded = probs.astype(jnp.bfloat16)
        dprob = jnp.einsum("rgd,ld->grl", g_part, v_part, preferred_element_type=jnp.float32)
        delta = jnp.sum(g_part.astype(jnp.float32) * o_part.astype(jnp.float32), -1).T[:, :, None]
        dscore = (probs * (dprob - delta) * scale).astype(jnp.bfloat16)
        grad_q = jnp.einsum("grl,ld->rgd", dscore, k_part, preferred_element_type=jnp.float32)
        grad_k = jnp.einsum("grl,rgd->ld", dscore, q_part, preferred_element_type=jnp.float32)
        grad_v = jnp.einsum("grl,rgd->ld", rounded, g_part, preferred_element_type=jnp.float32)
        return (grad_q, grad_k, grad_v)

    grad_q, grad_k, grad_v = lax.map(single, (q_split, k_split, v_split, o_split, g_split, logsum))
    return (join_heads(grad_q), grad_k.transpose(1, 0, 2), grad_v.transpose(1, 0, 2))


def gate_back(grad_hidden, gate, up):
    sigma = jax.nn.sigmoid(gate)
    activated = gate * sigma
    grad_gate_in = (grad_hidden * up * sigma * (1.0 + gate * (1.0 - sigma))).astype(jnp.bfloat16)
    grad_up_in = (grad_hidden * activated).astype(jnp.bfloat16)
    return (grad_gate_in, grad_up_in)


def shards(
    tokens,
    cotangent,
    block_table,
    gain_attn,
    w_query,
    w_key,
    w_value,
    w_output,
    gain_mlp,
    w_gate,
    w_up,
    w_down,
):
    rows_in = tokens[0]
    grad_out = cotangent[0]
    count = rows_in.shape[0]
    block = count // 2
    ctx_index = lax.axis_index("ctx")
    offsets = jnp.arange(block, dtype=jnp.int32)
    owned = lax.dynamic_slice_in_dim(block_table, 2 * ctx_index, 2)
    pos_rows = (owned[:, None] * block + offsets[None, :]).reshape(-1)
    pos_keys = (block_table[:, None] * block + offsets[None, :]).reshape(-1)
    cosine, sine = angles(pos_rows, HD)
    full_query, full_key, full_value, full_output = (
        lax.all_gather(w_query, "fsdp", axis=0, tiled=True),
        lax.all_gather(w_key, "fsdp", axis=0, tiled=True),
        lax.all_gather(w_value, "fsdp", axis=0, tiled=True),
        lax.all_gather(w_output, "fsdp", axis=1, tiled=True),
    )
    inputs = rows_in.astype(jnp.float32)
    unit_one, factor_one, normal_one = normed(inputs, gain_attn)
    queries = rotary(matmul(normal_one, full_query).reshape(count, H, HD), cosine, sine).astype(
        jnp.bfloat16
    )
    keys_own = (
        rotary(matmul(normal_one, full_key).reshape(count, KV, HD), cosine, sine)
        .astype(jnp.bfloat16)
        .reshape(count, KV * HD)
    )
    values_own = matmul(normal_one, full_value).astype(jnp.bfloat16)
    keys_flat, values_flat = (
        lax.all_gather(keys_own, "ctx", axis=0, tiled=True),
        lax.all_gather(values_own, "ctx", axis=0, tiled=True),
    )
    keys_all = keys_flat.reshape(-1, KV, HD)
    values_all = values_flat.reshape(-1, KV, HD)
    mixed, logsum = attend(queries, keys_all, values_all, pos_rows, pos_keys)
    mixed_flat = mixed.reshape(count, H * HD)
    hidden_one = inputs + matmul(mixed_flat, full_output)
    unit_two, factor_two, normal_two = normed(hidden_one, gain_mlp)
    rows_all = lax.all_gather(normal_two, "fsdp", axis=0, tiled=True)
    grad_all = lax.all_gather(grad_out, "fsdp", axis=0, tiled=True)
    gate = matmul(rows_all, w_gate)
    up = matmul(rows_all, w_up)
    hidden = (jax.nn.silu(gate) * up).astype(jnp.bfloat16)
    grad_hidden = through(grad_all, w_down)
    grad_gate_in, grad_up_in = gate_back(grad_hidden, gate, up)
    grad_normal_two = lax.psum_scatter(
        (through(grad_gate_in, w_gate) + through(grad_up_in, w_up)).astype(jnp.bfloat16),
        "fsdp",
        scatter_dimension=0,
        tiled=True,
    ).astype(jnp.float32)
    mlp_out = lax.psum_scatter(
        matmul(hidden, w_down).astype(jnp.bfloat16), "fsdp", scatter_dimension=0, tiled=True
    ).astype(jnp.float32)
    part_gate = across(rows_all, grad_gate_in)
    part_up = across(rows_all, grad_up_in)
    part_down = across(hidden, grad_all)
    result = (hidden_one + mlp_out).astype(jnp.bfloat16)
    grad_hidden_one = grad_out.astype(jnp.float32) + normed_back(
        unit_two, factor_two, grad_normal_two, gain_mlp
    )
    grad_mixed_in = grad_hidden_one.astype(jnp.bfloat16)
    grad_mixed = through(grad_mixed_in, full_output).astype(jnp.bfloat16).reshape(count, H, HD)
    grad_q, grad_k_all, grad_v_all = attend_back(
        queries, keys_all, values_all, mixed, grad_mixed, logsum, pos_rows, pos_keys
    )
    grad_k_own, grad_v_own = (
        lax.psum_scatter(
            grad_k_all.reshape(-1, KV * HD).astype(jnp.bfloat16),
            "ctx",
            scatter_dimension=0,
            tiled=True,
        ).astype(jnp.float32),
        lax.psum_scatter(
            grad_v_all.reshape(-1, KV * HD).astype(jnp.bfloat16),
            "ctx",
            scatter_dimension=0,
            tiled=True,
        ).astype(jnp.float32),
    )
    grad_queries = rotary(grad_q, cosine, -sine).astype(jnp.bfloat16).reshape(count, H * HD)
    grad_keys = (
        rotary(grad_k_own.reshape(count, KV, HD), cosine, -sine)
        .astype(jnp.bfloat16)
        .reshape(count, KV * HD)
    )
    grad_values = grad_v_own.astype(jnp.bfloat16)
    grad_normal_one = (
        through(grad_queries, full_query)
        + through(grad_keys, full_key)
        + through(grad_values, full_value)
    )
    grad_tokens = (
        grad_hidden_one + normed_back(unit_one, factor_one, grad_normal_one, gain_attn)
    ).astype(jnp.bfloat16)
    attn_stack = lax.psum_scatter(
        jnp.concatenate(
            [
                across(normal_one, grad_queries),
                across(normal_one, grad_keys),
                across(normal_one, grad_values),
                across(grad_mixed_in, mixed_flat),
            ],
            1,
        ).astype(jnp.bfloat16),
        "fsdp",
        scatter_dimension=0,
        tiled=True,
    ).astype(jnp.float32)
    query_cols = H * HD
    key_cols = KV * HD
    part_query = attn_stack[:, :query_cols]
    part_key = attn_stack[:, query_cols : query_cols + key_cols]
    part_value = attn_stack[:, query_cols + key_cols : query_cols + 2 * key_cols]
    part_output = attn_stack[:, query_cols + 2 * key_cols :].T
    summed = tuple(
        lax.psum(part.astype(jnp.bfloat16), "ctx").astype(jnp.float32)
        for part in (
            part_query,
            part_key,
            part_value,
            part_output,
            part_gate,
            part_up,
            part_down,
        )
    )
    gain_one, gain_two = lax.psum(
        (jnp.sum(grad_normal_one * unit_one, 0), jnp.sum(grad_normal_two * unit_two, 0)),
        ("ctx", "fsdp"),
    )
    return (
        result[None],
        grad_tokens[None],
        summed[0],
        summed[1],
        summed[2],
        summed[3],
        summed[4],
        summed[5],
        summed[6],
        gain_one,
        gain_two,
    )


def solution(mesh):
    in_specs = (
        P("fsdp", "ctx", None),
        P("fsdp", "ctx", None),
        P(),
        P(),
        P("fsdp", None),
        P("fsdp", None),
        P("fsdp", None),
        P(None, "fsdp"),
        P(),
        P(None, "fsdp"),
        P(None, "fsdp"),
        P("fsdp", None),
    )
    out_specs = (
        P("fsdp", "ctx", None),
        P("fsdp", "ctx", None),
        P("fsdp", None),
        P("fsdp", None),
        P("fsdp", None),
        P(None, "fsdp"),
        P(None, "fsdp"),
        P(None, "fsdp"),
        P("fsdp", None),
        P(),
        P(),
    )
    return jax.shard_map(shards, mesh=mesh, in_specs=in_specs, out_specs=out_specs, check_vma=False)
```

```python
import functools

import jax
import jax.numpy as jnp
from jax import lax
from jax.experimental import pallas as pl
from jax.experimental.pallas import tpu as pltpu
from jax.sharding import PartitionSpec as P

H = 32
KV = 4
HD = 64
GROUP = H // KV
PAIRS = GROUP // 2
LANES = 128

EPSILON = 1e-05
NEGATIVE = -1e30
SLOTS = 6
VMEM_LIMIT = 60 * 1024 * 1024
MESH = pl.DeviceIdType.MESH
F32 = jnp.float32
BF16 = jnp.bfloat16


def dot(left, right, left_dim, right_dim):
    return lax.dot_general(
        left, right, (((left_dim,), (right_dim,)), ((), ())), preferred_element_type=F32
    )


def matmul(left, right):
    return dot(left, right, 1, 0)


def across(left, right):
    return dot(left, right, 0, 0)


def through(left, right):
    return dot(left, right, 1, 1)


def normed(hidden, gain):
    factor = lax.rsqrt(jnp.mean(hidden * hidden, -1, keepdims=True) + EPSILON)
    unit = hidden * factor
    return (unit, factor, (unit * gain).astype(BF16))


def normed_back(unit, factor, grad_in, gain):
    scaled = grad_in * gain
    return factor * (scaled - unit * jnp.mean(scaled * unit, -1, keepdims=True))


def gate_back(grad_hidden, gate, up):
    sigma = jax.nn.sigmoid(gate)
    activated = gate * sigma
    grad_gate_in = (grad_hidden * up * sigma * (1.0 + gate * (1.0 - sigma))).astype(BF16)
    grad_up_in = (grad_hidden * activated).astype(BF16)
    return ((activated * up).astype(BF16), grad_gate_in, grad_up_in)


def lanes_of(shape):
    return lax.broadcasted_iota(jnp.int32, shape, len(shape) - 1)


def roll_lanes(value, amount):
    return pltpu.roll(value, amount, 1)


def turned(value):
    first = lax.rem(lanes_of(value.shape), HD) < HD // 2
    return jnp.where(first, -roll_lanes(value, LANES - HD // 2), roll_lanes(value, HD // 2))


def stacked(ref, rows, group):
    wide = PAIRS * LANES
    block = ref[rows, pl.ds(pl.multiple_of(group * wide, wide), wide)]
    return jnp.concatenate([block[:, j * LANES : (j + 1) * LANES] for j in range(PAIRS)], 0)


def spread_heads(ref, out_ref, group):
    at = pl.multiple_of((group // 2) * LANES, LANES)
    tile = ref[:, pl.ds(at, LANES)].astype(F32)
    other = roll_lanes(tile, HD)
    half = lanes_of(tile.shape) // HD
    here = lax.rem(group, 2)
    for par in range(2):
        picked = jnp.where(here == par, tile, other)
        out_ref[par] = jnp.where(half == par, picked, 0.0).astype(BF16)


def attend_kernel(q_ref, k_ref, v_ref, mask_ref, o_ref, lse_ref, kz, vz):
    block = q_ref.shape[0] // 2
    keys = k_ref.shape[0] // 2
    scale = HD ** (-0.5)
    lse_ref[...] = jnp.zeros_like(lse_ref)

    def per_group(group, _):
        spread_heads(k_ref, kz, group)
        spread_heads(v_ref, vz, group)
        for rb in range(2):
            rows = pl.ds(rb * block, block)
            q4 = stacked(q_ref, rows, group) * jnp.asarray(scale, BF16)
            mask = mask_ref[rb]
            mask = jnp.concatenate([mask] * PAIRS, 0)
            total = 0.0
            lse = lse_ref[rb]
            for par in range(2):
                low = through(q4, kz[par, pl.ds(0, keys)])
                scores = [low + mask] if rb == 0 else [low]
                if rb == 1:
                    scores.append(through(q4, kz[par, pl.ds(keys, keys)]) + mask)
                peak = functools.reduce(
                    jnp.maximum, [jnp.max(s, -1, keepdims=True) for s in scores]
                )
                probs = [jnp.exp(s - peak) for s in scores]
                norm = sum(jnp.sum(p, -1, keepdims=True) for p in probs)
                mixed = sum(
                    matmul(p.astype(BF16), vz[par, pl.ds(i * keys, keys)])
                    for i, p in enumerate(probs)
                )
                total = total + mixed / norm
                lse = jnp.where(lanes_of(lse.shape) == 2 * group + par, peak + jnp.log(norm), lse)
            lse_ref[rb] = lse
            for j in range(PAIRS):
                at = pl.multiple_of((group * PAIRS + j) * LANES, LANES)
                o_ref[rows, pl.ds(at, LANES)] = total[j * block : (j + 1) * block].astype(BF16)
        return 0

    lax.fori_loop(0, KV, per_group, 0)


def attend(q, k_all, v_all, mask):
    count = q.shape[0]
    total = k_all.shape[0]
    vmem = pl.BlockSpec(memory_space=pltpu.VMEM)
    return pl.pallas_call(
        attend_kernel,
        out_shape=(
            jax.ShapeDtypeStruct((count, H * HD), BF16),
            jax.ShapeDtypeStruct((2, PAIRS * count // 2, LANES), F32),
        ),
        in_specs=[vmem] * 4,
        out_specs=(vmem, vmem),
        scratch_shapes=[
            pltpu.VMEM((2, total, LANES), BF16),
            pltpu.VMEM((2, total, LANES), BF16),
        ],
        compiler_params=pltpu.CompilerParams(vmem_limit_bytes=VMEM_LIMIT),
        cost_estimate=pl.CostEstimate(
            flops=4 * count * total * H * HD, bytes_accessed=4 << 20, transcendentals=H * count * total
        ),
        name="attend",
    )(q, k_all, v_all, mask)


class LineSum:
    def __init__(self, count, index, first, second, sources, targets, bufs, sems):
        self.n = count
        self.first, self.second = first, second
        self.total = first + second
        self.mlp_src, self.att_src = sources
        self.gate_dst, self.up_dst, self.down_dst, self.query_dst, self.output_dst = targets
        self.own, self.rout, self.sums, self.rin, self.done, self.flip = bufs
        (
            self.load_sem,
            self.in_send,
            self.rout_sem,
            self.rin_sem,
            self.out_send,
            self.store_sem,
            self.credit_in,
            self.credit_out,
        ) = sems
        half = count // 2
        left = index < half
        self.depth = jnp.where(left, index, count - 1 - index)
        step = jnp.where(left, 1, -1)
        self.inward = index + step
        outward = index - step
        self.has_out = self.depth > 0
        self.outward = jnp.where(self.has_out, outward, index + step)
        self.is_mid = self.depth == half - 1
        deepest = half - 1
        self.lag_sum = 1 + 2 * self.depth
        self.lag_sent = self.lag_sum + 2
        self.lag_total = 1 + 2 * deepest + 2 + 2 * (deepest - self.depth)
        self.lag_end = self.lag_total + 3
        self.ticks = self.total + 1 + 2 * deepest + 2 + 2 * deepest + 3
        self.att_rows = self.att_src.shape[1]
        self.blocks = self.down_dst.shape[1] // LANES

    def view(self, buf, slot, att):
        return buf.at[slot, pl.ds(0, self.att_rows)] if att else buf.at[slot]

    def each(self, chunk, body):
        slot = lax.rem(jnp.maximum(chunk, 0), SLOTS)
        pl.when((chunk >= 0) & (chunk < self.first))(lambda: body(chunk, slot, False))
        if self.second:
            pl.when((chunk >= self.first) & (chunk < self.total))(lambda: body(chunk, slot, True))

    def send(self, src, dst, sems, target, slot, att):
        return pltpu.make_async_remote_copy(
            src_ref=self.view(src, slot, att),
            dst_ref=self.view(dst, slot, att),
            send_sem=sems[0].at[slot],
            recv_sem=sems[1].at[slot],
            device_id={"ctx": target},
            device_id_type=MESH,
        )

    def to_total(self, slot, att):
        return self.send(self.sums, self.rin, (self.in_send, self.rin_sem), self.inward, slot, att)

    def to_partial(self, slot, att):
        return self.send(
            self.sums, self.rout, (self.in_send, self.rout_sem), self.inward, slot, att
        )

    def to_outward(self, slot, att):
        return self.send(
            self.done, self.rin, (self.out_send, self.rin_sem), self.outward, slot, att
        )

    def load(self, chunk, slot):
        return pltpu.make_async_copy(
            self.mlp_src.at[chunk], self.own.at[slot], self.load_sem.at[slot]
        )

    def stores(self, chunk, slot, att):
        if att:
            rows = self.att_rows // 2
            wide = self.query_dst.shape[1] // LANES
            pairs = []
            for i in range(2):
                at = 2 * (chunk - self.first) + i
                src = self.done.at[slot, pl.ds(i * rows, rows)]
                sem = self.store_sem.at[slot, i]
                q_at = pl.multiple_of(jnp.minimum(at, wide - 1) * LANES, LANES)
                o_at = pl.multiple_of(jnp.maximum(at - wide, 0) * LANES, LANES)
                pairs.append(
                    (
                        at < wide,
                        pltpu.make_async_copy(src, self.query_dst.at[:, pl.ds(q_at, LANES)], sem),
                    )
                )
                pairs.append(
                    (
                        at >= wide,
                        pltpu.make_async_copy(src, self.output_dst.at[:, pl.ds(o_at, LANES)], sem),
                    )
                )
            return pairs
        kind = chunk // self.blocks
        at = pl.multiple_of(lax.rem(chunk, self.blocks) * LANES, LANES)
        sem = self.store_sem.at[slot, 0]
        return [
            (
                kind == 0,
                pltpu.make_async_copy(self.flip.at[slot], self.gate_dst.at[pl.ds(at, LANES)], sem),
            ),
            (
                kind == 1,
                pltpu.make_async_copy(self.flip.at[slot], self.up_dst.at[pl.ds(at, LANES)], sem),
            ),
            (
                kind == 2,
                pltpu.make_async_copy(
                    self.done.at[slot], self.down_dst.at[:, pl.ds(at, LANES)], sem
                ),
            ),
        ]

    def tick(self, i):
        self.each(i - self.lag_sum + 1, self.stage_load)
        self.each(i - self.lag_sum, self.stage_sum)
        self.each(i - self.lag_sent, self.stage_sent)
        self.each(i - self.lag_total, self.stage_total)
        self.each(i - self.lag_end, self.stage_end)

    def stage_load(self, chunk, slot, att):
        if not att:
            self.load(chunk, slot).start()

    def stage_sum(self, chunk, slot, att):
        if not att:
            self.load(chunk, slot).wait()

        def own():
            return self.att_src[chunk - self.first] if att else self.own[slot]

        @pl.when(self.has_out)
        def _():
            self.to_partial(slot, att).wait_recv()
            arrived = self.view(self.rout, slot, att)[...].astype(F32)
            self.view(self.sums, slot, att)[...] = (own().astype(F32) + arrived).astype(BF16)

            @pl.when(chunk < self.total - SLOTS)
            def _():
                pl.semaphore_signal(
                    self.credit_in, 1, device_id={"ctx": self.outward}, device_id_type=MESH
                )

        @pl.when(jnp.logical_not(self.has_out))
        def _():
            self.view(self.sums, slot, att)[...] = own()

        @pl.when(chunk >= SLOTS)
        def _():
            pl.semaphore_wait(self.credit_in, 1)

        pl.when(self.is_mid)(lambda: self.to_total(slot, att).start())
        pl.when(jnp.logical_not(self.is_mid))(lambda: self.to_partial(slot, att).start())

    def stage_sent(self, chunk, slot, att):
        self.to_total(slot, att).wait_send()

    def stage_total(self, chunk, slot, att):
        self.to_total(slot, att).wait_recv()
        arrived = self.view(self.rin, slot, att)
        done = self.view(self.done, slot, att)

        @pl.when(self.is_mid)
        def _():
            mine = self.view(self.sums, slot, att)[...].astype(F32)
            done[...] = (mine + arrived[...].astype(F32)).astype(BF16)

            @pl.when(chunk < self.total - SLOTS)
            def _():
                pl.semaphore_signal(
                    self.credit_in, 1, device_id={"ctx": self.inward}, device_id_type=MESH
                )

        @pl.when(jnp.logical_not(self.is_mid))
        def _():
            done[...] = arrived[...]

            @pl.when(chunk < self.total - SLOTS)
            def _():
                pl.semaphore_signal(
                    self.credit_out, 1, device_id={"ctx": self.inward}, device_id_type=MESH
                )

        @pl.when(self.has_out)
        def _():
            @pl.when(chunk >= SLOTS)
            def _():
                pl.semaphore_wait(self.credit_out, 1)

            self.to_outward(slot, att).start()

        if not att:

            @pl.when(chunk < 2 * self.blocks)
            def _():
                self.flip[slot] = self.done[slot].T

        for condition, copy in self.stores(chunk, slot, att):
            pl.when(condition)(copy.start)

    def stage_end(self, chunk, slot, att):
        pl.when(self.has_out)(lambda: self.to_outward(slot, att).wait_send())
        for condition, copy in self.stores(chunk, slot, att):
            pl.when(condition)(copy.wait)


def chip_at(place):
    return 2 * (place // 2) + lax.rem(place + place // 2, 2)


class Ring:
    def __init__(self, count, index):
        self.chips = count // 2
        chip = index // 2
        self.core = lax.rem(index, 2)
        self.place = chip_at(chip)
        self.partner = 2 * chip + 1 - self.core
        self.right = self.device(1)
        self.left = self.device(-1)

    def device(self, offset, core=None):
        place = lax.rem(self.place + offset + self.chips, self.chips)
        return 2 * chip_at(place) + (self.core if core is None else core)


class RingSum:
    def __init__(self, ring, partial, bufs, sems):
        self.ring, self.partial = ring, partial
        self.stage, self.pair, self.from_left, self.from_right = bufs
        (
            self.stage_send,
            self.pair_recv,
            self.right_send,
            self.right_recv,
            self.left_send,
            self.left_recv,
        ) = sems
        far = ring.chips // 2
        self.far = far
        offsets = [far]
        for s in range(far - 1, 0, -1):
            offsets += [s, -s]
        self.offsets = offsets + [0]
        self.at = {offset: i for i, offset in enumerate(self.offsets)}
        self.rows = self.pair.shape[1]

    def half(self, which):
        return pl.ds(which * (self.rows // 2), self.rows // 2)

    def pair_copy(self, i):
        return pltpu.make_async_remote_copy(
            src_ref=self.stage.at[i % 2],
            dst_ref=self.pair.at[i],
            send_sem=self.stage_send.at[i],
            recv_sem=self.pair_recv.at[i],
            device_id={"fsdp": self.ring.partner},
            device_id_type=MESH,
        )

    def pair_step(self, i):
        offset = self.offsets[i]
        if i >= 2:
            self.pair_copy(i - 2).wait_send()
        self.stage[i % 2] = self.partial(self.ring.device(offset, 1 - self.ring.core)).astype(BF16)
        self.pair_copy(i).start()

    def pair_add(self, i):
        mine = self.partial(self.ring.device(self.offsets[i]))
        self.pair_copy(i).wait_recv()
        self.pair[i] = (mine + self.pair[i].astype(F32)).astype(BF16)

    def pair_all(self):
        last = len(self.offsets)
        for i in range(last):
            self.pair_step(i)
            if i >= 1:
                self.pair_add(i - 1)
        self.pair_add(last - 1)
        for i in range(max(last - 2, 0), last):
            self.pair_copy(i).wait_send()

    def hop(self, s, right, which):
        owner = self.at[s if right or s == self.far else -s]
        rows = self.half(which)
        return pltpu.make_async_remote_copy(
            src_ref=self.pair.at[owner, rows],
            dst_ref=(self.from_left if right else self.from_right).at[s - 1, rows],
            send_sem=(self.right_send if right else self.left_send).at[s - 1, which],
            recv_sem=(self.right_recv if right else self.left_recv).at[s - 1, which],
            device_id={"fsdp": self.ring.right if right else self.ring.left},
            device_id_type=MESH,
        )

    def hops(self):
        far = self.far
        moves = [(far, True, 0), (far, False, 1)]
        if far > 1:
            moves += [(far - 1, True, 1), (far - 1, False, 0)]
            moves += [(far - 1, True, 0), (far - 1, False, 1)]
        for s in range(far - 2, 0, -1):
            for which in range(2):
                moves += [(s, True, which), (s, False, which)]
        return moves

    def free(self, s, right, which):
        return s == self.far or (s == self.far - 1 and which == (1 if right else 0))

    def launch(self, free):
        for s, right, which in self.hops():
            if self.free(s, right, which) == free:
                if not free:
                    before = self.hop(s + 1, right, which)
                    before.wait_recv()
                    owner = self.at[s if right else -s]
                    rows = self.half(which)
                    arrived = (self.from_left if right else self.from_right).at[s, rows]
                    self.pair[owner, rows] = (
                        self.pair[owner, rows].astype(F32) + arrived[...].astype(F32)
                    ).astype(BF16)
                self.hop(s, right, which).start()

    def finish(self):
        for s, right, which in self.hops():
            if s == 1:
                self.hop(s, right, which).wait_recv()
            self.hop(s, right, which).wait_send()
        own = self.pair[self.at[0]].astype(F32)
        if self.far == 1:
            joined = jnp.concatenate(
                [self.from_left[0, self.half(0)], self.from_right[0, self.half(1)]], 0
            )
            return own + joined.astype(F32)
        return own + self.from_left[0].astype(F32) + self.from_right[0].astype(F32)


def back_kernel(
    sizes,
    gz_ref,
    wqkv_ref,
    q_ref,
    o_ref,
    do_ref,
    dhb_ref,
    a1_ref,
    k_ref,
    v_ref,
    lse_ref,
    mask_ref,
    turn_ref,
    x_ref,
    dh1_ref,
    gain_ref,
    gpart_ref,
    gtok_ref,
    gains_ref,
    gate_out,
    up_out,
    down_out,
    query_out,
    output_out,
    *scratch,
):
    ctx_n, fsdp_n = sizes
    (
        zown,
        zrout,
        zsums,
        zrin,
        zdone,
        zflip,
        az,
        xstage,
        xpair,
        xleft,
        xright,
        ystage,
        ypair,
        yleft,
        yright,
        kz,
        vz,
        dk_acc,
        dv_acc,
        dkv,
        dkv_in,
        gqkv,
        wbuf,
        gslot,
        cslot,
        load_sem,
        in_send,
        rout_sem,
        rin_sem,
        out_send,
        store_sem,
        credit_in,
        credit_out,
        xs0,
        xs1,
        xs2,
        xs3,
        xs4,
        xs5,
        ys0,
        ys1,
        ys2,
        ys3,
        ys4,
        ys5,
        dkv_send,
        dkv_recv,
        gain_send,
        gain_recv,
        cgain_send,
        cgain_recv,
        wsem,
    ) = scratch
    ctx = lax.axis_index("ctx")
    fsdp = lax.axis_index("fsdp")
    ring = Ring(fsdp_n, fsdp)
    count = q_ref.shape[0]
    block = count // 2
    keys = k_ref.shape[0] // 2
    scale = HD ** (-0.5)
    width = q_ref.shape[1]
    shard = query_out.shape[0]

    barrier = pltpu.get_barrier_semaphore()
    for step in range(1, ctx_n):
        pl.semaphore_signal(
            barrier,
            1,
            device_id={"ctx": lax.rem(ctx + step, ctx_n)},
            device_id_type=MESH,
        )
    for step in range(1, fsdp_n):
        pl.semaphore_signal(
            barrier,
            1,
            device_id={"fsdp": lax.rem(fsdp + step, fsdp_n)},
            device_id_type=MESH,
        )
    pl.semaphore_wait(barrier, ctx_n + fsdp_n - 2)

    line = LineSum(
        ctx_n,
        ctx,
        gz_ref.shape[0],
        az.shape[0],
        (gz_ref, az),
        (gate_out, up_out, down_out, query_out, output_out),
        (zown, zrout, zsums, zrin, zdone, zflip),
        (load_sem, in_send, rout_sem, rin_sem, out_send, store_sem, credit_in, credit_out),
    )

    clock = [0]

    def ticks(number):
        start = clock[0]
        clock[0] = start + number

        def body(i, _):
            line.tick(i)
            return 0

        lax.fori_loop(start, start + number, body, 0)

    ticks(2)

    def output_partial(f):
        return across(dhb_ref[:, pl.ds(pl.multiple_of(f * shard, shard), shard)], o_ref[...])

    ysum = RingSum(
        ring, output_partial, (ystage, ypair, yleft, yright), (ys0, ys1, ys2, ys3, ys4, ys5)
    )
    ysum.pair_all()
    ysum.launch(True)

    def piece(group, rb, par, q4, do4, lse, delta, at, mask, grad_q):
        span = pl.ds(at, keys)
        k_part = kz[par, span]
        v_part = vz[par, span]
        scores = through(q4, k_part)
        if mask is not None:
            scores = scores + mask
        probs = jnp.exp(scores - lse)
        dprob = through(do4, v_part)
        dscore = (probs * (dprob - delta)).astype(BF16)
        dk_acc[par, span] += across(dscore, q4)
        dv_acc[par, span] += across(probs.astype(BF16), do4)
        return grad_q + matmul(dscore, k_part)

    def group_step(group, rb):
        rows = pl.ds(rb * block, block)
        q4 = stacked(q_ref, rows, group) * jnp.asarray(scale, BF16)
        do4 = stacked(do_ref, rows, group)
        prod = do4.astype(F32) * stacked(o_ref, rows, group).astype(F32)
        lse_all = lse_ref[rb]
        mask = jnp.concatenate([mask_ref[rb]] * PAIRS, 0)
        grad_q = jnp.zeros((PAIRS * block, LANES), F32)
        for par in range(2):
            lse = jnp.sum(
                jnp.where(lanes_of(lse_all.shape) == 2 * group + par, lse_all, 0.0),
                -1,
                keepdims=True,
            )
            delta = jnp.sum(
                jnp.where(lanes_of(prod.shape) // HD == par, prod, 0.0), -1, keepdims=True
            )
            grad_q = piece(
                group, rb, par, q4, do4, lse, delta, 0, mask if rb == 0 else None, grad_q
            )
            if rb == 1:
                grad_q = piece(group, rb, par, q4, do4, lse, delta, keys, mask, grad_q)
        grad_q = grad_q * scale
        cosine, sine = turn_ref[0, rows], turn_ref[1, rows]
        for j in range(PAIRS):
            part = grad_q[j * block : (j + 1) * block]
            at = pl.multiple_of((group * PAIRS + j) * LANES, LANES)
            gqkv[rows, pl.ds(at, LANES)] = (part * cosine - turned(part) * sine).astype(BF16)

    def dkv_copy(owner, tile, step):
        return pltpu.make_async_remote_copy(
            src_ref=dkv.at[owner, tile],
            dst_ref=dkv_in.at[ctx, tile],
            send_sem=dkv_send.at[step, tile],
            recv_sem=dkv_recv.at[step, tile],
            device_id={"ctx": owner},
            device_id_type=MESH,
        )

    def attention(lo, hi, per_rb):
        start = clock[0]

        def body(group, _):
            spread_heads(k_ref, kz, group)
            spread_heads(v_ref, vz, group)
            dk_acc[...] = jnp.zeros_like(dk_acc)
            dv_acc[...] = jnp.zeros_like(dv_acc)
            for rb in range(2):
                group_step(group, rb)
                base = start + (group - lo) * 2 * per_rb + rb * per_rb
                for t in range(per_rb):
                    line.tick(base + t)
            tile = group // 2
            for which, acc in enumerate((dk_acc, dv_acc)):
                for part in range(ctx_n):
                    for rb in range(2):
                        span = pl.ds(rb * keys + part * block, block)
                        both = jnp.where(
                            lanes_of((block, LANES)) < HD, acc[0, span], acc[1, span]
                        )
                        both = both + roll_lanes(both, HD)
                        there = (part, tile, which, pl.ds(rb * block, block))
                        mine = lanes_of((block, LANES)) // HD == lax.rem(group, 2)
                        dkv[there] = jnp.where(mine, both.astype(BF16), dkv[there])
            return 0

        lax.fori_loop(lo, hi, body, 0)
        clock[0] = start + (hi - lo) * 2 * per_rb

    for tile in range(KV // 2):
        attention(2 * tile, 2 * tile + 2, 1)
        for step in range(1, ctx_n):
            dkv_copy(lax.rem(ctx + step, ctx_n), tile, step - 1).start()
        if tile == 0:
            ysum.launch(False)

    ticks(2)
    def put_blocks(value, first):
        for j in range(value.shape[1] // LANES):
            at = first + j
            az[at // 2, pl.ds((at % 2) * shard, shard)] = value[:, j * LANES : (j + 1) * LANES]

    key_cols = KV * HD
    put_blocks(ysum.finish().astype(BF16), (width + 2 * key_cols) // LANES)

    for step in range(1, ctx_n):
        for tile in range(KV // 2):
            dkv_copy(lax.rem(ctx + step, ctx_n), tile, step - 1).wait_send()
            sender = lax.rem(ctx - step + ctx_n, ctx_n)
            pltpu.make_async_remote_copy(
                src_ref=dkv.at[sender, tile],
                dst_ref=dkv_in.at[sender, tile],
                send_sem=dkv_send.at[step - 1, tile],
                recv_sem=dkv_recv.at[step - 1, tile],
                device_id={"ctx": sender},
                device_id_type=MESH,
            ).wait_recv()
    cosine, sine = turn_ref[0], turn_ref[1]
    for tile in range(KV // 2):
        for which in range(2):
            part = dkv[ctx, tile, which].astype(F32)
            for step in range(1, ctx_n):
                part = part + dkv_in[lax.rem(ctx + step, ctx_n), tile, which].astype(F32)
            if which == 0:
                part = part * cosine - turned(part) * sine
            at = width + which * key_cols + tile * LANES
            gqkv[:, at : at + LANES] = part.astype(BF16)

    def query_partial(f):
        return across(a1_ref[:, pl.ds(pl.multiple_of(f * shard, shard), shard)], gqkv[...])

    xsum = RingSum(
        ring, query_partial, (xstage, xpair, xleft, xright), (xs0, xs1, xs2, xs3, xs4, xs5)
    )
    xsum.pair_all()
    xsum.launch(True)
    ticks(4)
    xsum.launch(False)
    ticks(4)

    def weight_copy(f):
        return pltpu.make_async_copy(wqkv_ref.at[f], wbuf.at[f % 2], wsem.at[f % 2])

    weight_copy(0).start()
    parts = []
    for f in range(fsdp_n):
        if f + 1 < fsdp_n:
            weight_copy(f + 1).start()
        weight_copy(f).wait()
        parts.append(through(gqkv[...], wbuf[f % 2]))
    da1 = jnp.concatenate(parts, 1)
    x = x_ref[...].astype(F32)
    factor = lax.rsqrt(jnp.mean(x * x, -1, keepdims=True) + EPSILON)
    unit = x * factor
    gain = gain_ref[...]
    gtok_ref[...] = (dh1_ref[...] + normed_back(unit, factor, da1, gain)).astype(BF16)
    mine = jnp.sum(da1 * unit, 0, keepdims=True)
    first_row = lax.broadcasted_iota(jnp.int32, (2, width), 0) == 0
    gslot[fsdp] = jnp.where(first_row, mine, gpart_ref[...])

    def gain_copy(slots, axis, here, step, sems):
        n = fsdp_n if axis == "fsdp" else ctx_n
        return pltpu.make_async_remote_copy(
            src_ref=slots.at[here],
            dst_ref=slots.at[here],
            send_sem=sems[0].at[step - 1],
            recv_sem=sems[1].at[step - 1],
            device_id={axis: lax.rem((fsdp if axis == "fsdp" else ctx) + step, n)},
            device_id_type=MESH,
        )

    def exchange(slots, axis, n, me, sems):
        for step in range(1, n):
            gain_copy(slots, axis, me, step, sems).start()
        for step in range(1, n):
            gain_copy(slots, axis, me, step, sems).wait_send()
            gain_copy(slots, axis, lax.rem(me - step + n, n), step, sems).wait_recv()
        total = slots[0]
        for i in range(1, n):
            total = total + slots[i]
        return total

    cslot[ctx] = exchange(gslot, "fsdp", fsdp_n, fsdp, (gain_send, gain_recv))
    gains_ref[...] = exchange(cslot, "ctx", ctx_n, ctx, (cgain_send, cgain_recv))

    put_blocks(xsum.finish().astype(BF16), 0)
    ticks(line.ticks - clock[0])


def back(gz, wqkv, q, o, do, dhb, a1, k_all, v_all, lse, mask, turn, x, dh1, gain, gpart):
    ctx_n = lax.axis_size("ctx")
    fsdp_n = lax.axis_size("fsdp")
    count, width = q.shape
    total = k_all.shape[0]
    local = gz.shape[1]
    shard = wqkv.shape[1]
    cols = wqkv.shape[2]
    chips = fsdp_n // 2
    far = chips // 2
    vmem = pl.BlockSpec(memory_space=pltpu.VMEM)
    hbm = pl.BlockSpec(memory_space=pl.ANY)
    dma = pltpu.SemaphoreType.DMA
    zbuf = pltpu.VMEM((SLOTS, local, LANES), BF16)

    def ring_bufs(wide):
        return [
            pltpu.VMEM((2, shard, wide), BF16),
            pltpu.VMEM((chips, shard, wide), BF16),
            pltpu.VMEM((far, shard, wide), BF16),
            pltpu.VMEM((far, shard, wide), BF16),
        ]

    ring_sems = [
        dma((chips,)),
        dma((chips,)),
        dma((far, 2)),
        dma((far, 2)),
        dma((far, 2)),
        dma((far, 2)),
    ]
    blocks = (cols + width) // LANES
    scratch = (
        [zbuf] * 5
        + [pltpu.VMEM((SLOTS, LANES, local), BF16)]
        + [pltpu.VMEM((blocks // 2, 2 * shard, LANES), BF16)]
        + ring_bufs(cols)
        + ring_bufs(width)
        + [
            pltpu.VMEM((2, total, LANES), BF16),
            pltpu.VMEM((2, total, LANES), BF16),
            pltpu.VMEM((2, total, LANES), F32),
            pltpu.VMEM((2, total, LANES), F32),
            pltpu.VMEM((ctx_n, KV // 2, 2, count, LANES), BF16),
            pltpu.VMEM((ctx_n, KV // 2, 2, count, LANES), BF16),
            pltpu.VMEM((count, cols), BF16),
            pltpu.VMEM((2, shard, cols), BF16),
            pltpu.VMEM((fsdp_n, 2, width), F32),
            pltpu.VMEM((ctx_n, 2, width), F32),
        ]
        + [
            dma((SLOTS,)),
            dma((SLOTS,)),
            dma((SLOTS,)),
            dma((SLOTS,)),
            dma((SLOTS,)),
            dma((SLOTS, 2)),
            pltpu.SemaphoreType.REGULAR,
            pltpu.SemaphoreType.REGULAR,
        ]
        + ring_sems
        + ring_sems
        + [
            dma((ctx_n - 1, KV // 2)),
            dma((ctx_n - 1, KV // 2)),
            dma((fsdp_n - 1,)),
            dma((fsdp_n - 1,)),
            dma((ctx_n - 1,)),
            dma((ctx_n - 1,)),
            dma((2,)),
        ]
    )
    return pl.pallas_call(
        functools.partial(back_kernel, (ctx_n, fsdp_n)),
        out_shape=(
            jax.ShapeDtypeStruct((count, width), BF16),
            jax.ShapeDtypeStruct((2, width), F32),
            jax.ShapeDtypeStruct((width, local), BF16),
            jax.ShapeDtypeStruct((width, local), BF16),
            jax.ShapeDtypeStruct((local, width), BF16),
            jax.ShapeDtypeStruct((shard, cols), BF16),
            jax.ShapeDtypeStruct((shard, width), BF16),
        ),
        in_specs=[hbm, hbm] + [vmem] * 14,
        out_specs=(vmem, vmem, hbm, hbm, hbm, hbm, hbm),
        scratch_shapes=scratch,
        compiler_params=pltpu.CompilerParams(
            collective_id=1, has_side_effects=True, vmem_limit_bytes=VMEM_LIMIT
        ),
        name="back",
    )(gz, wqkv, q, o, do, dhb, a1, k_all, v_all, lse, mask, turn, x, dh1, gain, gpart)


def shards(
    tokens,
    cotangent,
    block_table,
    gain_attn,
    w_query,
    w_key,
    w_value,
    w_output,
    gain_mlp,
    w_gate,
    w_up,
    w_down,
):
    ctx_n = lax.axis_size("ctx")
    ctx = lax.axis_index("ctx")
    count, width = tokens.shape[1:]
    block = count // 2
    local = w_gate.shape[1]

    table = block_table.reshape(ctx_n, 2)
    lower, upper = jnp.min(table, 1), jnp.max(table, 1)
    owned = table[ctx]
    swap = owned[0] > owned[1]

    def ordered(rows):
        return jnp.where(swap, jnp.concatenate([rows[block:], rows[:block]], 0), rows)

    offsets = jnp.arange(block, dtype=jnp.int32)
    spots = jnp.stack([lower, upper])[:, :, None] * block + offsets
    own_spots = spots[:, ctx]
    key_spots = spots.reshape(2, -1)
    mask = jnp.where(own_spots[:, :, None] >= key_spots[:, None, :], 0.0, NEGATIVE).astype(F32)
    freqs = 10000.0 ** (-jnp.arange(HD // 2, dtype=F32) / (HD // 2))
    angle = own_spots.reshape(-1).astype(F32)[:, None] * freqs[None, :]
    angle = jnp.concatenate([angle] * (LANES * 2 // HD), -1)
    turn = jnp.stack([jnp.cos(angle), jnp.sin(angle)])

    rows_in = ordered(tokens[0])
    grad_out = ordered(cotangent[0])

    wqkv = lax.all_gather(jnp.concatenate([w_query, w_key, w_value], 1), "fsdp", axis=0)
    full_output = lax.all_gather(w_output, "fsdp", axis=0)
    inputs = rows_in.astype(F32)
    unit_one, factor_one, normal_one = normed(inputs, gain_attn)
    qkv = matmul(normal_one, wqkv.reshape(width, -1))

    def rotary(values):
        heads = values.reshape(count, -1, HD)
        middle = HD // 2
        spun = jnp.concatenate([-heads[..., middle:], heads[..., :middle]], -1)
        cosine, sine = turn[:, :, None, :HD]
        return (heads * cosine + spun * sine).reshape(count, -1).astype(BF16)

    key_cols = KV * HD
    queries = rotary(qkv[:, :width])
    keys_own = rotary(qkv[:, width : width + key_cols])
    values_own = qkv[:, width + key_cols :].astype(BF16)

    def gathered(rows):
        every = lax.all_gather(rows, "ctx", axis=0).reshape(ctx_n, 2, block, key_cols)
        return every.transpose(1, 0, 2, 3).reshape(-1, key_cols)

    keys_all, values_all = gathered(keys_own), gathered(values_own)
    mixed, lse = attend(queries, keys_all, values_all, mask)
    attn_out = lax.dot_general(
        mixed, full_output, (((1,), (1,)), ((), ())), preferred_element_type=F32
    ).reshape(count, width)
    hidden_one = inputs + attn_out
    unit_two, factor_two, normal_two = normed(hidden_one, gain_mlp)
    rows_all = lax.all_gather(normal_two, "fsdp", axis=0, tiled=True)
    grad_all = lax.all_gather(grad_out, "fsdp", axis=0, tiled=True)
    gate = matmul(rows_all, w_gate)
    up = matmul(rows_all, w_up)
    grad_hidden = through(grad_all, w_down)
    hidden, grad_gate_in, grad_up_in = gate_back(grad_hidden, gate, up)

    def scattered(partial):
        return lax.psum_scatter(
            partial.astype(BF16), "fsdp", scatter_dimension=0, tiled=True
        ).astype(F32)

    grad_normal_two = scattered(through(grad_gate_in, w_gate) + through(grad_up_in, w_up))
    mlp_out = scattered(matmul(hidden, w_down))

    def chunks(partial):
        return partial.astype(BF16).reshape(local, -1, LANES).transpose(1, 0, 2)

    gz = jnp.concatenate(
        [
            chunks(across(grad_gate_in, rows_all)),
            chunks(across(grad_up_in, rows_all)),
            chunks(across(hidden, grad_all)),
        ],
        0,
    )
    result = (hidden_one + mlp_out).astype(BF16)
    grad_hidden_one = grad_out.astype(F32) + normed_back(
        unit_two, factor_two, grad_normal_two, gain_mlp
    )
    grad_mixed_in = grad_hidden_one.astype(BF16)
    shard = w_output.shape[1]
    split = grad_mixed_in.reshape(count, -1, shard)
    grad_mixed = lax.dot_general(
        split, full_output, (((1, 2), (0, 2)), ((), ())), preferred_element_type=F32
    ).astype(BF16)
    gpart = jnp.sum(grad_normal_two * unit_two, 0, keepdims=True)
    grad_tokens, gains, gate_sum, up_sum, down_sum, query_sum, output_sum = back(
        gz,
        wqkv,
        queries,
        mixed,
        grad_mixed,
        grad_mixed_in,
        normal_one,
        keys_all,
        values_all,
        lse,
        mask,
        turn,
        rows_in,
        grad_hidden_one,
        gain_attn[None],
        gpart,
    )
    query_sum = query_sum.astype(F32)
    return (
        ordered(result)[None],
        ordered(grad_tokens)[None],
        query_sum[:, :width],
        query_sum[:, width : width + key_cols],
        query_sum[:, width + key_cols :],
        output_sum.T.astype(F32),
        gate_sum.astype(F32),
        up_sum.astype(F32),
        down_sum.astype(F32),
        gains[0],
        gains[1],
    )


def solution(mesh):
    in_specs = (
        P("fsdp", "ctx", None),
        P("fsdp", "ctx", None),
        P(),
        P(),
        P("fsdp", None),
        P("fsdp", None),
        P("fsdp", None),
        P(None, "fsdp"),
        P(),
        P(None, "fsdp"),
        P(None, "fsdp"),
        P("fsdp", None),
    )
    out_specs = (
        P("fsdp", "ctx", None),
        P("fsdp", "ctx", None),
        P("fsdp", None),
        P("fsdp", None),
        P("fsdp", None),
        P(None, "fsdp"),
        P(None, "fsdp"),
        P(None, "fsdp"),
        P("fsdp", None),
        P(),
        P(),
    )
    return jax.shard_map(shards, mesh=mesh, in_specs=in_specs, out_specs=out_specs, check_vma=False)
```

```python
import functools

import jax
import jax.numpy as jnp
from jax import lax
from jax.experimental import pallas as pl
from jax.experimental.pallas import tpu as pltpu
from jax.sharding import PartitionSpec as P

H = 32
KV = 4
HD = 64
GROUP = H // KV
PAIRS = GROUP // 2
LANES = 128

EPSILON = 1e-05
NEGATIVE = -1e30
SLOTS = 6
VMEM_LIMIT = 60 * 1024 * 1024
MESH = pl.DeviceIdType.MESH
F32 = jnp.float32
BF16 = jnp.bfloat16


def dot(left, right, left_dim, right_dim):
    return lax.dot_general(
        left, right, (((left_dim,), (right_dim,)), ((), ())), preferred_element_type=F32
    )


def matmul(left, right):
    return dot(left, right, 1, 0)


def across(left, right):
    return dot(left, right, 0, 0)


def through(left, right):
    return dot(left, right, 1, 1)


def normed(hidden, gain):
    factor = lax.rsqrt(jnp.mean(hidden * hidden, -1, keepdims=True) + EPSILON)
    unit = hidden * factor
    return (unit, factor, (unit * gain).astype(BF16))


def normed_back(unit, factor, grad_in, gain):
    scaled = grad_in * gain
    return factor * (scaled - unit * jnp.mean(scaled * unit, -1, keepdims=True))


def gate_back(grad_hidden, gate, up):
    sigma = jax.nn.sigmoid(gate)
    activated = gate * sigma
    grad_gate_in = (grad_hidden * up * sigma * (1.0 + gate * (1.0 - sigma))).astype(BF16)
    grad_up_in = (grad_hidden * activated).astype(BF16)
    return ((activated * up).astype(BF16), grad_gate_in, grad_up_in)


def lanes_of(shape):
    return lax.broadcasted_iota(jnp.int32, shape, len(shape) - 1)


def roll_lanes(value, amount):
    return pltpu.roll(value, amount, 1)


def turned(value):
    first = lax.rem(lanes_of(value.shape), HD) < HD // 2
    return jnp.where(first, -roll_lanes(value, LANES - HD // 2), roll_lanes(value, HD // 2))


def stacked(ref, rows, group):
    wide = PAIRS * LANES
    block = ref[rows, pl.ds(pl.multiple_of(group * wide, wide), wide)]
    return jnp.concatenate([block[:, j * LANES : (j + 1) * LANES] for j in range(PAIRS)], 0)


def spread_heads(ref, out_ref, group):
    at = pl.multiple_of((group // 2) * LANES, LANES)
    tile = ref[:, pl.ds(at, LANES)].astype(F32)
    other = roll_lanes(tile, HD)
    half = lanes_of(tile.shape) // HD
    here = lax.rem(group, 2)
    for par in range(2):
        picked = jnp.where(here == par, tile, other)
        out_ref[par] = jnp.where(half == par, picked, 0.0).astype(BF16)


def attend_kernel(q_ref, k_ref, v_ref, mask_ref, o_ref, lse_ref, kz, vz):
    block = q_ref.shape[0] // 2
    keys = k_ref.shape[0] // 2
    scale = HD ** (-0.5)
    lse_ref[...] = jnp.zeros_like(lse_ref)

    def per_group(group, _):
        spread_heads(k_ref, kz, group)
        spread_heads(v_ref, vz, group)
        for rb in range(2):
            rows = pl.ds(rb * block, block)
            q4 = stacked(q_ref, rows, group) * jnp.asarray(scale, BF16)
            mask = mask_ref[rb]
            mask = jnp.concatenate([mask] * PAIRS, 0)
            total = 0.0
            lse = lse_ref[rb]
            for par in range(2):
                low = through(q4, kz[par, pl.ds(0, keys)])
                scores = [low + mask] if rb == 0 else [low]
                if rb == 1:
                    scores.append(through(q4, kz[par, pl.ds(keys, keys)]) + mask)
                peak = functools.reduce(
                    jnp.maximum, [jnp.max(s, -1, keepdims=True) for s in scores]
                )
                probs = [jnp.exp(s - peak) for s in scores]
                norm = sum(jnp.sum(p, -1, keepdims=True) for p in probs)
                mixed = sum(
                    matmul(p.astype(BF16), vz[par, pl.ds(i * keys, keys)])
                    for i, p in enumerate(probs)
                )
                total = total + mixed / norm
                lse = jnp.where(lanes_of(lse.shape) == 2 * group + par, peak + jnp.log(norm), lse)
            lse_ref[rb] = lse
            for j in range(PAIRS):
                at = pl.multiple_of((group * PAIRS + j) * LANES, LANES)
                o_ref[rows, pl.ds(at, LANES)] = total[j * block : (j + 1) * block].astype(BF16)
        return 0

    lax.fori_loop(0, KV, per_group, 0)


def attend(q, k_all, v_all, mask):
    count = q.shape[0]
    total = k_all.shape[0]
    vmem = pl.BlockSpec(memory_space=pltpu.VMEM)
    return pl.pallas_call(
        attend_kernel,
        out_shape=(
            jax.ShapeDtypeStruct((count, H * HD), BF16),
            jax.ShapeDtypeStruct((2, PAIRS * count // 2, LANES), F32),
        ),
        in_specs=[vmem] * 4,
        out_specs=(vmem, vmem),
        scratch_shapes=[
            pltpu.VMEM((2, total, LANES), BF16),
            pltpu.VMEM((2, total, LANES), BF16),
        ],
        compiler_params=pltpu.CompilerParams(vmem_limit_bytes=VMEM_LIMIT),
        cost_estimate=pl.CostEstimate(
            flops=4 * count * total * H * HD, bytes_accessed=4 << 20, transcendentals=H * count * total
        ),
        name="attend",
    )(q, k_all, v_all, mask)


class LineSum:
    def __init__(self, count, index, first, second, sources, targets, bufs, sems):
        self.n = count
        self.first, self.second = first, second
        self.total = first + second
        self.mlp_src, self.att_src = sources
        self.gate_dst, self.up_dst, self.down_dst, self.query_dst, self.output_dst = targets
        self.own, self.rout, self.sums, self.rin, self.done = bufs
        (
            self.load_sem,
            self.in_send,
            self.rout_sem,
            self.rin_sem,
            self.out_send,
            self.store_sem,
            self.credit_in,
            self.credit_out,
        ) = sems
        half = count // 2
        left = index < half
        self.depth = jnp.where(left, index, count - 1 - index)
        step = jnp.where(left, 1, -1)
        self.inward = index + step
        outward = index - step
        self.has_out = self.depth > 0
        self.outward = jnp.where(self.has_out, outward, index + step)
        self.is_mid = self.depth == half - 1
        deepest = half - 1
        self.lag_sum = 1 + 2 * self.depth
        self.lag_sent = self.lag_sum + 2
        self.lag_total = 1 + 2 * deepest + 2 + 2 * (deepest - self.depth)
        self.lag_end = self.lag_total + 3
        self.ticks = self.total + 1 + 2 * deepest + 2 + 2 * deepest + 3
        self.att_rows = 2 * self.att_src.shape[0]
        self.blocks = self.down_dst.shape[1] // LANES

    def view(self, buf, slot, att):
        return buf.at[slot, pl.ds(0, self.att_rows)] if att else buf.at[slot]

    def each(self, chunk, body):
        slot = lax.rem(jnp.maximum(chunk, 0), SLOTS)
        pl.when((chunk >= 0) & (chunk < self.first))(lambda: body(chunk, slot, False))
        if self.second:
            pl.when((chunk >= self.first) & (chunk < self.total))(lambda: body(chunk, slot, True))

    def send(self, src, dst, sems, target, slot, att):
        return pltpu.make_async_remote_copy(
            src_ref=self.view(src, slot, att),
            dst_ref=self.view(dst, slot, att),
            send_sem=sems[0].at[slot],
            recv_sem=sems[1].at[slot],
            device_id={"ctx": target},
            device_id_type=MESH,
        )

    def to_total(self, slot, att):
        return self.send(self.sums, self.rin, (self.in_send, self.rin_sem), self.inward, slot, att)

    def to_partial(self, slot, att):
        return self.send(
            self.sums, self.rout, (self.in_send, self.rout_sem), self.inward, slot, att
        )

    def to_outward(self, slot, att):
        return self.send(
            self.done, self.rin, (self.out_send, self.rin_sem), self.outward, slot, att
        )

    def load(self, chunk, slot):
        return pltpu.make_async_copy(
            self.mlp_src.at[chunk], self.own.at[slot], self.load_sem.at[slot]
        )

    def stores(self, chunk, slot, att):
        if att:
            rows = self.att_rows // 2
            wide = self.query_dst.shape[1] // LANES
            pairs = []
            for i in range(2):
                at = 2 * (chunk - self.first) + i
                src = self.done.at[slot, pl.ds(i * rows, rows)]
                sem = self.store_sem.at[slot, i]
                q_at = pl.multiple_of(jnp.minimum(at, wide - 1) * LANES, LANES)
                o_at = pl.multiple_of(jnp.maximum(at - wide, 0) * LANES, LANES)
                pairs.append(
                    (
                        at < wide,
                        pltpu.make_async_copy(src, self.query_dst.at[:, pl.ds(q_at, LANES)], sem),
                    )
                )
                pairs.append(
                    (
                        at >= wide,
                        pltpu.make_async_copy(src, self.output_dst.at[:, pl.ds(o_at, LANES)], sem),
                    )
                )
            return pairs
        kind = chunk // self.blocks
        at = pl.multiple_of(lax.rem(chunk, self.blocks) * LANES, LANES)
        sem = self.store_sem.at[slot, 0]
        return [
            (kind == i, pltpu.make_async_copy(self.done.at[slot], dst.at[:, pl.ds(at, LANES)], sem))
            for i, dst in enumerate((self.gate_dst, self.up_dst, self.down_dst))
        ]

    def tick(self, i):
        self.each(i - self.lag_sum + 1, self.stage_load)
        self.each(i - self.lag_sum, self.stage_sum)
        self.each(i - self.lag_sent, self.stage_sent)
        self.each(i - self.lag_total, self.stage_total)
        self.each(i - self.lag_end, self.stage_end)

    def stage_load(self, chunk, slot, att):
        if not att:
            self.load(chunk, slot).start()

    def stage_sum(self, chunk, slot, att):
        if not att:
            self.load(chunk, slot).wait()

        def own():
            if not att:
                return self.own[slot]
            at = (chunk - self.first) * 2 * LANES
            return jnp.concatenate(
                [
                    self.att_src[:, pl.ds(pl.multiple_of(at + i * LANES, LANES), LANES)]
                    for i in range(2)
                ],
                0,
            )

        @pl.when(self.has_out)
        def _():
            self.to_partial(slot, att).wait_recv()
            arrived = self.view(self.rout, slot, att)[...].astype(F32)
            self.view(self.sums, slot, att)[...] = (own().astype(F32) + arrived).astype(BF16)

            @pl.when(chunk < self.total - SLOTS)
            def _():
                pl.semaphore_signal(
                    self.credit_in, 1, device_id={"ctx": self.outward}, device_id_type=MESH
                )

        @pl.when(jnp.logical_not(self.has_out))
        def _():
            self.view(self.sums, slot, att)[...] = own()

        @pl.when(chunk >= SLOTS)
        def _():
            pl.semaphore_wait(self.credit_in, 1)

        pl.when(self.is_mid)(lambda: self.to_total(slot, att).start())
        pl.when(jnp.logical_not(self.is_mid))(lambda: self.to_partial(slot, att).start())

    def stage_sent(self, chunk, slot, att):
        self.to_total(slot, att).wait_send()

    def stage_total(self, chunk, slot, att):
        self.to_total(slot, att).wait_recv()
        arrived = self.view(self.rin, slot, att)
        done = self.view(self.done, slot, att)

        @pl.when(self.is_mid)
        def _():
            mine = self.view(self.sums, slot, att)[...].astype(F32)
            done[...] = (mine + arrived[...].astype(F32)).astype(BF16)

            @pl.when(chunk < self.total - SLOTS)
            def _():
                pl.semaphore_signal(
                    self.credit_in, 1, device_id={"ctx": self.inward}, device_id_type=MESH
                )

        @pl.when(jnp.logical_not(self.is_mid))
        def _():
            done[...] = arrived[...]

            @pl.when(chunk < self.total - SLOTS)
            def _():
                pl.semaphore_signal(
                    self.credit_out, 1, device_id={"ctx": self.inward}, device_id_type=MESH
                )

        @pl.when(self.has_out)
        def _():
            @pl.when(chunk >= SLOTS)
            def _():
                pl.semaphore_wait(self.credit_out, 1)

            self.to_outward(slot, att).start()

        for condition, copy in self.stores(chunk, slot, att):
            pl.when(condition)(copy.start)

    def stage_end(self, chunk, slot, att):
        pl.when(self.has_out)(lambda: self.to_outward(slot, att).wait_send())
        for condition, copy in self.stores(chunk, slot, att):
            pl.when(condition)(copy.wait)


def chip_at(place):
    return 2 * (place // 2) + lax.rem(place + place // 2, 2)


class Ring:
    def __init__(self, count, index):
        self.chips = count // 2
        chip = index // 2
        self.core = lax.rem(index, 2)
        self.place = chip_at(chip)
        self.partner = 2 * chip + 1 - self.core
        self.right = self.device(1)
        self.left = self.device(-1)

    def device(self, offset, core=None):
        place = lax.rem(self.place + offset + self.chips, self.chips)
        return 2 * chip_at(place) + (self.core if core is None else core)


class RingGather:
    def __init__(self, ring, source, slots, sems):
        self.ring, self.source, self.slots = ring, source, slots
        self.sems = sems
        self.far = ring.chips // 2
        self.rows = slots.shape[1]

    def copy(self, offset, target, kind, index, half=None):
        block = self.ring.device(offset)
        src = self.source if offset == 0 else self.slots.at[block]
        dst = self.slots.at[block]
        if half is not None:
            rows = pl.ds(half * (self.rows // 2), self.rows // 2)
            src, dst = src.at[rows], dst.at[rows]
        return pltpu.make_async_remote_copy(
            src_ref=src,
            dst_ref=dst,
            send_sem=self.sems[2 * kind].at[index],
            recv_sem=self.sems[2 * kind + 1].at[index],
            device_id={"fsdp": target},
            device_id_type=MESH,
        )

    def rightward(self, s):
        return self.copy(-s, self.ring.right, 0, s, 0 if s + 1 == self.far else None)

    def leftward(self, s):
        return self.copy(s, self.ring.left, 1, s, 1 if s + 1 == self.far else None)

    def across(self, offset):
        index = 0 if offset == 0 else 2 * abs(offset) - (1 if offset < 0 else 0)
        return self.copy(offset, self.ring.partner, 2, index)

    def arrived(self, s):
        half = self.far == s
        self.copy(-s, self.ring.right, 0, s - 1, 0 if half else None).wait_recv()
        self.copy(s, self.ring.left, 1, s - 1, 1 if half else None).wait_recv()

    def offsets(self, s):
        return [s] if s == self.far else [-s, s]

    def begin(self):
        self.rightward(0).start()
        self.leftward(0).start()
        self.across(0).start()

    def advance(self, s):
        self.arrived(s)
        if s < self.far:
            self.rightward(s).start()
            self.leftward(s).start()
        for offset in self.offsets(s):
            self.across(offset).start()

    def from_partner(self, offset):
        block = self.ring.device(offset, 1 - self.ring.core)
        index = 0 if offset == 0 else 2 * abs(offset) - (1 if offset < 0 else 0)
        pltpu.make_async_remote_copy(
            src_ref=self.slots.at[block],
            dst_ref=self.slots.at[block],
            send_sem=self.sems[4].at[index],
            recv_sem=self.sems[5].at[index],
            device_id={"fsdp": self.ring.partner},
            device_id_type=MESH,
        ).wait_recv()

    def end(self):
        for s in range(self.far):
            self.rightward(s).wait_send()
            self.leftward(s).wait_send()
        self.across(0).wait_send()
        for s in range(1, self.far + 1):
            for offset in self.offsets(s):
                self.across(offset).wait_send()


def gather_sems(chips):
    far = chips // 2
    dma = pltpu.SemaphoreType.DMA
    return [dma((far,))] * 4 + [dma((2 * far + 1,))] * 2


class RingSum:
    def __init__(self, ring, partial, arena, rows, cols, sems):
        self.ring, self.partial = ring, partial
        self.arena, self.rows, self.cols = arena, rows, cols
        (
            self.stage_send,
            self.pair_recv,
            self.right_send,
            self.right_recv,
            self.left_send,
            self.left_recv,
        ) = sems
        far = ring.chips // 2
        self.far = far
        offsets = [far]
        for s in range(far - 1, 0, -1):
            offsets += [s, -s]
        self.offsets = offsets + [0]
        self.at = {offset: i for i, offset in enumerate(self.offsets)}

    def view(self, slot, rows=None):
        return self.arena.at[slot, pl.ds(0, self.rows) if rows is None else rows, pl.ds(0, self.cols)]

    def stage(self, i):
        return self.view(i % 2)

    def pair(self, i, rows=None):
        return self.view(2 + i, rows)

    def side(self, right, s, rows=None):
        return self.view(2 + self.ring.chips + (0 if right else self.far) + s - 1, rows)

    def half(self, which):
        return pl.ds(which * (self.rows // 2), self.rows // 2)

    def pair_copy(self, i):
        return pltpu.make_async_remote_copy(
            src_ref=self.stage(i),
            dst_ref=self.pair(i),
            send_sem=self.stage_send.at[i],
            recv_sem=self.pair_recv.at[i],
            device_id={"fsdp": self.ring.partner},
            device_id_type=MESH,
        )

    def by_columns(self, piece):
        wide = 4 * LANES

        def body(j, _):
            piece(pl.ds(pl.multiple_of(j * wide, wide), wide))
            return 0

        lax.fori_loop(0, self.cols // wide, body, 0)

    def pair_step(self, i):
        offset = self.offsets[i]
        if i >= 2:
            self.pair_copy(i - 2).wait_send()
        owner = self.ring.device(offset, 1 - self.ring.core)
        rows = pl.ds(0, self.rows)

        def piece(at):
            self.arena[i % 2, rows, at] = self.partial(owner, at).astype(BF16)

        self.by_columns(piece)
        self.pair_copy(i).start()

    def pair_add(self, i):
        owner = self.ring.device(self.offsets[i])
        self.pair_copy(i).wait_recv()
        rows = pl.ds(0, self.rows)

        def piece(at):
            mine = self.partial(owner, at)
            there = (2 + i, rows, at)
            self.arena[there] = (mine + self.arena[there].astype(F32)).astype(BF16)

        self.by_columns(piece)

    def pair_all(self, between=None):
        last = len(self.offsets)
        for i in range(last):
            self.pair_step(i)
            if i >= 1:
                self.pair_add(i - 1)
                self.launch_free(i - 1)
            if between is not None:
                between(i)
        self.pair_add(last - 1)
        for i in range(max(last - 2, 0), last):
            self.pair_copy(i).wait_send()

    def hop(self, s, right, which):
        owner = self.at[s if right or s == self.far else -s]
        rows = self.half(which)
        return pltpu.make_async_remote_copy(
            src_ref=self.pair(owner, rows),
            dst_ref=self.side(right, s, rows),
            send_sem=(self.right_send if right else self.left_send).at[s - 1, which],
            recv_sem=(self.right_recv if right else self.left_recv).at[s - 1, which],
            device_id={"fsdp": self.ring.right if right else self.ring.left},
            device_id_type=MESH,
        )

    def hops(self):
        far = self.far
        moves = [(far, True, 0), (far, False, 1)]
        if far > 1:
            moves += [(far - 1, True, 1), (far - 1, False, 0)]
            moves += [(far - 1, True, 0), (far - 1, False, 1)]
        for s in range(far - 2, 0, -1):
            for which in range(2):
                moves += [(s, True, which), (s, False, which)]
        return moves

    def free(self, s, right, which):
        return s == self.far or (s == self.far - 1 and which == (1 if right else 0))

    def launch_free(self, i):
        offset = self.offsets[i]
        for s, right, which in self.hops():
            owner = s if right or s == self.far else -s
            if self.free(s, right, which) and owner == offset:
                self.hop(s, right, which).start()

    def launch(self):
        for s, right, which in self.hops():
            if not self.free(s, right, which):
                self.hop(s + 1, right, which).wait_recv()
                owner = self.at[s if right else -s]
                rows = self.half(which)
                arrived = self.side(right, s + 1, rows)
                mine = self.pair(owner, rows)
                mine[...] = (mine[...].astype(F32) + arrived[...].astype(F32)).astype(BF16)
                self.hop(s, right, which).start()

    def finish(self):
        for s, right, which in self.hops():
            if s == 1:
                self.hop(s, right, which).wait_recv()
            self.hop(s, right, which).wait_send()

    def by_rows(self, piece):
        step = self.rows // 4

        def body(i, _):
            piece(pl.ds(pl.multiple_of(i * step, step), step))
            return 0

        lax.fori_loop(0, 4, body, 0)

    def value(self, rows):
        own = self.pair(self.at[0], rows)[...].astype(F32)
        left = self.side(True, 1, rows)[...].astype(F32)
        return own + left + self.side(False, 1, rows)[...].astype(F32)


def sum_sems(chips):
    far = chips // 2
    dma = pltpu.SemaphoreType.DMA
    return [dma((chips,))] * 2 + [dma((far, 2))] * 4


def back_kernel(
    sizes,
    a2_ref,
    cot_ref,
    wgate_ref,
    wup_ref,
    wdown_ref,
    wout_ref,
    wqkv_ref,
    h1_ref,
    q_in,
    o_in,
    a1_in,
    x_in,
    k_in,
    v_in,
    lse_in,
    mask_in,
    turn_in,
    gain1_ref,
    gain2_ref,
    result_out,
    gtok_out,
    gains_ref,
    gate_out,
    up_out,
    down_out,
    query_out,
    output_out,
    rows_all,
    gz_ref,
    *scratch,
):
    ctx_n, fsdp_n = sizes
    (
        zown,
        zrout,
        zsums,
        zrin,
        zdone,
        az,
        arena,
        dh1,
        gqkv,
        dkv,
        dkv_in,
        gslot,
        cslot,
    ) = scratch[:13]
    scratch = scratch[13:]
    zsems, scratch = scratch[:8], scratch[8:]
    gsems, scratch = scratch[:6], scratch[6:]
    da2_sems, scratch = scratch[:6], scratch[6:]
    out_sems, scratch = scratch[:6], scratch[6:]
    ysems, scratch = scratch[:6], scratch[6:]
    xsems, scratch = scratch[:6], scratch[6:]
    (
        dkv_send,
        dkv_recv,
        gain_send,
        gain_recv,
        cgain_send,
        cgain_recv,
        wsem,
        isem,
        ssem,
        ready,
    ) = scratch
    ctx = lax.axis_index("ctx")
    fsdp = lax.axis_index("fsdp")
    ring = Ring(fsdp_n, fsdp)
    count, width = a2_ref.shape
    block = count // 2
    keys = k_in.shape[0] // 2
    scale = HD ** (-0.5)
    shard = query_out.shape[0]
    cols = gqkv.shape[1]
    local = wgate_ref.shape[0]
    key_cols = KV * HD

    barrier = pltpu.get_barrier_semaphore()
    for axis, me, n in (("ctx", ctx, ctx_n), ("fsdp", fsdp, fsdp_n)):
        for step in range(1, n):
            pl.semaphore_signal(
                barrier, 1, device_id={axis: lax.rem(me + step, n)}, device_id_type=MESH
            )
    pl.semaphore_wait(barrier, ctx_n + fsdp_n - 2)

    rounds = [0]

    def settle():
        sem = ready.at[rounds[0]]
        rounds[0] += 1
        for target in (ring.partner, ring.left, ring.right):
            pl.semaphore_signal(sem, 1, device_id={"fsdp": target}, device_id_type=MESH)
        pl.semaphore_wait(sem, 3)

    line = LineSum(
        ctx_n,
        ctx,
        gz_ref.shape[0],
        az.shape[1] // (2 * LANES),
        (gz_ref, az),
        (gate_out, up_out, down_out, query_out, output_out),
        (zown, zrout, zsums, zrin, zdone),
        zsems,
    )
    clock = [0]

    def ticks(number):
        start = clock[0]
        clock[0] = start + number

        def body(i, _):
            line.tick(i)
            return 0

        lax.fori_loop(start, start + number, body, 0)

    gather = RingGather(ring, a2_ref, rows_all, gsems)
    gather.begin()

    def ring_sum(partial, rows, wide, sems):
        return RingSum(ring, partial, arena, rows, wide, sems)

    def feed_forward(wgate, wup, wdown, hb, abuf, cbuf, stage):
        loads = [
            pltpu.make_async_copy(wdown_ref, wdown, isem.at[0]),
            pltpu.make_async_copy(wgate_ref, wgate, isem.at[1]),
            pltpu.make_async_copy(wup_ref, wup, isem.at[2]),
            pltpu.make_async_copy(a2_ref, rows_all.at[fsdp], isem.at[3]),
            pltpu.make_async_copy(a2_ref, abuf.at[0], isem.at[4]),
            pltpu.make_async_copy(h1_ref, dh1, isem.at[5]),
        ]

        def cot_load(f):
            slot = 2 + lax.rem(f, 2)
            return pltpu.make_async_copy(cot_ref.at[f], abuf.at[slot], wsem.at[slot - 2])

        cot_load(0).start()
        for load in loads:
            load.start()
        loads[0].wait()

        def dhid(f, _):
            pl.when(f + 1 < fsdp_n)(lambda: cot_load(f + 1).start())
            cot_load(f).wait()
            hb[2, f] = through(abuf[2 + lax.rem(f, 2)], wdown[...]).astype(BF16)
            return 0

        lax.fori_loop(0, fsdp_n, dhid, 0)
        for load in loads[1:]:
            load.wait()

        def fetch(f, slot):
            return pltpu.make_async_copy(rows_all.at[f], abuf.at[slot], isem.at[slot])

        def gates(f, slot):
            rows = abuf[slot]
            hidden, dgate, dup = gate_back(
                hb[2, f].astype(F32), through(rows, wgate[...]), through(rows, wup[...])
            )
            hb[0, f] = dgate
            hb[1, f] = dup
            hb[2, f] = hidden

        gates(fsdp, 0)
        gather.from_partner(0)
        fetch(ring.partner, 1).start()
        fetch(ring.partner, 1).wait()
        gates(ring.partner, 1)
        for s in range(1, gather.far + 1):
            gather.advance(s)
            offsets = gather.offsets(s)
            blocks = [ring.device(offset) for offset in offsets]
            blocks += [ring.device(offset, 1 - ring.core) for offset in offsets]
            for i in range(len(offsets)):
                fetch(blocks[i], i).start()
            for i, offset in enumerate(offsets):
                gather.from_partner(offset)
                fetch(blocks[len(offsets) + i], len(offsets) + i).start()

            def each(i, _, blocks=blocks):
                f = blocks[0]
                for j in range(1, len(blocks)):
                    f = jnp.where(i == j, blocks[j], f)
                fetch(f, i).wait()
                gates(f, i)
                return 0

            lax.fori_loop(0, len(blocks), each, 0)
        gather.end()

        wide = 2 * LANES
        per_kind = width // wide
        total = 3 * per_kind

        def chunk_load(m, start):
            slot = lax.rem(m, 2)
            at = pl.multiple_of(lax.rem(m, per_kind) * wide, wide)
            for source, use in ((rows_all, m < 2 * per_kind), (cot_ref, m >= 2 * per_kind)):
                copy = pltpu.make_async_copy(
                    source.at[:, :, pl.ds(at, wide)], cbuf.at[slot], wsem.at[slot]
                )
                pl.when(use)(copy.start if start else copy.wait)

        def chunk_store(m):
            slot = lax.rem(m, 2)
            return pltpu.make_async_copy(
                stage.at[slot], gz_ref.at[pl.ds(2 * m, 2)], ssem.at[slot]
            )

        def gradients(m, lo):
            slot = lax.rem(m, 2)
            pl.when(m + 1 < total)(lambda: chunk_load(jnp.minimum(m + 1, total - 1), True))
            chunk_load(m, False)
            right = cbuf[slot].reshape(fsdp_n * count, wide)
            left = hb[m // per_kind].reshape(fsdp_n * count, local)
            out = across(left, right).astype(BF16)
            pl.when(m >= lo + 2)(lambda: chunk_store(jnp.maximum(m - 2, 0)).wait())
            stage[slot, 0] = out[:, :LANES]
            stage[slot, 1] = out[:, LANES:]
            chunk_store(m).start()

        def run(lo, hi, every=0):
            start = clock[0]

            def body(m, _):
                gradients(m, lo)
                if every:
                    pl.when(lax.rem(m - lo, every) == every - 1)(
                        lambda: line.tick(start + (m - lo) // every)
                    )
                return 0

            lax.fori_loop(lo, hi, body, 0)
            for m in (hi - 2, hi - 1):
                chunk_store(jnp.int32(m)).wait()
            if every:
                clock[0] = start + (hi - lo) // every

        chunk_load(jnp.int32(0), True)
        head = 4
        run(0, head)
        ticks(3)

        def da2_partial(f, at):
            return matmul(hb[0, f], wgate[:, at]) + matmul(hb[1, f], wup[:, at])

        da2 = ring_sum(da2_partial, count, width, da2_sems)
        da2.pair_all(lambda i: ticks(1) if i < 3 else None)
        middle = head + (total - head) // 2
        run(head, middle, 3)
        da2.launch()
        run(middle, total, 3)
        own_cot = pltpu.make_async_copy(cot_ref.at[fsdp], abuf.at[0], isem.at[0])
        own_cot.start()
        da2.finish()
        own_cot.wait()
        gain = gain2_ref[...]
        piece = count // 4

        def norm_back(i, acc):
            rows = pl.ds(pl.multiple_of(i * piece, piece), piece)
            hidden = dh1[rows]
            grad = da2.value(rows)
            factor = lax.rsqrt(jnp.mean(hidden * hidden, -1, keepdims=True) + EPSILON)
            unit = hidden * factor
            dh1[rows] = abuf[0, rows].astype(F32) + normed_back(unit, factor, grad, gain)
            return acc + jnp.sum(grad * unit, 0, keepdims=True)

        gain2_sum = lax.fori_loop(0, 4, norm_back, jnp.zeros((1, width), F32))
        gslot[fsdp, 1:2] = gain2_sum
        settle()

        def out_partial(f, at):
            return matmul(hb[2, f], wdown[:, at])

        mlp_out = ring_sum(out_partial, count, width, out_sems)
        mlp_out.pair_all(lambda i: ticks(1))
        holder.append(mlp_out)

    holder = []
    pl.run_scoped(
        feed_forward,
        pltpu.VMEM((local, width), BF16),
        pltpu.VMEM((local, width), BF16),
        pltpu.VMEM((local, width), BF16),
        pltpu.VMEM((3, fsdp_n, count, local), BF16),
        pltpu.VMEM((4, count, width), BF16),
        pltpu.VMEM((2, fsdp_n, count, 2 * LANES), BF16),
        pltpu.VMEM((2, 2, local, LANES), BF16),
    )
    mlp_out = holder[0]

    def attention_back(
        q_ref, o_ref, do_ref, a1_ref, dhb_ref, k_ref, v_ref, lse_ref, mask_ref, turn_ref,
        h1_buf, obuf, wbuf, kz, vz, dk_acc, dv_acc,
    ):
        loads = [
            pltpu.make_async_copy(src, dst, isem.at[i])
            for i, (src, dst) in enumerate(
                [
                    (q_in, q_ref),
                    (o_in, o_ref),
                    (a1_in, a1_ref),
                    (k_in, k_ref),
                    (v_in, v_ref),
                    (lse_in, lse_ref),
                    (mask_in, mask_ref),
                    (turn_in, turn_ref),
                ]
            )
        ]

        def wout_load(f):
            return pltpu.make_async_copy(wout_ref.at[f], obuf.at[f % 2], wsem.at[f % 2])

        wout_load(0).start()
        for load in loads:
            load.start()
        dhb_ref[...] = dh1[...].astype(BF16)
        for f in range(fsdp_n):
            if f + 1 < fsdp_n:
                wout_load(f + 1).start()
            wout_load(f).wait()
            term = through(dhb_ref[:, f * shard : (f + 1) * shard], obuf[f % 2])
            h1_buf[...] = term if f == 0 else h1_buf[...] + term
        do_ref[...] = h1_buf[...].astype(BF16)
        h1_load = pltpu.make_async_copy(h1_ref, h1_buf, ssem.at[0])
        h1_load.start()
        ticks(1)
        mlp_out.launch()
        for load in loads:
            load.wait()

        step_keys = min(keys, 4 * LANES)

        def piece(par, q4, do4, lse, delta, at, mask, grad_q):
            span = pl.ds(at, step_keys)
            k_part = kz[par, span]
            v_part = vz[par, span]
            scores = through(q4, k_part)
            if mask is not None:
                scores = scores + mask
            probs = jnp.exp(scores - lse)
            dprob = through(do4, v_part)
            dscore = (probs * (dprob - delta)).astype(BF16)
            dk_acc[par, span] += across(dscore, q4)
            dv_acc[par, span] += across(probs.astype(BF16), do4)
            return grad_q + matmul(dscore, k_part)

        def group_step(group, rb):
            rows = pl.ds(rb * block, block)
            q4 = stacked(q_ref, rows, group) * jnp.asarray(scale, BF16)
            do4 = stacked(do_ref, rows, group)
            prod = do4.astype(F32) * stacked(o_ref, rows, group).astype(F32)
            lse_all = lse_ref[rb]
            grad_q = jnp.zeros((PAIRS * block, LANES), F32)
            for par in range(2):
                lse = jnp.sum(
                    jnp.where(lanes_of(lse_all.shape) == 2 * group + par, lse_all, 0.0),
                    -1,
                    keepdims=True,
                )
                delta = jnp.sum(
                    jnp.where(lanes_of(prod.shape) // HD == par, prod, 0.0), -1, keepdims=True
                )
                for at in range(0, (rb + 1) * keys, step_keys):
                    mask = None
                    if at >= rb * keys:
                        mask = mask_ref[rb, :, pl.ds(at - rb * keys, step_keys)]
                        mask = jnp.concatenate([mask] * PAIRS, 0)
                    grad_q = piece(par, q4, do4, lse, delta, at, mask, grad_q)
            grad_q = grad_q * scale
            cosine, sine = turn_ref[0, rows], turn_ref[1, rows]
            for j in range(PAIRS):
                part = grad_q[j * block : (j + 1) * block]
                at = pl.multiple_of((group * PAIRS + j) * LANES, LANES)
                gqkv[rows, pl.ds(at, LANES)] = (part * cosine - turned(part) * sine).astype(BF16)

        def dkv_copy(owner, tile, step):
            return pltpu.make_async_remote_copy(
                src_ref=dkv.at[owner, tile],
                dst_ref=dkv_in.at[ctx, tile],
                send_sem=dkv_send.at[step, tile],
                recv_sem=dkv_recv.at[step, tile],
                device_id={"ctx": owner},
                device_id_type=MESH,
            )

        def attention(lo, hi):
            start = clock[0]

            def body(group, _):
                spread_heads(k_ref, kz, group)
                spread_heads(v_ref, vz, group)
                dk_acc[...] = jnp.zeros_like(dk_acc)
                dv_acc[...] = jnp.zeros_like(dv_acc)
                for rb in range(2):
                    group_step(group, rb)
                    line.tick(start + (group - lo) * 2 + rb)
                tile = group // 2
                for which, acc in enumerate((dk_acc, dv_acc)):
                    for part in range(ctx_n):
                        for rb in range(2):
                            span = pl.ds(rb * keys + part * block, block)
                            both = jnp.where(
                                lanes_of((block, LANES)) < HD, acc[0, span], acc[1, span]
                            )
                            both = both + roll_lanes(both, HD)
                            there = (part, tile, which, pl.ds(rb * block, block))
                            mine = lanes_of((block, LANES)) // HD == lax.rem(group, 2)
                            dkv[there] = jnp.where(mine, both.astype(BF16), dkv[there])
                return 0

            lax.fori_loop(lo, hi, body, 0)
            clock[0] = start + (hi - lo) * 2

        def send_dkv(tile):
            for step in range(1, ctx_n):
                dkv_copy(lax.rem(ctx + step, ctx_n), tile, step - 1).start()

        attention(0, 2)
        send_dkv(0)
        mlp_out.finish()
        h1_load.wait()

        def add_out(rows):
            h1_buf[rows] = h1_buf[rows] + mlp_out.value(rows)

        mlp_out.by_rows(add_out)
        settle()

        def output_partial(f, at):
            return across(dhb_ref[:, pl.ds(pl.multiple_of(f * shard, shard), shard)], o_ref[:, at])

        ysum = ring_sum(output_partial, shard, width, ysems)
        ysum.pair_all(lambda i: ticks(1))
        attention(2, 3)
        ysum.launch()
        attention(3, 4)
        send_dkv(1)
        ticks(2)
        do_ref[...] = h1_buf[...].astype(BF16)
        result_copy = pltpu.make_async_copy(do_ref, result_out, isem.at[0])
        result_copy.start()
        ysum.finish()

        def keep_output(rows):
            az[rows, cols:] = ysum.value(rows).astype(BF16)

        ysum.by_rows(keep_output)
        settle()
        x_load = pltpu.make_async_copy(x_in, q_ref, isem.at[1])
        x_load.start()

        for step in range(1, ctx_n):
            for tile in range(KV // 2):
                dkv_copy(lax.rem(ctx + step, ctx_n), tile, step - 1).wait_send()
                sender = lax.rem(ctx - step + ctx_n, ctx_n)
                pltpu.make_async_remote_copy(
                    src_ref=dkv.at[sender, tile],
                    dst_ref=dkv_in.at[sender, tile],
                    send_sem=dkv_send.at[step - 1, tile],
                    recv_sem=dkv_recv.at[step - 1, tile],
                    device_id={"ctx": sender},
                    device_id_type=MESH,
                ).wait_recv()
        cosine, sine = turn_ref[0], turn_ref[1]
        for tile in range(KV // 2):
            for which in range(2):
                part = dkv[ctx, tile, which].astype(F32)
                for step in range(1, ctx_n):
                    part = part + dkv_in[lax.rem(ctx + step, ctx_n), tile, which].astype(F32)
                if which == 0:
                    part = part * cosine - turned(part) * sine
                at = width + which * key_cols + tile * LANES
                gqkv[:, at : at + LANES] = part.astype(BF16)

        def query_partial(f, at):
            return across(a1_ref[:, pl.ds(pl.multiple_of(f * shard, shard), shard)], gqkv[:, at])

        xsum = ring_sum(query_partial, shard, cols, xsems)
        xsum.pair_all(lambda i: ticks(1))
        ticks(2)
        xsum.launch()
        ticks(2)

        def weight_copy(f):
            return pltpu.make_async_copy(wqkv_ref.at[f], wbuf.at[f % 2], wsem.at[f % 2])

        weight_copy(0).start()
        for f in range(fsdp_n):
            if f + 1 < fsdp_n:
                weight_copy(f + 1).start()
            weight_copy(f).wait()
            h1_buf[:, f * shard : (f + 1) * shard] = through(gqkv[...], wbuf[f % 2])
        x_load.wait()
        gain = gain1_ref[...]
        piece_rows = count // 4

        def norm_back(i, acc):
            rows = pl.ds(pl.multiple_of(i * piece_rows, piece_rows), piece_rows)
            x = q_ref[rows].astype(F32)
            grad = h1_buf[rows]
            factor = lax.rsqrt(jnp.mean(x * x, -1, keepdims=True) + EPSILON)
            unit = x * factor
            o_ref[rows] = (dh1[rows] + normed_back(unit, factor, grad, gain)).astype(BF16)
            return acc + jnp.sum(grad * unit, 0, keepdims=True)

        gslot[fsdp, 0:1] = lax.fori_loop(0, 4, norm_back, jnp.zeros((1, width), F32))
        gtok_copy = pltpu.make_async_copy(o_ref, gtok_out, isem.at[2])
        gtok_copy.start()

        def gain_copy(slots, axis, here, step, sems):
            n = fsdp_n if axis == "fsdp" else ctx_n
            return pltpu.make_async_remote_copy(
                src_ref=slots.at[here],
                dst_ref=slots.at[here],
                send_sem=sems[0].at[step - 1],
                recv_sem=sems[1].at[step - 1],
                device_id={axis: lax.rem((fsdp if axis == "fsdp" else ctx) + step, n)},
                device_id_type=MESH,
            )

        def exchange(slots, axis, n, me, sems):
            for step in range(1, n):
                gain_copy(slots, axis, me, step, sems).start()
            for step in range(1, n):
                gain_copy(slots, axis, me, step, sems).wait_send()
                gain_copy(slots, axis, lax.rem(me - step + n, n), step, sems).wait_recv()
            total = slots[0]
            for i in range(1, n):
                total = total + slots[i]
            return total

        cslot[ctx] = exchange(gslot, "fsdp", fsdp_n, fsdp, (gain_send, gain_recv))
        gains_ref[...] = exchange(cslot, "ctx", ctx_n, ctx, (cgain_send, cgain_recv))

        xsum.finish()

        def keep_query(rows):
            az[rows, :cols] = xsum.value(rows).astype(BF16)

        xsum.by_rows(keep_query)
        result_copy.wait()
        gtok_copy.wait()

    total_keys = k_in.shape[0]
    rows_type = pltpu.VMEM((count, width), BF16)
    pl.run_scoped(
        attention_back,
        rows_type,
        rows_type,
        rows_type,
        rows_type,
        rows_type,
        pltpu.VMEM(k_in.shape, BF16),
        pltpu.VMEM(v_in.shape, BF16),
        pltpu.VMEM(lse_in.shape, F32),
        pltpu.VMEM(mask_in.shape, F32),
        pltpu.VMEM(turn_in.shape, F32),
        pltpu.VMEM((count, width), F32),
        pltpu.VMEM((2,) + wout_ref.shape[1:], BF16),
        pltpu.VMEM((2,) + wqkv_ref.shape[1:], BF16),
        pltpu.VMEM((2, total_keys, LANES), BF16),
        pltpu.VMEM((2, total_keys, LANES), BF16),
        pltpu.VMEM((2, total_keys, LANES), F32),
        pltpu.VMEM((2, total_keys, LANES), F32),
    )
    ticks(line.ticks - clock[0])


def back(
    a2, cot, w_gate, w_up, w_down, w_out, wqkv, h1, q, o, a1, x, k_all, v_all, lse, mask, turn,
    gain_one, gain_two,
):
    ctx_n = lax.axis_size("ctx")
    fsdp_n = lax.axis_size("fsdp")
    count, width = q.shape
    local = w_gate.shape[0]
    shard, cols = wqkv.shape[1:]
    chips = fsdp_n // 2
    far = chips // 2
    vmem = pl.BlockSpec(memory_space=pltpu.VMEM)
    hbm = pl.BlockSpec(memory_space=pl.ANY)
    dma = pltpu.SemaphoreType.DMA
    regular = pltpu.SemaphoreType.REGULAR
    zbuf = pltpu.VMEM((SLOTS, local, LANES), BF16)
    scratch = (
        [zbuf] * 5
        + [
            pltpu.VMEM((shard, cols + width), BF16),
            pltpu.VMEM((2 + chips + 2 * far, max(count, shard), cols), BF16),
            pltpu.VMEM((count, width), F32),
            pltpu.VMEM((count, cols), BF16),
            pltpu.VMEM((ctx_n, KV // 2, 2, count, LANES), BF16),
            pltpu.VMEM((ctx_n, KV // 2, 2, count, LANES), BF16),
            pltpu.VMEM((fsdp_n, 2, width), F32),
            pltpu.VMEM((ctx_n, 2, width), F32),
        ]
        + [dma((SLOTS,))] * 5
        + [dma((SLOTS, 2)), regular, regular]
        + gather_sems(chips)
        + sum_sems(chips) * 4
        + [
            dma((ctx_n - 1, KV // 2)),
            dma((ctx_n - 1, KV // 2)),
            dma((fsdp_n - 1,)),
            dma((fsdp_n - 1,)),
            dma((ctx_n - 1,)),
            dma((ctx_n - 1,)),
            dma((2,)),
            dma((9,)),
            dma((2,)),
            regular((4,)),
        ]
    )
    return pl.pallas_call(
        functools.partial(back_kernel, (ctx_n, fsdp_n)),
        out_shape=(
            jax.ShapeDtypeStruct((count, width), BF16),
            jax.ShapeDtypeStruct((count, width), BF16),
            jax.ShapeDtypeStruct((2, width), F32),
            jax.ShapeDtypeStruct((local, width), BF16),
            jax.ShapeDtypeStruct((local, width), BF16),
            jax.ShapeDtypeStruct((local, width), BF16),
            jax.ShapeDtypeStruct((shard, cols), BF16),
            jax.ShapeDtypeStruct((shard, width), BF16),
            jax.ShapeDtypeStruct((fsdp_n, count, width), BF16),
            jax.ShapeDtypeStruct((3 * width // LANES, local, LANES), BF16),
        ),
        in_specs=[hbm] * 17 + [vmem] * 2,
        out_specs=(hbm, hbm, vmem) + (hbm,) * 7,
        scratch_shapes=scratch,
        compiler_params=pltpu.CompilerParams(
            collective_id=1, has_side_effects=True, vmem_limit_bytes=VMEM_LIMIT
        ),
        name="back",
    )(
        a2, cot, w_gate, w_up, w_down, w_out, wqkv, h1, q, o, a1, x, k_all, v_all, lse, mask, turn,
        gain_one, gain_two,
    )[:8]


def shards(
    tokens,
    cotangent,
    block_table,
    gain_attn,
    w_query,
    w_key,
    w_value,
    w_output,
    gain_mlp,
    w_gate,
    w_up,
    w_down,
):
    ctx_n = lax.axis_size("ctx")
    ctx = lax.axis_index("ctx")
    count, width = tokens.shape[1:]
    block = count // 2
    local = w_gate.shape[1]

    table = block_table.reshape(ctx_n, 2)
    lower, upper = jnp.min(table, 1), jnp.max(table, 1)
    owned = table[ctx]
    swap = owned[0] > owned[1]

    def ordered(rows):
        return jnp.where(swap, jnp.concatenate([rows[block:], rows[:block]], 0), rows)

    offsets = jnp.arange(block, dtype=jnp.int32)
    spots = jnp.stack([lower, upper])[:, :, None] * block + offsets
    own_spots = spots[:, ctx]
    key_spots = spots.reshape(2, -1)
    mask = jnp.where(own_spots[:, :, None] >= key_spots[:, None, :], 0.0, NEGATIVE).astype(F32)
    freqs = 10000.0 ** (-jnp.arange(HD // 2, dtype=F32) / (HD // 2))
    angle = own_spots.reshape(-1).astype(F32)[:, None] * freqs[None, :]
    angle = jnp.concatenate([angle] * (LANES * 2 // HD), -1)
    turn = jnp.stack([jnp.cos(angle), jnp.sin(angle)])

    rows_in = ordered(tokens[0])
    grad_out = ordered(cotangent[0])

    wqkv = lax.all_gather(jnp.concatenate([w_query, w_key, w_value], 1), "fsdp", axis=0)
    full_output = lax.all_gather(w_output, "fsdp", axis=0)
    inputs = rows_in.astype(F32)
    normal_one = normed(inputs, gain_attn)[2]
    qkv = matmul(normal_one, wqkv.reshape(width, -1))

    def rotary(values):
        heads = values.reshape(count, -1, HD)
        middle = HD // 2
        spun = jnp.concatenate([-heads[..., middle:], heads[..., :middle]], -1)
        cosine, sine = turn[:, :, None, :HD]
        return (heads * cosine + spun * sine).reshape(count, -1).astype(BF16)

    key_cols = KV * HD
    queries = rotary(qkv[:, :width])
    keys_own = rotary(qkv[:, width : width + key_cols])
    values_own = qkv[:, width + key_cols :].astype(BF16)

    def gathered(rows):
        every = lax.all_gather(rows, "ctx", axis=0).reshape(ctx_n, 2, block, key_cols)
        return every.transpose(1, 0, 2, 3).reshape(-1, key_cols)

    keys_all, values_all = gathered(keys_own), gathered(values_own)
    mixed, lse = attend(queries, keys_all, values_all, mask)
    attn_out = lax.dot_general(
        mixed, full_output, (((1,), (1,)), ((), ())), preferred_element_type=F32
    ).reshape(count, width)
    hidden_one = inputs + attn_out
    normal_two = normed(hidden_one, gain_mlp)[2]
    grad_all = lax.all_gather(grad_out, "fsdp", axis=0)
    result, grad_tokens, gains, gate_sum, up_sum, down_sum, query_sum, output_sum = back(
        normal_two,
        grad_all,
        w_gate.T,
        w_up.T,
        w_down,
        full_output,
        wqkv,
        hidden_one,
        queries,
        mixed,
        normal_one,
        rows_in,
        keys_all,
        values_all,
        lse,
        mask,
        turn,
        gain_attn[None],
        gain_mlp[None],
    )
    query_sum = query_sum.astype(F32)
    return (
        ordered(result)[None],
        ordered(grad_tokens)[None],
        query_sum[:, :width],
        query_sum[:, width : width + key_cols],
        query_sum[:, width + key_cols :],
        output_sum.T.astype(F32),
        gate_sum.astype(F32).T,
        up_sum.astype(F32).T,
        down_sum.astype(F32),
        gains[0],
        gains[1],
    )


def solution(mesh):
    in_specs = (
        P("fsdp", "ctx", None),
        P("fsdp", "ctx", None),
        P(),
        P(),
        P("fsdp", None),
        P("fsdp", None),
        P("fsdp", None),
        P(None, "fsdp"),
        P(),
        P(None, "fsdp"),
        P(None, "fsdp"),
        P("fsdp", None),
    )
    out_specs = (
        P("fsdp", "ctx", None),
        P("fsdp", "ctx", None),
        P("fsdp", None),
        P("fsdp", None),
        P("fsdp", None),
        P(None, "fsdp"),
        P(None, "fsdp"),
        P(None, "fsdp"),
        P("fsdp", None),
        P(),
        P(),
    )
    return jax.shard_map(shards, mesh=mesh, in_specs=in_specs, out_specs=out_specs, check_vma=False)
```

```python
import functools

import jax
import jax.numpy as jnp
from jax import lax
from jax.experimental import pallas as pl
from jax.experimental.pallas import tpu as pltpu
from jax.sharding import PartitionSpec as P

H = 32
KV = 4
HD = 64
GROUP = H // KV
PAIRS = GROUP // 2
LANES = 128

EPSILON = 1e-05
NEGATIVE = -1e30
SLOTS = 8
GAP = 3
VMEM_LIMIT = 61 * 1024 * 1024
MESH = pl.DeviceIdType.MESH
F32 = jnp.float32
BF16 = jnp.bfloat16


def dot(left, right, left_dim, right_dim):
    return lax.dot_general(
        left, right, (((left_dim,), (right_dim,)), ((), ())), preferred_element_type=F32
    )


def matmul(left, right):
    return dot(left, right, 1, 0)


def across(left, right):
    return dot(left, right, 0, 0)


def through(left, right):
    return dot(left, right, 1, 1)


def normed(hidden, gain):
    factor = lax.rsqrt(jnp.mean(hidden * hidden, -1, keepdims=True) + EPSILON)
    unit = hidden * factor
    return (unit, factor, (unit * gain).astype(BF16))


def normed_back(unit, factor, grad_in, gain):
    scaled = grad_in * gain
    return factor * (scaled - unit * jnp.mean(scaled * unit, -1, keepdims=True))


def gate_back(grad_hidden, gate, up):
    sigma = jax.nn.sigmoid(gate)
    activated = gate * sigma
    grad_gate_in = (grad_hidden * up * sigma * (1.0 + gate * (1.0 - sigma))).astype(BF16)
    grad_up_in = (grad_hidden * activated).astype(BF16)
    return ((activated * up).astype(BF16), grad_gate_in, grad_up_in)


def lanes_of(shape):
    return lax.broadcasted_iota(jnp.int32, shape, len(shape) - 1)


def roll_lanes(value, amount):
    return pltpu.roll(value, amount, 1)


def turned(value):
    first = lax.rem(lanes_of(value.shape), HD) < HD // 2
    return jnp.where(first, -roll_lanes(value, LANES - HD // 2), roll_lanes(value, HD // 2))


def stacked(ref, rows, group):
    wide = PAIRS * LANES
    block = ref[rows, pl.ds(pl.multiple_of(group * wide, wide), wide)]
    return jnp.concatenate([block[:, j * LANES : (j + 1) * LANES] for j in range(PAIRS)], 0)


def spread_heads(kv_ref, which, out_ref, group):
    devices, _, count, _ = kv_ref.shape
    block = count // 2
    at = pl.multiple_of((group // 2) * LANES, LANES)
    here = lax.rem(group, 2)
    for part in range(devices):
        tile = kv_ref[part, which, :, pl.ds(at, LANES)].astype(F32)
        other = roll_lanes(tile, HD)
        half = lanes_of(tile.shape) // HD
        for par in range(2):
            picked = jnp.where(here == par, tile, other)
            picked = jnp.where(half == par, picked, 0.0).astype(BF16)
            for rb in range(2):
                rows = pl.ds((rb * devices + part) * block, block)
                out_ref[par, rows] = picked[rb * block : (rb + 1) * block]


def attend_group(group, q_ref, kz, vz, mask_ref, o_ref, lse_ref):
    block = q_ref.shape[0] // 2
    keys = kz.shape[1] // 2
    together = PAIRS if keys <= 4 * LANES else PAIRS // 2
    for rb in range(2):
        rows = pl.ds(rb * block, block)
        every = stacked(q_ref, rows, group) * jnp.asarray(HD ** (-0.5), BF16)
        mask = jnp.concatenate([mask_ref[rb]] * together, 0)
        for first in range(0, PAIRS, together):
            some = slice(first * block, (first + together) * block)
            q4 = every[some]
            total = 0.0
            lse = lse_ref[rb, some]
            for par in range(2):
                scores = []
                for part in range(rb + 1):
                    score = through(q4, kz[par, pl.ds(part * keys, keys)])
                    scores.append(score + mask if part == rb else score)
                peak = functools.reduce(
                    jnp.maximum, [jnp.max(s, -1, keepdims=True) for s in scores]
                )
                probs = [jnp.exp(s - peak) for s in scores]
                norm = sum(jnp.sum(p, -1, keepdims=True) for p in probs)
                mixed = sum(
                    matmul(p.astype(BF16), vz[par, pl.ds(i * keys, keys)])
                    for i, p in enumerate(probs)
                )
                total = total + mixed / norm
                here = lanes_of(lse.shape) == 2 * group + par
                lse = jnp.where(here, peak + jnp.log(norm), lse)
            lse_ref[rb, some] = lse
            for j in range(together):
                at = pl.multiple_of((group * PAIRS + first + j) * LANES, LANES)
                o_ref[rows, pl.ds(at, LANES)] = total[j * block : (j + 1) * block].astype(BF16)


class LineSum:
    def __init__(self, count, index, first, second, sources, targets, bufs, sems):
        self.n = count
        self.first, self.second = first, second
        self.total = first + second
        self.mlp_src, self.att_src = sources
        self.gate_dst, self.up_dst, self.down_dst, self.query_dst, self.output_dst = targets
        self.own, self.rout, self.sums, self.rin, self.done = bufs
        (
            self.load_sem,
            self.in_send,
            self.rout_sem,
            self.rin_sem,
            self.out_send,
            self.store_sem,
            self.credit_in,
            self.credit_out,
        ) = sems
        half = count // 2
        left = index < half
        self.depth = jnp.where(left, index, count - 1 - index)
        step = jnp.where(left, 1, -1)
        self.inward = index + step
        outward = index - step
        self.has_out = self.depth > 0
        self.outward = jnp.where(self.has_out, outward, index + step)
        self.is_mid = self.depth == half - 1
        deepest = half - 1
        self.lag_sum = 1 + GAP * self.depth
        self.lag_sent = self.lag_sum + GAP
        self.lag_total = 1 + GAP * deepest + GAP + GAP * (deepest - self.depth)
        self.lag_end = self.lag_total + GAP
        self.ticks = self.total + 1 + 3 * GAP * deepest + 3 * GAP
        self.att_rows = 2 * self.att_src.shape[0]
        self.blocks = self.down_dst.shape[1] // LANES

    def view(self, buf, slot, att):
        return buf.at[slot, pl.ds(0, self.att_rows)] if att else buf.at[slot]

    def each(self, chunk, body):
        slot = lax.rem(jnp.maximum(chunk, 0), SLOTS)
        pl.when((chunk >= 0) & (chunk < self.first))(lambda: body(chunk, slot, False))
        if self.second:
            pl.when((chunk >= self.first) & (chunk < self.total))(lambda: body(chunk, slot, True))

    def send(self, src, dst, sems, target, slot, att):
        return pltpu.make_async_remote_copy(
            src_ref=self.view(src, slot, att),
            dst_ref=self.view(dst, slot, att),
            send_sem=sems[0].at[slot],
            recv_sem=sems[1].at[slot],
            device_id={"ctx": target},
            device_id_type=MESH,
        )

    def to_total(self, slot, att):
        return self.send(self.sums, self.rin, (self.in_send, self.rin_sem), self.inward, slot, att)

    def to_partial(self, slot, att):
        return self.send(
            self.sums, self.rout, (self.in_send, self.rout_sem), self.inward, slot, att
        )

    def to_outward(self, slot, att):
        return self.send(
            self.done, self.rin, (self.out_send, self.rin_sem), self.outward, slot, att
        )

    def load(self, chunk, slot):
        return pltpu.make_async_copy(
            self.mlp_src.at[chunk], self.own.at[slot], self.load_sem.at[slot]
        )

    def stores(self, chunk, slot, att):
        if att:
            rows = self.att_rows // 2
            wide = self.output_dst.shape[1] // LANES
            pairs = []
            for i in range(2):
                at = 2 * (chunk - self.first) + i
                src = self.done.at[slot, pl.ds(i * rows, rows)]
                sem = self.store_sem.at[slot, i]
                o_at = pl.multiple_of(jnp.minimum(at, wide - 1) * LANES, LANES)
                q_at = pl.multiple_of(jnp.maximum(at - wide, 0) * LANES, LANES)
                pairs.append(
                    (
                        at < wide,
                        pltpu.make_async_copy(src, self.output_dst.at[:, pl.ds(o_at, LANES)], sem),
                    )
                )
                pairs.append(
                    (
                        at >= wide,
                        pltpu.make_async_copy(src, self.query_dst.at[:, pl.ds(q_at, LANES)], sem),
                    )
                )
            return pairs
        kind = chunk // self.blocks
        at = pl.multiple_of(lax.rem(chunk, self.blocks) * LANES, LANES)
        sem = self.store_sem.at[slot, 0]
        return [
            (kind == i, pltpu.make_async_copy(self.done.at[slot], dst.at[:, pl.ds(at, LANES)], sem))
            for i, dst in enumerate((self.gate_dst, self.up_dst, self.down_dst))
        ]

    def tick(self, i):
        self.each(i - self.lag_sum + 1, self.stage_load)
        self.each(i - self.lag_sum, self.stage_sum)
        self.each(i - self.lag_sent, self.stage_sent)
        self.each(i - self.lag_total, self.stage_total)
        self.each(i - self.lag_end, self.stage_end)

    def stage_load(self, chunk, slot, att):
        if not att:
            self.load(chunk, slot).start()

    def stage_sum(self, chunk, slot, att):
        if not att:
            self.load(chunk, slot).wait()

        def own():
            if not att:
                return self.own[slot]
            at = (chunk - self.first) * 2 * LANES
            return jnp.concatenate(
                [
                    self.att_src[:, pl.ds(pl.multiple_of(at + i * LANES, LANES), LANES)]
                    for i in range(2)
                ],
                0,
            )

        @pl.when(self.has_out)
        def _():
            self.to_partial(slot, att).wait_recv()
            arrived = self.view(self.rout, slot, att)[...].astype(F32)
            self.view(self.sums, slot, att)[...] = (own().astype(F32) + arrived).astype(BF16)

            @pl.when(chunk < self.total - SLOTS)
            def _():
                pl.semaphore_signal(
                    self.credit_in, 1, device_id={"ctx": self.outward}, device_id_type=MESH
                )

        @pl.when(jnp.logical_not(self.has_out))
        def _():
            self.view(self.sums, slot, att)[...] = own()

        @pl.when(chunk >= SLOTS)
        def _():
            pl.semaphore_wait(self.credit_in, 1)

        pl.when(self.is_mid)(lambda: self.to_total(slot, att).start())
        pl.when(jnp.logical_not(self.is_mid))(lambda: self.to_partial(slot, att).start())

    def stage_sent(self, chunk, slot, att):
        self.to_total(slot, att).wait_send()

    def stage_total(self, chunk, slot, att):
        self.to_total(slot, att).wait_recv()
        arrived = self.view(self.rin, slot, att)
        done = self.view(self.done, slot, att)

        @pl.when(self.is_mid)
        def _():
            mine = self.view(self.sums, slot, att)[...].astype(F32)
            done[...] = (mine + arrived[...].astype(F32)).astype(BF16)

            @pl.when(chunk < self.total - SLOTS)
            def _():
                pl.semaphore_signal(
                    self.credit_in, 1, device_id={"ctx": self.inward}, device_id_type=MESH
                )

        @pl.when(jnp.logical_not(self.is_mid))
        def _():
            done[...] = arrived[...]

            @pl.when(chunk < self.total - SLOTS)
            def _():
                pl.semaphore_signal(
                    self.credit_out, 1, device_id={"ctx": self.inward}, device_id_type=MESH
                )

        @pl.when(self.has_out)
        def _():
            @pl.when(chunk >= SLOTS)
            def _():
                pl.semaphore_wait(self.credit_out, 1)

            self.to_outward(slot, att).start()

        for condition, copy in self.stores(chunk, slot, att):
            pl.when(condition)(copy.start)

    def stage_end(self, chunk, slot, att):
        pl.when(self.has_out)(lambda: self.to_outward(slot, att).wait_send())
        for condition, copy in self.stores(chunk, slot, att):
            pl.when(condition)(copy.wait)


def chip_at(place):
    return 2 * (place // 2) + lax.rem(place + place // 2, 2)


class Ring:
    def __init__(self, count, index):
        self.chips = count // 2
        chip = index // 2
        self.core = lax.rem(index, 2)
        self.place = chip_at(chip)
        self.partner = 2 * chip + 1 - self.core
        self.right = self.device(1)
        self.left = self.device(-1)

    def device(self, offset, core=None):
        place = lax.rem(self.place + offset + self.chips, self.chips)
        return 2 * chip_at(place) + (self.core if core is None else core)


class RingGather:
    def __init__(self, ring, source, slots, sems, mate=None, odd=None):
        self.ring, self.source, self.slots = ring, source, slots
        self.sems, self.mate = sems, mate
        self.far = ring.chips // 2
        rows = slots.shape[1]
        self.share = rows // 4 if mate is not None else 0
        self.rows = rows - self.share
        if mate is None:
            self.start, self.give, self.take = 0, 0, 0
        else:
            self.start = pl.multiple_of(odd * self.share, 16)
            self.give = pl.multiple_of(odd * self.rows, 16)
            self.take = pl.multiple_of((1 - odd) * self.rows, 16)

    def span(self, half=None):
        if half is None:
            return pl.ds(self.start, self.rows)
        size = self.rows // 2
        return pl.ds(self.start + half * size, size)

    def move(self, src, dst, kind, index, target):
        return pltpu.make_async_remote_copy(
            src_ref=src,
            dst_ref=dst,
            send_sem=self.sems[2 * kind].at[index],
            recv_sem=self.sems[2 * kind + 1].at[index],
            device_id=target,
            device_id_type=MESH,
        )

    def copy(self, offset, target, kind, index, rows):
        block = self.ring.device(offset)
        src = self.source if offset == 0 else self.slots.at[block]
        return self.move(
            src.at[rows], self.slots.at[block, rows], kind, index, {"fsdp": target}
        )

    def rightward(self, s, half):
        return self.copy(-s, self.ring.right, 0, (s, half), self.span(half))

    def leftward(self, s, half):
        return self.copy(s, self.ring.left, 1, (s, half), self.span(half))

    def firsts(self, s):
        return [self.rightward(s, 0), self.leftward(s, 1)]

    def seconds(self, s):
        return [self.rightward(s, 1), self.leftward(s, 0)] if s + 1 < self.far else []

    def coming(self, s, half_left, half_right):
        return [
            self.copy(-s, self.ring.right, 0, (s - 1, half_left), self.span(half_left)),
            self.copy(s, self.ring.left, 1, (s - 1, half_right), self.span(half_right)),
        ]

    def index(self, offset):
        return 0 if offset == 0 else 2 * abs(offset) - (1 if offset < 0 else 0)

    def across(self, offset):
        rows = pl.ds(0, self.rows + self.share) if offset == 0 else self.span()
        return self.copy(offset, self.ring.partner, 2, self.index(offset), rows)

    def across_share(self, offset):
        rows = pl.ds(self.take, self.share)
        return self.copy(offset, self.ring.partner, 3, self.index(offset), rows)

    def to_mate(self, offset, core=None):
        block = self.ring.device(offset)
        rows = pl.ds(self.give, self.share)
        place = self.slots.at[block, rows]
        return self.move(place, place, 4, self.index(offset), {"ctx": self.mate})

    def offsets(self, s):
        return [s] if s == self.far else [-s, s]

    def begin(self):
        for message in self.firsts(0) + self.seconds(0):
            message.start()
        self.across(0).start()

    def advance(self, s):
        for message in self.coming(s, 0, 1):
            message.wait_recv()
        if s < self.far:
            for message in self.firsts(s):
                message.start()

    def settle(self, s):
        if s < self.far:
            for message in self.coming(s, 1, 0):
                message.wait_recv()
            for message in self.seconds(s):
                message.start()
        for offset in self.offsets(s):
            self.across(offset).start()
            if self.share:
                self.to_mate(offset).start()

    def complete(self, s):
        if self.share:
            for offset in self.offsets(s):
                block = self.ring.device(offset)
                place = self.slots.at[block, pl.ds(self.take, self.share)]
                self.move(
                    place, place, 4, self.index(offset), {"ctx": self.mate}
                ).wait_recv()
                self.across_share(offset).start()

    def from_partner(self, offset):
        block = self.ring.device(offset, 1 - self.ring.core)
        rows = pl.ds(0, self.rows + self.share) if offset == 0 else self.span()
        index = self.index(offset)
        target = {"fsdp": self.ring.partner}
        place = self.slots.at[block, rows]
        self.move(place, place, 2, index, target).wait_recv()
        if self.share and offset != 0:
            place = self.slots.at[block, pl.ds(self.take, self.share)]
            self.move(place, place, 3, index, target).wait_recv()

    def blocks(self, s):
        offsets = [0] if s == 0 else self.offsets(s)
        return [self.ring.device(o) for o in offsets] + [
            self.ring.device(o, 1 - self.ring.core) for o in offsets
        ]

    def all_from_partner(self, s):
        for offset in [0] if s == 0 else self.offsets(s):
            self.from_partner(offset)

    def end(self):
        for s in range(self.far):
            for message in self.firsts(s) + self.seconds(s):
                message.wait_send()
        self.across(0).wait_send()
        for s in range(1, self.far + 1):
            for offset in self.offsets(s):
                self.across(offset).wait_send()
                if self.share:
                    self.across_share(offset).wait_send()
                    self.to_mate(offset).wait_send()


def gather_sems(chips):
    far = chips // 2
    dma = pltpu.SemaphoreType.DMA
    return [dma((far, 2))] * 4 + [dma((2 * far + 1,))] * 6


def pick(index, choices):
    out = choices[0]
    for i, choice in enumerate(choices[1:]):
        out = jnp.where(index == i + 1, choice, out)
    return out


class RingSum:
    def __init__(self, ring, partial, arena, rows, cols, sems, first=0):
        self.ring, self.partial, self.first = ring, partial, first
        self.arena, self.rows, self.cols = arena, rows, cols
        (
            self.stage_send,
            self.pair_recv,
            self.right_send,
            self.right_recv,
            self.left_send,
            self.left_recv,
        ) = sems
        far = ring.chips // 2
        self.far = far
        offsets = [far]
        for s in range(far - 1, 0, -1):
            offsets += [s, -s]
        self.offsets = offsets + [0]
        self.at = {offset: i for i, offset in enumerate(self.offsets)}

    def view(self, slot, rows=None):
        rows = pl.ds(0, self.rows) if rows is None else rows
        return self.arena.at[slot, rows, pl.ds(self.first, self.cols)]

    def stage(self, i):
        return self.view(i % 2)

    def pair(self, i, rows=None):
        return self.view(2 + i, rows)

    def side(self, right, s, rows=None):
        return self.view(2 + self.ring.chips + (0 if right else self.far) + s - 1, rows)

    def half(self, which):
        return pl.ds(which * (self.rows // 2), self.rows // 2)

    def pair_copy(self, i):
        return pltpu.make_async_remote_copy(
            src_ref=self.stage(i),
            dst_ref=self.pair(i),
            send_sem=self.stage_send.at[i],
            recv_sem=self.pair_recv.at[i],
            device_id={"fsdp": self.ring.partner},
            device_id_type=MESH,
        )

    def by_columns(self, piece):
        wide = 4 * LANES

        def body(j, _):
            at = pl.multiple_of(j * wide, wide)
            piece(pl.ds(at, wide), pl.ds(pl.multiple_of(self.first + at, wide), wide))
            return 0

        lax.fori_loop(0, self.cols // wide, body, 0)

    def pair_step(self, i):
        offset = self.offsets[i]
        if i >= 2:
            self.pair_copy(i - 2).wait_send()
        owner = self.ring.device(offset, 1 - self.ring.core)
        rows = pl.ds(0, self.rows)

        def piece(at, place):
            self.arena[i % 2, rows, place] = self.partial(owner, at).astype(BF16)

        self.by_columns(piece)
        self.pair_copy(i).start()

    def pair_add(self, i):
        owner = self.ring.device(self.offsets[i])
        self.pair_copy(i).wait_recv()
        rows = pl.ds(0, self.rows)

        def piece(at, place):
            mine = self.partial(owner, at)
            there = (2 + i, rows, place)
            self.arena[there] = (mine + self.arena[there].astype(F32)).astype(BF16)

        self.by_columns(piece)

    def pair_all(self, between=None):
        last = len(self.offsets)
        for i in range(last):
            self.pair_step(i)
            if i >= 1:
                self.pair_add(i - 1)
                self.launch_free(i - 1)
            if between is not None:
                between(i)
        self.pair_add(last - 1)
        for i in range(max(last - 2, 0), last):
            self.pair_copy(i).wait_send()

    def hop(self, s, right, which):
        owner = self.at[s if right or s == self.far else -s]
        rows = self.half(which)
        return pltpu.make_async_remote_copy(
            src_ref=self.pair(owner, rows),
            dst_ref=self.side(right, s, rows),
            send_sem=(self.right_send if right else self.left_send).at[s - 1, which],
            recv_sem=(self.right_recv if right else self.left_recv).at[s - 1, which],
            device_id={"fsdp": self.ring.right if right else self.ring.left},
            device_id_type=MESH,
        )

    def hops(self):
        far = self.far
        moves = [(far, True, 0), (far, False, 1)]
        if far > 1:
            moves += [(far - 1, True, 1), (far - 1, False, 0)]
            moves += [(far - 1, True, 0), (far - 1, False, 1)]
        for s in range(far - 2, 0, -1):
            for which in range(2):
                moves += [(s, True, which), (s, False, which)]
        return moves

    def free(self, s, right, which):
        return s == self.far or (s == self.far - 1 and which == (1 if right else 0))

    def launch_free(self, i):
        offset = self.offsets[i]
        for s, right, which in self.hops():
            owner = s if right or s == self.far else -s
            if self.free(s, right, which) and owner == offset:
                self.hop(s, right, which).start()

    def launch(self):
        for s, right, which in self.hops():
            if not self.free(s, right, which):
                self.hop(s + 1, right, which).wait_recv()
                owner = self.at[s if right else -s]
                rows = self.half(which)
                arrived = self.side(right, s + 1, rows)
                mine = self.pair(owner, rows)
                mine[...] = (mine[...].astype(F32) + arrived[...].astype(F32)).astype(BF16)
                self.hop(s, right, which).start()

    def finish(self):
        for s, right, which in self.hops():
            if s == 1:
                self.hop(s, right, which).wait_recv()
            self.hop(s, right, which).wait_send()

    def by_rows(self, piece):
        step = self.rows // 4

        def body(i, _):
            piece(pl.ds(pl.multiple_of(i * step, step), step))
            return 0

        lax.fori_loop(0, 4, body, 0)

    def value(self, rows):
        own = self.pair(self.at[0], rows)[...].astype(F32)
        left = self.side(True, 1, rows)[...].astype(F32)
        return own + left + self.side(False, 1, rows)[...].astype(F32)


def sum_sems(chips):
    far = chips // 2
    dma = pltpu.SemaphoreType.DMA
    return [dma((chips,))] * 2 + [dma((far, 2))] * 4


def layer_kernel(
    sizes,
    x_in,
    cot_in,
    wq_in,
    wkv_in,
    wout_in,
    wgate_ref,
    wup_ref,
    wdown_ref,
    mask_in,
    turn_in,
    gain1_ref,
    gain2_ref,
    result_out,
    gtok_out,
    gains_ref,
    gate_out,
    up_out,
    down_out,
    query_out,
    output_out,
    rows_all,
    gz_ref,
    wq_ref,
    wkv_ref,
    wout_ref,
    cot_ref,
    q_in,
    o_in,
    a1_in,
    h1_ref,
    lse_in,
    *scratch,
):
    ctx_n, fsdp_n = sizes
    (
        zown,
        zrout,
        zsums,
        zrin,
        zdone,
        az,
        arena,
        dh1,
        dkv_in,
        kv,
        gslot,
        cslot,
    ) = scratch[:12]
    scratch = scratch[12:]
    zsems, scratch = scratch[:8], scratch[8:]
    gathers, scratch = [scratch[10 * i : 10 * i + 10] for i in range(5)], scratch[50:]
    da2_sems, scratch = scratch[:6], scratch[6:]
    out_sems, scratch = scratch[:6], scratch[6:]
    ysems, scratch = scratch[:6], scratch[6:]
    xsems, scratch = scratch[:6], scratch[6:]
    kvsems, scratch = scratch[:6], scratch[6:]
    (
        dkv_send,
        dkv_recv,
        kv_send,
        kv_recv,
        gain_send,
        gain_recv,
        cgain_send,
        cgain_recv,
        wsem,
        isem,
        ssem,
        ready,
    ) = scratch
    ctx = lax.axis_index("ctx")
    fsdp = lax.axis_index("fsdp")
    ring = Ring(fsdp_n, fsdp)
    count, width = x_in.shape
    block = count // 2
    keys = ctx_n * block
    scale = HD ** (-0.5)
    shard = query_out.shape[0]
    cols = query_out.shape[1]
    local = wgate_ref.shape[0]
    key_cols = KV * HD

    barrier = pltpu.get_barrier_semaphore()
    for axis, me, n in (("ctx", ctx, ctx_n), ("fsdp", fsdp, fsdp_n)):
        for step in range(1, n):
            pl.semaphore_signal(
                barrier, 1, device_id={axis: lax.rem(me + step, n)}, device_id_type=MESH
            )
    pl.semaphore_wait(barrier, ctx_n + fsdp_n - 2)

    rounds = [0]

    def settle():
        sem = ready.at[rounds[0]]
        rounds[0] += 1
        for target in (ring.partner, ring.left, ring.right):
            pl.semaphore_signal(sem, 1, device_id={"fsdp": target}, device_id_type=MESH)
        pl.semaphore_wait(sem, 3)

    line = LineSum(
        ctx_n,
        ctx,
        gz_ref.shape[0],
        az.shape[1] // (2 * LANES),
        (gz_ref, az),
        (gate_out, up_out, down_out, query_out, output_out),
        (zown, zrout, zsums, zrin, zdone),
        zsems,
    )
    clock = [0]

    def ticks(number):
        start = clock[0]
        clock[0] = start + number

        def body(i, _):
            line.tick(i)
            return 0

        lax.fori_loop(start, start + number, body, 0)

    odd = lax.rem(ctx, 2)
    mate = ctx + 1 - 2 * odd
    help_along = ()
    wkv_gather = RingGather(ring, wkv_in, wkv_ref, gathers[0], *help_along)
    wq_gather = RingGather(ring, wq_in, wq_ref, gathers[1], *help_along)
    wout_gather = RingGather(ring, wout_in, wout_ref, gathers[2], mate, odd)
    cot_gather = RingGather(ring, cot_in, cot_ref, gathers[3])
    gather = RingGather(ring, rows_all.at[fsdp], rows_all, gathers[4])
    far = gather.far

    def forward(x_ref, a1_ref, wkv, acc, wbuf, q_ref, o_ref, kz, vz, mask_ref, turn_ref, lse_ref, obuf):
        wkv_gather.begin()
        loads = [
            pltpu.make_async_copy(src, dst, isem.at[i])
            for i, (src, dst) in enumerate(
                [
                    (x_in, x_ref),
                    (mask_in, mask_ref),
                    (turn_in, turn_ref),
                    (wkv_in, wkv.at[fsdp]),
                    (wq_in, wbuf.at[0]),
                    (wout_in, obuf.at[0]),
                    (cot_in, o_ref),
                ]
            )
        ]
        owns = [
            pltpu.make_async_copy(src, dst, isem.at[3 + i])
            for i, (src, dst) in enumerate(
                [
                    (wkv.at[fsdp], wkv_ref.at[fsdp]),
                    (wbuf.at[0], wq_ref.at[fsdp]),
                    (obuf.at[0], wout_ref.at[fsdp]),
                    (o_ref, cot_ref.at[fsdp]),
                ]
            )
        ]
        for load in loads:
            load.start()
        wkv_gather.advance(1)
        wq_gather.begin()
        loads[0].wait()
        gain = gain1_ref[...]
        step_rows = count // 4

        def norm_one(i, _):
            rows = pl.ds(pl.multiple_of(i * step_rows, step_rows), step_rows)
            a1_ref[rows] = normed(x_ref[rows].astype(F32), gain)[2]
            return 0

        lax.fori_loop(0, 4, norm_one, 0)
        a1_store = pltpu.make_async_copy(a1_ref, a1_in, ssem.at[0])
        a1_store.start()
        for load in loads[1:]:
            load.wait()
        for own in owns:
            own.start()

        wkv_gather.settle(1)
        for s in range(2, far + 1):
            wkv_gather.advance(s)
            wkv_gather.settle(s)
        for s in range(1, far + 1):
            wkv_gather.complete(s)
        for s in range(0, far + 1):
            wkv_gather.all_from_partner(s)
        owns[0].wait()
        wkv_load = pltpu.make_async_copy(wkv_ref, wkv, wsem.at[0])
        wkv_load.start()
        wkv_load.wait()
        pairs = matmul(a1_ref[...], wkv[...].reshape(width, 2 * key_cols))
        cosine, sine = turn_ref[0], turn_ref[1]
        for tile in range(2 * key_cols // LANES):
            part = pairs[:, tile * LANES : (tile + 1) * LANES]
            which, at = tile * LANES // key_cols, tile * LANES % key_cols
            if which == 0:
                part = part * cosine + turned(part) * sine
            kv[ctx, which, :, at : at + LANES] = part.astype(BF16)

        def kv_copy(source, target, step):
            return pltpu.make_async_remote_copy(
                src_ref=kv.at[source],
                dst_ref=kv.at[source],
                send_sem=kv_send.at[step - 1],
                recv_sem=kv_recv.at[step - 1],
                device_id={"ctx": target},
                device_id_type=MESH,
            )

        for step in range(1, ctx_n):
            kv_copy(ctx, lax.rem(ctx + step, ctx_n), step).start()

        def wq_load(f, slot):
            return pltpu.make_async_copy(wq_ref.at[f], wbuf.at[slot], wsem.at[slot])

        def add_queries(blocks, first):
            for i, f in enumerate(blocks):
                wq_load(f, i).start()

            def one(i, _):
                f = pick(i, blocks)
                wq_load(f, i).wait()
                left = a1_ref[:, pl.ds(pl.multiple_of(f * shard, shard), shard)]
                acc[...] += matmul(left, wbuf[i])
                return 0

            if first:
                acc[...] = jnp.zeros_like(acc)
            lax.fori_loop(0, len(blocks), one, 0)

        for own in owns[1:]:
            own.wait()
        wq_gather.all_from_partner(0)
        add_queries(wq_gather.blocks(0), True)
        for s in range(1, far + 1):
            wq_gather.advance(s)
            if s == max(far - 1, 1):
                wout_gather.begin()
            wq_gather.settle(s)
            wq_gather.complete(s)
            wq_gather.all_from_partner(s)
            add_queries(wq_gather.blocks(s), False)

        def turn_tile(j, _):
            at = pl.ds(pl.multiple_of(j * LANES, LANES), LANES)
            part = acc[:, at]
            q_ref[:, at] = (part * turn_ref[0] + turned(part) * turn_ref[1]).astype(BF16)
            return 0

        lax.fori_loop(0, width // LANES, turn_tile, 0)
        a1_store.wait()
        q_store = pltpu.make_async_copy(q_ref, q_in, ssem.at[0])
        q_store.start()
        for step in range(1, ctx_n):
            kv_copy(ctx, lax.rem(ctx + step, ctx_n), step).wait_send()
            sender = lax.rem(ctx - step + ctx_n, ctx_n)
            kv_copy(sender, sender, step).wait_recv()

        lse_ref[...] = jnp.zeros_like(lse_ref)

        def groups(lo, hi):
            def body(group, _):
                spread_heads(kv, 0, kz, group)
                spread_heads(kv, 1, vz, group)
                attend_group(group, q_ref, kz, vz, mask_ref, o_ref, lse_ref)
                return 0

            lax.fori_loop(lo, hi, body, 0)

        groups(0, 2)
        for s in range(1, far):
            wout_gather.advance(s)
            if s < far - 1:
                wout_gather.settle(s)
        cot_gather.begin()
        groups(2, KV)
        q_store.wait()
        stores = [
            pltpu.make_async_copy(o_ref, o_in, isem.at[0]),
            pltpu.make_async_copy(lse_ref, lse_in, isem.at[1]),
        ]
        for store in stores:
            store.start()
        def wout_load(f, slot):
            return pltpu.make_async_copy(wout_ref.at[f], obuf.at[slot], wsem.at[slot])

        for s in range(0, far + 1):
            if s == 0:
                for late in range(max(far - 1, 1), far + 1):
                    if late == far:
                        wout_gather.advance(late)
                    wout_gather.settle(late)
            if s:
                wout_gather.complete(s)
            wout_gather.all_from_partner(s)
            blocks = wout_gather.blocks(s)
            for i in range(len(blocks)):
                wout_load(blocks[i], i).start()

            def project(i, _, blocks=blocks):
                f = pick(i, blocks)
                wout_load(f, i).wait()
                at = pl.ds(pl.multiple_of(f * shard, shard), shard)
                dh1[:, at] = x_ref[:, at].astype(F32) + matmul(o_ref[...], obuf[i])
                return 0

            lax.fori_loop(0, len(blocks), project, 0)
        gain = gain2_ref[...]

        def norm_two(i, _):
            rows = pl.ds(pl.multiple_of(i * step_rows, step_rows), step_rows)
            a1_ref[rows] = normed(dh1[rows], gain)[2]
            return 0

        lax.fori_loop(0, 4, norm_two, 0)
        a2_store = pltpu.make_async_copy(a1_ref, rows_all.at[fsdp], ssem.at[0])
        a2_store.start()
        h1_store = pltpu.make_async_copy(dh1, h1_ref, ssem.at[1])
        h1_store.start()
        a2_store.wait()
        gather.begin()
        h1_store.wait()
        for store in stores:
            store.wait()
        wkv_gather.end()
        wq_gather.end()
        wout_gather.end()

    rows_type = pltpu.VMEM((count, width), BF16)
    pl.run_scoped(
        forward,
        rows_type,
        rows_type,
        pltpu.VMEM(wkv_ref.shape, BF16),
        pltpu.VMEM((count, width), F32),
        pltpu.VMEM((4,) + wq_ref.shape[1:], BF16),
        rows_type,
        rows_type,
        pltpu.VMEM((2, 2 * keys, LANES), BF16),
        pltpu.VMEM((2, 2 * keys, LANES), BF16),
        pltpu.VMEM(mask_in.shape, F32),
        pltpu.VMEM(turn_in.shape, F32),
        pltpu.VMEM(lse_in.shape, F32),
        pltpu.VMEM((4,) + wout_ref.shape[1:], BF16),
    )

    def ring_sum(partial, rows, wide, sems, first=0):
        return RingSum(ring, partial, arena, rows, wide, sems, first)

    def feed_forward(wgate, wup, wdown, hb, abuf, cbuf, stage):
        loads = [
            pltpu.make_async_copy(wdown_ref, wdown, isem.at[4]),
            pltpu.make_async_copy(wgate_ref, wgate, isem.at[5]),
            pltpu.make_async_copy(wup_ref, wup, isem.at[6]),
        ]
        for load in loads:
            load.start()

        def each(source, blocks, body):
            def fetch(f, slot):
                return pltpu.make_async_copy(source.at[f], abuf.at[slot], isem.at[slot])

            for i, f in enumerate(blocks):
                fetch(f, i).start()

            def step(i, _):
                f = pick(i, blocks)
                fetch(f, i).wait()
                body(f, i)
                return 0

            lax.fori_loop(0, len(blocks), step, 0)

        def dhid(f, slot):
            hb[2, f] = through(abuf[slot], wdown[...]).astype(BF16)

        def gates(f, slot):
            rows = abuf[slot]
            hidden, dgate, dup = gate_back(
                hb[2, f].astype(F32), through(rows, wgate[...]), through(rows, wup[...])
            )
            hb[0, f] = dgate
            hb[1, f] = dup
            hb[2, f] = hidden

        for load in loads:
            load.wait()
        for s in range(far + 1):
            if s == 1:
                cot_gather.advance(s)
            if s:
                cot_gather.settle(s)
            cot_gather.all_from_partner(s)
            each(cot_ref, cot_gather.blocks(s), dhid)
            if s:
                gather.advance(s)
                if s < far:
                    cot_gather.advance(s + 1)
                gather.settle(s)
            gather.all_from_partner(s)
            each(rows_all, gather.blocks(s), gates)
        cot_gather.end()
        gather.end()

        wide = 2 * LANES
        per_kind = width // wide
        total = 3 * per_kind

        def chunk_load(m, start):
            slot = lax.rem(m, 2)
            at = pl.multiple_of(lax.rem(m, per_kind) * wide, wide)
            for source, use in ((rows_all, m < 2 * per_kind), (cot_ref, m >= 2 * per_kind)):
                copy = pltpu.make_async_copy(
                    source.at[:, :, pl.ds(at, wide)], cbuf.at[slot], wsem.at[slot]
                )
                pl.when(use)(copy.start if start else copy.wait)

        def chunk_store(m):
            slot = lax.rem(m, 2)
            return pltpu.make_async_copy(
                stage.at[slot], gz_ref.at[pl.ds(2 * m, 2)], ssem.at[slot]
            )

        def gradients(m, lo):
            slot = lax.rem(m, 2)
            pl.when(m + 1 < total)(lambda: chunk_load(jnp.minimum(m + 1, total - 1), True))
            chunk_load(m, False)
            right = cbuf[slot].reshape(fsdp_n * count, wide)
            left = hb[m // per_kind].reshape(fsdp_n * count, local)
            out = across(left, right).astype(BF16)
            pl.when(m >= lo + 2)(lambda: chunk_store(jnp.maximum(m - 2, 0)).wait())
            stage[slot, 0] = out[:, :LANES]
            stage[slot, 1] = out[:, LANES:]
            chunk_store(m).start()

        def run(lo, hi, every=0):
            start = clock[0]

            def body(m, _):
                gradients(m, lo)
                if every:
                    pl.when(lax.rem(m - lo, every) == every - 1)(
                        lambda: line.tick(start + (m - lo) // every)
                    )
                return 0

            lax.fori_loop(lo, hi, body, 0)
            for m in (hi - 2, hi - 1):
                chunk_store(jnp.int32(m)).wait()
            if every:
                clock[0] = start + (hi - lo) // every

        chunk_load(jnp.int32(0), True)
        head = 4
        run(0, head)
        ticks(3)

        def da2_partial(f, at):
            return matmul(hb[0, f], wgate[:, at]) + matmul(hb[1, f], wup[:, at])

        da2 = ring_sum(da2_partial, count, width, da2_sems)
        da2.pair_all(lambda i: ticks(1))
        middle = head + (total - head) // 2
        run(head, middle, 3)
        da2.launch()
        run(middle, total, 3)
        ticks(1)
        own_cot = pltpu.make_async_copy(cot_ref.at[fsdp], abuf.at[0], isem.at[0])
        own_cot.start()
        da2.finish()
        own_cot.wait()
        gain = gain2_ref[...]
        piece = count // 4

        def norm_back(i, acc):
            rows = pl.ds(pl.multiple_of(i * piece, piece), piece)
            hidden = dh1[rows]
            grad = da2.value(rows)
            factor = lax.rsqrt(jnp.mean(hidden * hidden, -1, keepdims=True) + EPSILON)
            unit = hidden * factor
            dh1[rows] = abuf[0, rows].astype(F32) + normed_back(unit, factor, grad, gain)
            return acc + jnp.sum(grad * unit, 0, keepdims=True)

        gain2_sum = lax.fori_loop(0, 4, norm_back, jnp.zeros((1, width), F32))
        gslot[fsdp, 1:2] = gain2_sum
        settle()

        def out_partial(f, at):
            return matmul(hb[2, f], wdown[:, at])

        mlp_out = ring_sum(out_partial, count, width, out_sems)
        mlp_out.pair_all(lambda i: ticks(1))
        holder.append(mlp_out)

    holder = []
    pl.run_scoped(
        feed_forward,
        pltpu.VMEM((local, width), BF16),
        pltpu.VMEM((local, width), BF16),
        pltpu.VMEM((local, width), BF16),
        pltpu.VMEM((3, fsdp_n, count, local), BF16),
        pltpu.VMEM((4, count, width), BF16),
        pltpu.VMEM((2, fsdp_n, count, 2 * LANES), BF16),
        pltpu.VMEM((2, 2, local, LANES), BF16),
    )
    mlp_out = holder[0]

    def attention_back(
        q_ref, o_ref, do_ref, a1_ref, dhb_ref, lse_ref, mask_ref, turn_ref,
        h1_buf, obuf, wbuf, wkv, kz, vz, dk_acc, dv_acc, gqkv, dkv,
    ):
        loads = [
            pltpu.make_async_copy(src, dst, isem.at[i])
            for i, (src, dst) in enumerate(
                [
                    (q_in, q_ref),
                    (o_in, o_ref),
                    (a1_in, a1_ref),
                    (lse_in, lse_ref),
                    (mask_in, mask_ref),
                    (turn_in, turn_ref),
                ]
            )
        ]

        def wout_load(f):
            return pltpu.make_async_copy(wout_ref.at[f], obuf.at[f % 2], wsem.at[f % 2])

        wout_load(0).start()
        for load in loads:
            load.start()
        dhb_ref[...] = dh1[...].astype(BF16)
        for f in range(fsdp_n):
            if f + 1 < fsdp_n:
                wout_load(f + 1).start()
            wout_load(f).wait()
            term = through(dhb_ref[:, f * shard : (f + 1) * shard], obuf[f % 2])
            h1_buf[...] = term if f == 0 else h1_buf[...] + term
        do_ref[...] = h1_buf[...].astype(BF16)
        h1_load = pltpu.make_async_copy(h1_ref, h1_buf, ssem.at[0])
        h1_load.start()
        ticks(2)
        mlp_out.launch()
        for load in loads:
            load.wait()

        step_keys = min(keys, 4 * LANES)

        def piece(par, q4, do4, lse, delta, at, mask, grad_q):
            span = pl.ds(at, step_keys)
            k_part = kz[par, span]
            v_part = vz[par, span]
            scores = through(q4, k_part)
            if mask is not None:
                scores = scores + mask
            probs = jnp.exp(scores - lse)
            dprob = through(do4, v_part)
            dscore = (probs * (dprob - delta)).astype(BF16)
            dk_acc[par, span] += across(dscore, q4)
            dv_acc[par, span] += across(probs.astype(BF16), do4)
            return grad_q + matmul(dscore, k_part)

        def group_step(group, rb):
            rows = pl.ds(rb * block, block)
            q4 = stacked(q_ref, rows, group) * jnp.asarray(scale, BF16)
            do4 = stacked(do_ref, rows, group)
            prod = do4.astype(F32) * stacked(o_ref, rows, group).astype(F32)
            lse_all = lse_ref[rb]
            grad_q = jnp.zeros((PAIRS * block, LANES), F32)
            for par in range(2):
                lse = jnp.sum(
                    jnp.where(lanes_of(lse_all.shape) == 2 * group + par, lse_all, 0.0),
                    -1,
                    keepdims=True,
                )
                delta = jnp.sum(
                    jnp.where(lanes_of(prod.shape) // HD == par, prod, 0.0), -1, keepdims=True
                )
                for at in range(0, (rb + 1) * keys, step_keys):
                    mask = None
                    if at >= rb * keys:
                        mask = mask_ref[rb, :, pl.ds(at - rb * keys, step_keys)]
                        mask = jnp.concatenate([mask] * PAIRS, 0)
                    grad_q = piece(par, q4, do4, lse, delta, at, mask, grad_q)
            grad_q = grad_q * scale
            cosine, sine = turn_ref[0, rows], turn_ref[1, rows]
            for j in range(PAIRS):
                part = grad_q[j * block : (j + 1) * block]
                at = pl.multiple_of((group * PAIRS + j) * LANES, LANES)
                gqkv[rows, pl.ds(at, LANES)] = (part * cosine - turned(part) * sine).astype(BF16)

        def dkv_copy(owner, tile, step):
            return pltpu.make_async_remote_copy(
                src_ref=dkv.at[owner, tile],
                dst_ref=dkv_in.at[ctx, tile],
                send_sem=dkv_send.at[step, tile],
                recv_sem=dkv_recv.at[step, tile],
                device_id={"ctx": owner},
                device_id_type=MESH,
            )

        def attention(lo, hi):
            start = clock[0]

            def body(group, _):
                spread_heads(kv, 0, kz, group)
                spread_heads(kv, 1, vz, group)
                dk_acc[...] = jnp.zeros_like(dk_acc)
                dv_acc[...] = jnp.zeros_like(dv_acc)
                for rb in range(2):
                    group_step(group, rb)
                    line.tick(start + (group - lo) * 2 + rb)
                tile = group // 2
                for which, acc in enumerate((dk_acc, dv_acc)):
                    for part in range(ctx_n):
                        for rb in range(2):
                            span = pl.ds(rb * keys + part * block, block)
                            both = jnp.where(
                                lanes_of((block, LANES)) < HD, acc[0, span], acc[1, span]
                            )
                            both = both + roll_lanes(both, HD)
                            there = (part, tile, which, pl.ds(rb * block, block))
                            mine = lanes_of((block, LANES)) // HD == lax.rem(group, 2)
                            dkv[there] = jnp.where(mine, both.astype(BF16), dkv[there])
                return 0

            lax.fori_loop(lo, hi, body, 0)
            clock[0] = start + (hi - lo) * 2

        def send_dkv(tile):
            for step in range(1, ctx_n):
                dkv_copy(lax.rem(ctx + step, ctx_n), tile, step - 1).start()

        attention(0, 2)
        send_dkv(0)
        mlp_out.finish()
        h1_load.wait()

        def add_out(rows):
            h1_buf[rows] = h1_buf[rows] + mlp_out.value(rows)

        mlp_out.by_rows(add_out)
        settle()

        def output_partial(f, at):
            return across(dhb_ref[:, pl.ds(pl.multiple_of(f * shard, shard), shard)], o_ref[:, at])

        ysum = ring_sum(output_partial, shard, width, ysems)
        ysum.pair_all(lambda i: ticks(1) if i else None)
        attention(2, 3)
        ysum.launch()
        attention(3, 4)
        send_dkv(1)
        ticks(3)
        do_ref[...] = h1_buf[...].astype(BF16)
        result_copy = pltpu.make_async_copy(do_ref, result_out, isem.at[0])
        result_copy.start()
        ysum.finish()

        def keep_output(rows):
            az[rows, :width] = ysum.value(rows).astype(BF16)

        ysum.by_rows(keep_output)
        settle()
        x_load = pltpu.make_async_copy(x_in, q_ref, isem.at[1])
        x_load.start()

        def query_partial(f, at):
            return across(a1_ref[:, pl.ds(pl.multiple_of(f * shard, shard), shard)], gqkv[:, at])

        def pair_partial(f, at):
            return across(
                a1_ref[:, pl.ds(pl.multiple_of(f * shard, shard), shard)],
                gqkv[:, pl.ds(width, 2 * key_cols)],
            )

        xsum = ring_sum(query_partial, shard, width, xsems)
        xsum.pair_all(lambda i: ticks(1))
        for step in range(1, ctx_n):
            for tile in range(KV // 2):
                dkv_copy(lax.rem(ctx + step, ctx_n), tile, step - 1).wait_send()
                sender = lax.rem(ctx - step + ctx_n, ctx_n)
                pltpu.make_async_remote_copy(
                    src_ref=dkv.at[sender, tile],
                    dst_ref=dkv_in.at[sender, tile],
                    send_sem=dkv_send.at[step - 1, tile],
                    recv_sem=dkv_recv.at[step - 1, tile],
                    device_id={"ctx": sender},
                    device_id_type=MESH,
                ).wait_recv()
        cosine, sine = turn_ref[0], turn_ref[1]
        for tile in range(KV // 2):
            for which in range(2):
                part = dkv[ctx, tile, which].astype(F32)
                for step in range(1, ctx_n):
                    part = part + dkv_in[lax.rem(ctx + step, ctx_n), tile, which].astype(F32)
                if which == 0:
                    part = part * cosine - turned(part) * sine
                at = width + which * key_cols + tile * LANES
                gqkv[:, at : at + LANES] = part.astype(BF16)

        kvsum = ring_sum(pair_partial, shard, 2 * key_cols, kvsems, width)
        kvsum.pair_all()
        ticks(2)
        xsum.launch()
        kvsum.launch()
        ticks(2)

        def weight_copies(f):
            slot = f % 2
            return (
                pltpu.make_async_copy(wq_ref.at[f], wbuf.at[slot], wsem.at[slot]),
                pltpu.make_async_copy(wkv_ref.at[f], wkv.at[slot], wsem.at[2 + slot]),
            )

        for copy in weight_copies(0):
            copy.start()
        for f in range(fsdp_n):
            if f + 1 < fsdp_n:
                for copy in weight_copies(f + 1):
                    copy.start()
            for copy in weight_copies(f):
                copy.wait()
            h1_buf[:, f * shard : (f + 1) * shard] = through(
                gqkv[:, :width], wbuf[f % 2]
            ) + through(gqkv[:, width:], wkv[f % 2])
            if f % (fsdp_n // 4) == 0:
                ticks(1)
        ticks(1)
        x_load.wait()
        gain = gain1_ref[...]
        piece_rows = count // 4

        def norm_back(i, acc):
            rows = pl.ds(pl.multiple_of(i * piece_rows, piece_rows), piece_rows)
            x = q_ref[rows].astype(F32)
            grad = h1_buf[rows]
            factor = lax.rsqrt(jnp.mean(x * x, -1, keepdims=True) + EPSILON)
            unit = x * factor
            o_ref[rows] = (dh1[rows] + normed_back(unit, factor, grad, gain)).astype(BF16)
            return acc + jnp.sum(grad * unit, 0, keepdims=True)

        gslot[fsdp, 0:1] = lax.fori_loop(0, 4, norm_back, jnp.zeros((1, width), F32))
        gtok_copy = pltpu.make_async_copy(o_ref, gtok_out, isem.at[2])
        gtok_copy.start()

        def gain_copy(slots, axis, here, step, sems):
            n = fsdp_n if axis == "fsdp" else ctx_n
            return pltpu.make_async_remote_copy(
                src_ref=slots.at[here],
                dst_ref=slots.at[here],
                send_sem=sems[0].at[step - 1],
                recv_sem=sems[1].at[step - 1],
                device_id={axis: lax.rem((fsdp if axis == "fsdp" else ctx) + step, n)},
                device_id_type=MESH,
            )

        def exchange(slots, axis, n, me, sems):
            for step in range(1, n):
                gain_copy(slots, axis, me, step, sems).start()
            for step in range(1, n):
                gain_copy(slots, axis, me, step, sems).wait_send()
                gain_copy(slots, axis, lax.rem(me - step + n, n), step, sems).wait_recv()
            total = slots[0]
            for i in range(1, n):
                total = total + slots[i]
            return total

        ticks(1)
        cslot[ctx] = exchange(gslot, "fsdp", fsdp_n, fsdp, (gain_send, gain_recv))
        ticks(2)
        gains_ref[...] = exchange(cslot, "ctx", ctx_n, ctx, (cgain_send, cgain_recv))

        ticks(2)
        xsum.finish()
        kvsum.finish()

        def keep_query(rows):
            az[rows, width : 2 * width] = xsum.value(rows).astype(BF16)
            az[rows, 2 * width :] = kvsum.value(rows).astype(BF16)

        xsum.by_rows(keep_query)
        result_copy.wait()
        gtok_copy.wait()

    pl.run_scoped(
        attention_back,
        rows_type,
        rows_type,
        rows_type,
        rows_type,
        rows_type,
        pltpu.VMEM(lse_in.shape, F32),
        pltpu.VMEM(mask_in.shape, F32),
        pltpu.VMEM(turn_in.shape, F32),
        pltpu.VMEM((count, width), F32),
        pltpu.VMEM((2,) + wout_ref.shape[1:], BF16),
        pltpu.VMEM((2,) + wq_ref.shape[1:], BF16),
        pltpu.VMEM((2,) + wkv_ref.shape[1:], BF16),
        pltpu.VMEM((2, 2 * keys, LANES), BF16),
        pltpu.VMEM((2, 2 * keys, LANES), BF16),
        pltpu.VMEM((2, 2 * keys, LANES), F32),
        pltpu.VMEM((2, 2 * keys, LANES), F32),
        pltpu.VMEM((count, cols), BF16),
        pltpu.VMEM(dkv_in.shape, BF16),
    )
    ticks(line.ticks - clock[0])


def layer(x, cot, wq, wkv, w_out, w_gate, w_up, w_down, mask, turn, gain_one, gain_two):
    ctx_n = lax.axis_size("ctx")
    fsdp_n = lax.axis_size("fsdp")
    count, width = x.shape
    local = w_gate.shape[0]
    shard = wq.shape[0]
    cols = wq.shape[1] + wkv.shape[1]
    chips = fsdp_n // 2
    far = chips // 2
    vmem = pl.BlockSpec(memory_space=pltpu.VMEM)
    hbm = pl.BlockSpec(memory_space=pl.ANY)
    dma = pltpu.SemaphoreType.DMA
    regular = pltpu.SemaphoreType.REGULAR
    zbuf = pltpu.VMEM((SLOTS, local, LANES), BF16)
    scratch = (
        [zbuf] * 5
        + [
            pltpu.VMEM((shard, cols + width), BF16),
            pltpu.VMEM((2 + chips + 2 * far, max(count, shard), cols), BF16),
            pltpu.VMEM((count, width), F32),
            pltpu.VMEM((ctx_n, KV // 2, 2, count, LANES), BF16),
            pltpu.VMEM((ctx_n, 2, count, KV * HD), BF16),
            pltpu.VMEM((fsdp_n, 2, width), F32),
            pltpu.VMEM((ctx_n, 2, width), F32),
        ]
        + [dma((SLOTS,))] * 5
        + [dma((SLOTS, 2)), regular, regular]
        + gather_sems(chips) * 5
        + sum_sems(chips) * 5
        + [
            dma((ctx_n - 1, KV // 2)),
            dma((ctx_n - 1, KV // 2)),
            dma((ctx_n - 1,)),
            dma((ctx_n - 1,)),
            dma((fsdp_n - 1,)),
            dma((fsdp_n - 1,)),
            dma((ctx_n - 1,)),
            dma((ctx_n - 1,)),
            dma((4,)),
            dma((9,)),
            dma((2,)),
            regular((4,)),
        ]
    )

    def bf16(*shape):
        return jax.ShapeDtypeStruct(shape, BF16)

    return pl.pallas_call(
        functools.partial(layer_kernel, (ctx_n, fsdp_n)),
        out_shape=(
            bf16(count, width),
            bf16(count, width),
            jax.ShapeDtypeStruct((2, width), F32),
            bf16(local, width),
            bf16(local, width),
            bf16(local, width),
            bf16(shard, cols),
            bf16(shard, width),
            bf16(fsdp_n, count, width),
            bf16(3 * width // LANES, local, LANES),
            bf16(fsdp_n, *wq.shape),
            bf16(fsdp_n, *wkv.shape),
            bf16(fsdp_n, *w_out.shape),
            bf16(fsdp_n, count, width),
            bf16(count, width),
            bf16(count, width),
            bf16(count, width),
            jax.ShapeDtypeStruct((count, width), F32),
            jax.ShapeDtypeStruct((2, PAIRS * count // 2, LANES), F32),
        ),
        in_specs=[hbm] * 10 + [vmem] * 2,
        out_specs=(hbm, hbm, vmem) + (hbm,) * 16,
        scratch_shapes=scratch,
        compiler_params=pltpu.CompilerParams(
            collective_id=1, has_side_effects=True, vmem_limit_bytes=VMEM_LIMIT
        ),
        name="layer",
    )(x, cot, wq, wkv, w_out, w_gate, w_up, w_down, mask, turn, gain_one, gain_two)[:8]


def shards(
    tokens,
    cotangent,
    block_table,
    gain_attn,
    w_query,
    w_key,
    w_value,
    w_output,
    gain_mlp,
    w_gate,
    w_up,
    w_down,
):
    ctx_n = lax.axis_size("ctx")
    ctx = lax.axis_index("ctx")
    count, width = tokens.shape[1:]
    block = count // 2

    table = block_table.reshape(ctx_n, 2)
    lower, upper = jnp.min(table, 1), jnp.max(table, 1)
    owned = table[ctx]
    swap = owned[0] > owned[1]

    def ordered(rows):
        return jnp.where(swap, jnp.concatenate([rows[block:], rows[:block]], 0), rows)

    offsets = jnp.arange(block, dtype=jnp.int32)
    spots = jnp.stack([lower, upper])[:, :, None] * block + offsets
    own_spots = spots[:, ctx]
    key_spots = spots.reshape(2, -1)
    mask = jnp.where(own_spots[:, :, None] >= key_spots[:, None, :], 0.0, NEGATIVE).astype(F32)
    freqs = 10000.0 ** (-jnp.arange(HD // 2, dtype=F32) / (HD // 2))
    angle = own_spots.reshape(-1).astype(F32)[:, None] * freqs[None, :]
    angle = jnp.concatenate([angle] * (LANES * 2 // HD), -1)
    turn = jnp.stack([jnp.cos(angle), jnp.sin(angle)])

    rows_in = ordered(tokens[0])
    grad_out = ordered(cotangent[0])

    result, grad_tokens, gains, gate_sum, up_sum, down_sum, query_sum, output_sum = layer(
        rows_in,
        grad_out,
        w_query,
        jnp.concatenate([w_key, w_value], 1),
        w_output,
        w_gate.T,
        w_up.T,
        w_down,
        mask,
        turn,
        gain_attn[None],
        gain_mlp[None],
    )
    key_cols = KV * HD
    query_sum = query_sum.astype(F32)
    return (
        ordered(result)[None],
        ordered(grad_tokens)[None],
        query_sum[:, :width],
        query_sum[:, width : width + key_cols],
        query_sum[:, width + key_cols :],
        output_sum.T.astype(F32),
        gate_sum.astype(F32).T,
        up_sum.astype(F32).T,
        down_sum.astype(F32),
        gains[0],
        gains[1],
    )


def solution(mesh):
    in_specs = (
        P("fsdp", "ctx", None),
        P("fsdp", "ctx", None),
        P(),
        P(),
        P("fsdp", None),
        P("fsdp", None),
        P("fsdp", None),
        P(None, "fsdp"),
        P(),
        P(None, "fsdp"),
        P(None, "fsdp"),
        P("fsdp", None),
    )
    out_specs = (
        P("fsdp", "ctx", None),
        P("fsdp", "ctx", None),
        P("fsdp", None),
        P("fsdp", None),
        P("fsdp", None),
        P(None, "fsdp"),
        P(None, "fsdp"),
        P(None, "fsdp"),
        P("fsdp", None),
        P(),
        P(),
    )
    return jax.shard_map(shards, mesh=mesh, in_specs=in_specs, out_specs=out_specs, check_vma=False)
```

```python
import functools

import jax
import jax.numpy as jnp
from jax import lax
from jax.experimental import pallas as pl
from jax.experimental.pallas import tpu as pltpu
from jax.sharding import PartitionSpec as P

H = 32
KV = 4
HD = 64
GROUP = H // KV
PAIRS = GROUP // 2
LANES = 128

EPSILON = 1e-05
NEGATIVE = -1e30
SLOTS = 8
GAP = 3
VMEM_LIMIT = 61 * 1024 * 1024
MESH = pl.DeviceIdType.MESH
F32 = jnp.float32
BF16 = jnp.bfloat16


def dot(left, right, left_dim, right_dim):
    return lax.dot_general(
        left, right, (((left_dim,), (right_dim,)), ((), ())), preferred_element_type=F32
    )


def matmul(left, right):
    return dot(left, right, 1, 0)


def across(left, right):
    return dot(left, right, 0, 0)


def through(left, right):
    return dot(left, right, 1, 1)


def normed(hidden, gain):
    factor = lax.rsqrt(jnp.mean(hidden * hidden, -1, keepdims=True) + EPSILON)
    unit = hidden * factor
    return (unit, factor, (unit * gain).astype(BF16))


def normed_back(unit, factor, grad_in, gain):
    scaled = grad_in * gain
    return factor * (scaled - unit * jnp.mean(scaled * unit, -1, keepdims=True))


def gate_back(grad_hidden, gate, up):
    sigma = jax.nn.sigmoid(gate)
    activated = gate * sigma
    grad_gate_in = (grad_hidden * up * sigma * (1.0 + gate * (1.0 - sigma))).astype(BF16)
    grad_up_in = (grad_hidden * activated).astype(BF16)
    return ((activated * up).astype(BF16), grad_gate_in, grad_up_in)


def lanes_of(shape):
    return lax.broadcasted_iota(jnp.int32, shape, len(shape) - 1)


def roll_lanes(value, amount):
    return pltpu.roll(value, amount, 1)


def turned(value):
    first = lax.rem(lanes_of(value.shape), HD) < HD // 2
    return jnp.where(first, -roll_lanes(value, LANES - HD // 2), roll_lanes(value, HD // 2))


def stacked(ref, rows, group):
    wide = PAIRS * LANES
    block = ref[rows, pl.ds(pl.multiple_of(group * wide, wide), wide)]
    return jnp.concatenate([block[:, j * LANES : (j + 1) * LANES] for j in range(PAIRS)], 0)


def spread_heads(kv_ref, which, out_ref, group):
    devices, _, count, _ = kv_ref.shape
    block = count // 2
    at = pl.multiple_of((group // 2) * LANES, LANES)
    here = lax.rem(group, 2)
    for part in range(devices):
        tile = kv_ref[part, which, :, pl.ds(at, LANES)].astype(F32)
        other = roll_lanes(tile, HD)
        half = lanes_of(tile.shape) // HD
        for par in range(2):
            picked = jnp.where(here == par, tile, other)
            picked = jnp.where(half == par, picked, 0.0).astype(BF16)
            for rb in range(2):
                rows = pl.ds((rb * devices + part) * block, block)
                out_ref[par, rows] = picked[rb * block : (rb + 1) * block]


def attend_group(group, q_ref, kz, vz, mask_ref, o_ref, lse_ref):
    block = q_ref.shape[0] // 2
    keys = kz.shape[1] // 2
    together = PAIRS if keys <= 4 * LANES else PAIRS // 2
    for rb in range(2):
        rows = pl.ds(rb * block, block)
        every = stacked(q_ref, rows, group) * jnp.asarray(HD ** (-0.5), BF16)
        mask = jnp.concatenate([mask_ref[rb]] * together, 0)
        for first in range(0, PAIRS, together):
            some = slice(first * block, (first + together) * block)
            q4 = every[some]
            total = 0.0
            lse = lse_ref[rb, some]
            for par in range(2):
                scores = []
                for part in range(rb + 1):
                    score = through(q4, kz[par, pl.ds(part * keys, keys)])
                    scores.append(score + mask if part == rb else score)
                peak = functools.reduce(
                    jnp.maximum, [jnp.max(s, -1, keepdims=True) for s in scores]
                )
                probs = [jnp.exp(s - peak) for s in scores]
                norm = sum(jnp.sum(p, -1, keepdims=True) for p in probs)
                mixed = sum(
                    matmul(p.astype(BF16), vz[par, pl.ds(i * keys, keys)])
                    for i, p in enumerate(probs)
                )
                total = total + mixed / norm
                here = lanes_of(lse.shape) == 2 * group + par
                lse = jnp.where(here, peak + jnp.log(norm), lse)
            lse_ref[rb, some] = lse
            for j in range(together):
                at = pl.multiple_of((group * PAIRS + first + j) * LANES, LANES)
                o_ref[rows, pl.ds(at, LANES)] = total[j * block : (j + 1) * block].astype(BF16)


class LineSum:
    def __init__(self, count, index, first, second, sources, targets, bufs, sems):
        self.n = count
        self.first, self.second = first, second
        self.total = first + second
        self.mlp_src, self.att_src = sources
        self.gate_dst, self.up_dst, self.down_dst, self.query_dst, self.output_dst = targets
        self.own, self.rout, self.sums, self.rin, self.done = bufs
        (
            self.load_sem,
            self.in_send,
            self.rout_sem,
            self.rin_sem,
            self.out_send,
            self.store_sem,
            self.credit_in,
            self.credit_out,
        ) = sems
        half = count // 2
        left = index < half
        self.depth = jnp.where(left, index, count - 1 - index)
        step = jnp.where(left, 1, -1)
        self.inward = index + step
        outward = index - step
        self.has_out = self.depth > 0
        self.outward = jnp.where(self.has_out, outward, index + step)
        self.is_mid = self.depth == half - 1
        deepest = half - 1
        self.lag_sum = 1 + GAP * self.depth
        self.lag_sent = self.lag_sum + GAP
        self.lag_total = 1 + GAP * deepest + GAP + GAP * (deepest - self.depth)
        self.lag_end = self.lag_total + GAP
        self.ticks = self.total + 1 + 3 * GAP * deepest + 3 * GAP
        self.att_rows = 2 * self.att_src.shape[0]
        self.blocks = self.down_dst.shape[1] // LANES

    def view(self, buf, slot, att):
        return buf.at[slot, pl.ds(0, self.att_rows)] if att else buf.at[slot]

    def each(self, chunk, body):
        slot = lax.rem(jnp.maximum(chunk, 0), SLOTS)
        pl.when((chunk >= 0) & (chunk < self.first))(lambda: body(chunk, slot, False))
        if self.second:
            pl.when((chunk >= self.first) & (chunk < self.total))(lambda: body(chunk, slot, True))

    def send(self, src, dst, sems, target, slot, att):
        return pltpu.make_async_remote_copy(
            src_ref=self.view(src, slot, att),
            dst_ref=self.view(dst, slot, att),
            send_sem=sems[0].at[slot],
            recv_sem=sems[1].at[slot],
            device_id={"ctx": target},
            device_id_type=MESH,
        )

    def to_total(self, slot, att):
        return self.send(self.sums, self.rin, (self.in_send, self.rin_sem), self.inward, slot, att)

    def to_partial(self, slot, att):
        return self.send(
            self.sums, self.rout, (self.in_send, self.rout_sem), self.inward, slot, att
        )

    def to_outward(self, slot, att):
        return self.send(
            self.done, self.rin, (self.out_send, self.rin_sem), self.outward, slot, att
        )

    def load(self, chunk, slot):
        return pltpu.make_async_copy(
            self.mlp_src.at[chunk], self.own.at[slot], self.load_sem.at[slot]
        )

    def stores(self, chunk, slot, att):
        if att:
            rows = self.att_rows // 2
            wide = self.output_dst.shape[1] // LANES
            pairs = []
            for i in range(2):
                at = 2 * (chunk - self.first) + i
                src = self.done.at[slot, pl.ds(i * rows, rows)]
                sem = self.store_sem.at[slot, i]
                o_at = pl.multiple_of(jnp.minimum(at, wide - 1) * LANES, LANES)
                q_at = pl.multiple_of(jnp.maximum(at - wide, 0) * LANES, LANES)
                pairs.append(
                    (
                        at < wide,
                        pltpu.make_async_copy(src, self.output_dst.at[:, pl.ds(o_at, LANES)], sem),
                    )
                )
                pairs.append(
                    (
                        at >= wide,
                        pltpu.make_async_copy(src, self.query_dst.at[:, pl.ds(q_at, LANES)], sem),
                    )
                )
            return pairs
        kind = chunk // self.blocks
        at = pl.multiple_of(lax.rem(chunk, self.blocks) * LANES, LANES)
        sem = self.store_sem.at[slot, 0]
        return [
            (kind == i, pltpu.make_async_copy(self.done.at[slot], dst.at[:, pl.ds(at, LANES)], sem))
            for i, dst in enumerate((self.gate_dst, self.up_dst, self.down_dst))
        ]

    def tick(self, i):
        self.each(i - self.lag_sum + 1, self.stage_load)
        self.each(i - self.lag_sum, self.stage_sum)
        self.each(i - self.lag_sent, self.stage_sent)
        self.each(i - self.lag_total, self.stage_total)
        self.each(i - self.lag_end, self.stage_end)

    def stage_load(self, chunk, slot, att):
        if not att:
            self.load(chunk, slot).start()

    def stage_sum(self, chunk, slot, att):
        if not att:
            self.load(chunk, slot).wait()

        def own():
            if not att:
                return self.own[slot]
            at = (chunk - self.first) * 2 * LANES
            return jnp.concatenate(
                [
                    self.att_src[:, pl.ds(pl.multiple_of(at + i * LANES, LANES), LANES)]
                    for i in range(2)
                ],
                0,
            )

        @pl.when(self.has_out)
        def _():
            self.to_partial(slot, att).wait_recv()
            arrived = self.view(self.rout, slot, att)[...].astype(F32)
            self.view(self.sums, slot, att)[...] = (own().astype(F32) + arrived).astype(BF16)

            @pl.when(chunk < self.total - SLOTS)
            def _():
                pl.semaphore_signal(
                    self.credit_in, 1, device_id={"ctx": self.outward}, device_id_type=MESH
                )

        @pl.when(jnp.logical_not(self.has_out))
        def _():
            self.view(self.sums, slot, att)[...] = own()

        @pl.when(chunk >= SLOTS)
        def _():
            pl.semaphore_wait(self.credit_in, 1)

        pl.when(self.is_mid)(lambda: self.to_total(slot, att).start())
        pl.when(jnp.logical_not(self.is_mid))(lambda: self.to_partial(slot, att).start())

    def stage_sent(self, chunk, slot, att):
        self.to_total(slot, att).wait_send()

    def stage_total(self, chunk, slot, att):
        self.to_total(slot, att).wait_recv()
        arrived = self.view(self.rin, slot, att)
        done = self.view(self.done, slot, att)

        @pl.when(self.is_mid)
        def _():
            mine = self.view(self.sums, slot, att)[...].astype(F32)
            done[...] = (mine + arrived[...].astype(F32)).astype(BF16)

            @pl.when(chunk < self.total - SLOTS)
            def _():
                pl.semaphore_signal(
                    self.credit_in, 1, device_id={"ctx": self.inward}, device_id_type=MESH
                )

        @pl.when(jnp.logical_not(self.is_mid))
        def _():
            done[...] = arrived[...]

            @pl.when(chunk < self.total - SLOTS)
            def _():
                pl.semaphore_signal(
                    self.credit_out, 1, device_id={"ctx": self.inward}, device_id_type=MESH
                )

        @pl.when(self.has_out)
        def _():
            @pl.when(chunk >= SLOTS)
            def _():
                pl.semaphore_wait(self.credit_out, 1)

            self.to_outward(slot, att).start()

        for condition, copy in self.stores(chunk, slot, att):
            pl.when(condition)(copy.start)

    def stage_end(self, chunk, slot, att):
        pl.when(self.has_out)(lambda: self.to_outward(slot, att).wait_send())
        for condition, copy in self.stores(chunk, slot, att):
            pl.when(condition)(copy.wait)


def chip_at(place):
    return 2 * (place // 2) + lax.rem(place + place // 2, 2)


class Ring:
    def __init__(self, count, index):
        self.chips = count // 2
        chip = index // 2
        self.core = lax.rem(index, 2)
        self.place = chip_at(chip)
        self.partner = 2 * chip + 1 - self.core
        self.right = self.device(1)
        self.left = self.device(-1)

    def device(self, offset, core=None):
        place = lax.rem(self.place + offset + self.chips, self.chips)
        return 2 * chip_at(place) + (self.core if core is None else core)


class RingGather:
    def __init__(self, ring, source, slots, sems, mate=None, odd=None):
        self.ring, self.source, self.slots = ring, source, slots
        self.sems, self.mate = sems, mate
        self.far = ring.chips // 2
        rows = slots.shape[1]
        self.share = rows // 4 if mate is not None else 0
        self.rows = rows - self.share
        if mate is None:
            self.start, self.give, self.take = 0, 0, 0
        else:
            self.start = pl.multiple_of(odd * self.share, 16)
            self.give = pl.multiple_of(odd * self.rows, 16)
            self.take = pl.multiple_of((1 - odd) * self.rows, 16)

    def span(self, half=None):
        if half is None:
            return pl.ds(self.start, self.rows)
        size = self.rows // 2
        return pl.ds(self.start + half * size, size)

    def move(self, src, dst, kind, index, target):
        return pltpu.make_async_remote_copy(
            src_ref=src,
            dst_ref=dst,
            send_sem=self.sems[2 * kind].at[index],
            recv_sem=self.sems[2 * kind + 1].at[index],
            device_id=target,
            device_id_type=MESH,
        )

    def copy(self, offset, target, kind, index, rows):
        block = self.ring.device(offset)
        src = self.source if offset == 0 else self.slots.at[block]
        return self.move(
            src.at[rows], self.slots.at[block, rows], kind, index, {"fsdp": target}
        )

    def rightward(self, s, half):
        return self.copy(-s, self.ring.right, 0, (s, half), self.span(half))

    def leftward(self, s, half):
        return self.copy(s, self.ring.left, 1, (s, half), self.span(half))

    def firsts(self, s):
        return [self.rightward(s, 0), self.leftward(s, 1)]

    def seconds(self, s):
        return [self.rightward(s, 1), self.leftward(s, 0)] if s + 1 < self.far else []

    def coming(self, s, half_left, half_right):
        return [
            self.copy(-s, self.ring.right, 0, (s - 1, half_left), self.span(half_left)),
            self.copy(s, self.ring.left, 1, (s - 1, half_right), self.span(half_right)),
        ]

    def index(self, offset):
        return 0 if offset == 0 else 2 * abs(offset) - (1 if offset < 0 else 0)

    def across(self, offset):
        rows = pl.ds(0, self.rows + self.share) if offset == 0 else self.span()
        return self.copy(offset, self.ring.partner, 2, self.index(offset), rows)

    def across_share(self, offset):
        rows = pl.ds(self.take, self.share)
        return self.copy(offset, self.ring.partner, 3, self.index(offset), rows)

    def to_mate(self, offset, core=None):
        block = self.ring.device(offset)
        rows = pl.ds(self.give, self.share)
        place = self.slots.at[block, rows]
        return self.move(place, place, 4, self.index(offset), {"ctx": self.mate})

    def offsets(self, s):
        return [s] if s == self.far else [-s, s]

    def begin(self):
        for message in self.firsts(0) + self.seconds(0):
            message.start()
        self.across(0).start()

    def advance(self, s):
        for message in self.coming(s, 0, 1):
            message.wait_recv()
        if s < self.far:
            for message in self.firsts(s):
                message.start()

    def settle(self, s):
        if s < self.far:
            for message in self.coming(s, 1, 0):
                message.wait_recv()
            for message in self.seconds(s):
                message.start()
        for offset in self.offsets(s):
            self.across(offset).start()
            if self.share:
                self.to_mate(offset).start()

    def complete(self, s):
        if self.share:
            for offset in self.offsets(s):
                block = self.ring.device(offset)
                place = self.slots.at[block, pl.ds(self.take, self.share)]
                self.move(
                    place, place, 4, self.index(offset), {"ctx": self.mate}
                ).wait_recv()
                self.across_share(offset).start()

    def from_partner(self, offset):
        block = self.ring.device(offset, 1 - self.ring.core)
        rows = pl.ds(0, self.rows + self.share) if offset == 0 else self.span()
        index = self.index(offset)
        target = {"fsdp": self.ring.partner}
        place = self.slots.at[block, rows]
        self.move(place, place, 2, index, target).wait_recv()
        if self.share and offset != 0:
            place = self.slots.at[block, pl.ds(self.take, self.share)]
            self.move(place, place, 3, index, target).wait_recv()

    def blocks(self, s):
        offsets = [0] if s == 0 else self.offsets(s)
        return [self.ring.device(o) for o in offsets] + [
            self.ring.device(o, 1 - self.ring.core) for o in offsets
        ]

    def all_from_partner(self, s):
        for offset in [0] if s == 0 else self.offsets(s):
            self.from_partner(offset)

    def end(self):
        for s in range(self.far):
            for message in self.firsts(s) + self.seconds(s):
                message.wait_send()
        self.across(0).wait_send()
        for s in range(1, self.far + 1):
            for offset in self.offsets(s):
                self.across(offset).wait_send()
                if self.share:
                    self.across_share(offset).wait_send()
                    self.to_mate(offset).wait_send()


def gather_sems(chips):
    far = chips // 2
    dma = pltpu.SemaphoreType.DMA
    return [dma((far, 2))] * 4 + [dma((2 * far + 1,))] * 6


def pick(index, choices):
    out = choices[0]
    for i, choice in enumerate(choices[1:]):
        out = jnp.where(index == i + 1, choice, out)
    return out


class RingSum:
    def __init__(self, ring, partial, arena, rows, cols, sems, first=0):
        self.ring, self.partial, self.first = ring, partial, first
        self.arena, self.rows, self.cols = arena, rows, cols
        (
            self.stage_send,
            self.pair_recv,
            self.right_send,
            self.right_recv,
            self.left_send,
            self.left_recv,
        ) = sems
        far = ring.chips // 2
        self.far = far
        offsets = [far]
        for s in range(far - 1, 0, -1):
            offsets += [s, -s]
        self.offsets = offsets + [0]
        self.at = {offset: i for i, offset in enumerate(self.offsets)}

    def view(self, slot, rows=None):
        rows = pl.ds(0, self.rows) if rows is None else rows
        return self.arena.at[slot, rows, pl.ds(self.first, self.cols)]

    def stage(self, i):
        return self.view(i % 2)

    def pair(self, i, rows=None):
        return self.view(2 + i, rows)

    def side(self, right, s, rows=None):
        return self.view(2 + self.ring.chips + (0 if right else self.far) + s - 1, rows)

    def half(self, which):
        return pl.ds(which * (self.rows // 2), self.rows // 2)

    def pair_copy(self, i):
        return pltpu.make_async_remote_copy(
            src_ref=self.stage(i),
            dst_ref=self.pair(i),
            send_sem=self.stage_send.at[i],
            recv_sem=self.pair_recv.at[i],
            device_id={"fsdp": self.ring.partner},
            device_id_type=MESH,
        )

    def by_columns(self, piece):
        wide = 4 * LANES

        def body(j, _):
            at = pl.multiple_of(j * wide, wide)
            piece(pl.ds(at, wide), pl.ds(pl.multiple_of(self.first + at, wide), wide))
            return 0

        lax.fori_loop(0, self.cols // wide, body, 0)

    def pair_step(self, i):
        offset = self.offsets[i]
        if i >= 2:
            self.pair_copy(i - 2).wait_send()
        owner = self.ring.device(offset, 1 - self.ring.core)
        rows = pl.ds(0, self.rows)

        def piece(at, place):
            self.arena[i % 2, rows, place] = self.partial(owner, at).astype(BF16)

        self.by_columns(piece)
        self.pair_copy(i).start()

    def pair_add(self, i):
        owner = self.ring.device(self.offsets[i])
        self.pair_copy(i).wait_recv()
        rows = pl.ds(0, self.rows)

        def piece(at, place):
            mine = self.partial(owner, at)
            there = (2 + i, rows, place)
            self.arena[there] = (mine + self.arena[there].astype(F32)).astype(BF16)

        self.by_columns(piece)

    def pair_all(self, between=None):
        last = len(self.offsets)
        for i in range(last):
            self.pair_step(i)
            if i >= 1:
                self.pair_add(i - 1)
                self.launch_free(i - 1)
            if between is not None:
                between(i)
        self.pair_add(last - 1)
        for i in range(max(last - 2, 0), last):
            self.pair_copy(i).wait_send()

    def hop(self, s, right, which):
        owner = self.at[s if right or s == self.far else -s]
        rows = self.half(which)
        return pltpu.make_async_remote_copy(
            src_ref=self.pair(owner, rows),
            dst_ref=self.side(right, s, rows),
            send_sem=(self.right_send if right else self.left_send).at[s - 1, which],
            recv_sem=(self.right_recv if right else self.left_recv).at[s - 1, which],
            device_id={"fsdp": self.ring.right if right else self.ring.left},
            device_id_type=MESH,
        )

    def hops(self):
        far = self.far
        moves = [(far, True, 0), (far, False, 1)]
        if far > 1:
            moves += [(far - 1, True, 1), (far - 1, False, 0)]
            moves += [(far - 1, True, 0), (far - 1, False, 1)]
        for s in range(far - 2, 0, -1):
            for which in range(2):
                moves += [(s, True, which), (s, False, which)]
        return moves

    def free(self, s, right, which):
        return s == self.far or (s == self.far - 1 and which == (1 if right else 0))

    def launch_free(self, i):
        offset = self.offsets[i]
        for s, right, which in self.hops():
            owner = s if right or s == self.far else -s
            if self.free(s, right, which) and owner == offset:
                self.hop(s, right, which).start()

    def launch(self):
        for s, right, which in self.hops():
            if not self.free(s, right, which):
                self.hop(s + 1, right, which).wait_recv()
                owner = self.at[s if right else -s]
                rows = self.half(which)
                arrived = self.side(right, s + 1, rows)
                mine = self.pair(owner, rows)
                mine[...] = (mine[...].astype(F32) + arrived[...].astype(F32)).astype(BF16)
                self.hop(s, right, which).start()

    def finish(self):
        for s, right, which in self.hops():
            if s == 1:
                self.hop(s, right, which).wait_recv()
            self.hop(s, right, which).wait_send()

    def by_rows(self, piece):
        step = self.rows // 4

        def body(i, _):
            piece(pl.ds(pl.multiple_of(i * step, step), step))
            return 0

        lax.fori_loop(0, 4, body, 0)

    def value(self, rows):
        own = self.pair(self.at[0], rows)[...].astype(F32)
        left = self.side(True, 1, rows)[...].astype(F32)
        return own + left + self.side(False, 1, rows)[...].astype(F32)


def sum_sems(chips):
    far = chips // 2
    dma = pltpu.SemaphoreType.DMA
    return [dma((chips,))] * 2 + [dma((far, 2))] * 4


def layer_kernel(
    sizes,
    x_in,
    cot_in,
    wq_in,
    wkv_in,
    wout_in,
    wgate_ref,
    wup_ref,
    wdown_ref,
    mask_in,
    turn_in,
    gain1_ref,
    gain2_ref,
    result_out,
    gtok_out,
    gains_ref,
    gate_out,
    up_out,
    down_out,
    query_out,
    output_out,
    rows_all,
    gz_ref,
    wq_ref,
    wkv_ref,
    wout_ref,
    cot_ref,
    q_in,
    o_in,
    a1_in,
    h1_ref,
    lse_in,
    *scratch,
):
    ctx_n, fsdp_n = sizes
    (
        zown,
        zrout,
        zsums,
        zrin,
        zdone,
        az,
        arena,
        dh1,
        dkv_in,
        kv,
        gslot,
        cslot,
    ) = scratch[:12]
    scratch = scratch[12:]
    zsems, scratch = scratch[:8], scratch[8:]
    gathers, scratch = [scratch[10 * i : 10 * i + 10] for i in range(5)], scratch[50:]
    da2_sems, scratch = scratch[:6], scratch[6:]
    out_sems, scratch = scratch[:6], scratch[6:]
    ysems, scratch = scratch[:6], scratch[6:]
    xsems, scratch = scratch[:6], scratch[6:]
    kvsems, scratch = scratch[:6], scratch[6:]
    (
        dkv_send,
        dkv_recv,
        kv_send,
        kv_recv,
        gain_send,
        gain_recv,
        cgain_send,
        cgain_recv,
        wsem,
        isem,
        ssem,
        ready,
    ) = scratch
    ctx = lax.axis_index("ctx")
    fsdp = lax.axis_index("fsdp")
    ring = Ring(fsdp_n, fsdp)
    count, width = x_in.shape
    block = count // 2
    keys = ctx_n * block
    scale = HD ** (-0.5)
    shard = query_out.shape[0]
    cols = query_out.shape[1]
    local = wgate_ref.shape[0]
    key_cols = KV * HD

    barrier = pltpu.get_barrier_semaphore()
    for axis, me, n in (("ctx", ctx, ctx_n), ("fsdp", fsdp, fsdp_n)):
        for step in range(1, n):
            pl.semaphore_signal(
                barrier, 1, device_id={axis: lax.rem(me + step, n)}, device_id_type=MESH
            )
    pl.semaphore_wait(barrier, ctx_n + fsdp_n - 2)

    rounds = [0]

    def settle():
        sem = ready.at[rounds[0]]
        rounds[0] += 1
        for target in (ring.partner, ring.left, ring.right):
            pl.semaphore_signal(sem, 1, device_id={"fsdp": target}, device_id_type=MESH)
        pl.semaphore_wait(sem, 3)

    line = LineSum(
        ctx_n,
        ctx,
        gz_ref.shape[0],
        az.shape[1] // (2 * LANES),
        (gz_ref, az),
        (gate_out, up_out, down_out, query_out, output_out),
        (zown, zrout, zsums, zrin, zdone),
        zsems,
    )
    clock = [0]
    cap = [0]

    def ticks(number):
        start = clock[0]
        number = max(min(number, cap[0] - start), 0)
        clock[0] = start + number

        def body(i, _):
            line.tick(i)
            return 0

        lax.fori_loop(start, start + number, body, 0)

    odd = lax.rem(ctx, 2)
    mate = ctx + 1 - 2 * odd
    help_along = ()
    wkv_gather = RingGather(ring, wkv_in, wkv_ref, gathers[0], *help_along)
    wq_gather = RingGather(ring, wq_in, wq_ref, gathers[1], *help_along)
    wout_gather = RingGather(ring, wout_in, wout_ref, gathers[2], mate, odd)
    cot_gather = RingGather(ring, cot_in, cot_ref, gathers[3])
    gather = RingGather(ring, rows_all.at[fsdp], rows_all, gathers[4])
    far = gather.far

    def forward(x_ref, a1_ref, wkv, acc, wbuf, q_ref, o_ref, kz, vz, mask_ref, turn_ref, lse_ref, obuf):
        wkv_gather.begin()
        loads = [
            pltpu.make_async_copy(src, dst, isem.at[i])
            for i, (src, dst) in enumerate(
                [
                    (x_in, x_ref),
                    (mask_in, mask_ref),
                    (turn_in, turn_ref),
                    (wkv_in, wkv.at[fsdp]),
                    (wq_in, wbuf.at[0]),
                    (wout_in, obuf.at[0]),
                    (cot_in, o_ref),
                ]
            )
        ]
        owns = [
            pltpu.make_async_copy(src, dst, isem.at[3 + i])
            for i, (src, dst) in enumerate(
                [
                    (wkv.at[fsdp], wkv_ref.at[fsdp]),
                    (wbuf.at[0], wq_ref.at[fsdp]),
                    (obuf.at[0], wout_ref.at[fsdp]),
                    (o_ref, cot_ref.at[fsdp]),
                ]
            )
        ]
        for load in loads:
            load.start()
        wkv_gather.advance(1)
        wq_gather.begin()
        loads[0].wait()
        gain = gain1_ref[...]
        step_rows = count // 4

        def norm_one(i, _):
            rows = pl.ds(pl.multiple_of(i * step_rows, step_rows), step_rows)
            a1_ref[rows] = normed(x_ref[rows].astype(F32), gain)[2]
            return 0

        lax.fori_loop(0, 4, norm_one, 0)
        a1_store = pltpu.make_async_copy(a1_ref, a1_in, ssem.at[0])
        a1_store.start()
        for load in loads[1:]:
            load.wait()
        for own in owns:
            own.start()

        wkv_gather.settle(1)
        for s in range(2, far + 1):
            wkv_gather.advance(s)
            wkv_gather.settle(s)
        for s in range(1, far + 1):
            wkv_gather.complete(s)
        for s in range(0, far + 1):
            wkv_gather.all_from_partner(s)
        owns[0].wait()
        wkv_load = pltpu.make_async_copy(wkv_ref, wkv, wsem.at[0])
        wkv_load.start()
        wkv_load.wait()
        pairs = matmul(a1_ref[...], wkv[...].reshape(width, 2 * key_cols))
        cosine, sine = turn_ref[0], turn_ref[1]
        for tile in range(2 * key_cols // LANES):
            part = pairs[:, tile * LANES : (tile + 1) * LANES]
            which, at = tile * LANES // key_cols, tile * LANES % key_cols
            if which == 0:
                part = part * cosine + turned(part) * sine
            kv[ctx, which, :, at : at + LANES] = part.astype(BF16)

        def kv_copy(source, target, step):
            return pltpu.make_async_remote_copy(
                src_ref=kv.at[source],
                dst_ref=kv.at[source],
                send_sem=kv_send.at[step - 1],
                recv_sem=kv_recv.at[step - 1],
                device_id={"ctx": target},
                device_id_type=MESH,
            )

        for step in range(1, ctx_n):
            kv_copy(ctx, lax.rem(ctx + step, ctx_n), step).start()

        def wq_load(f, slot):
            return pltpu.make_async_copy(wq_ref.at[f], wbuf.at[slot], wsem.at[slot])

        def add_queries(blocks, first):
            for i, f in enumerate(blocks):
                wq_load(f, i).start()

            def one(i, _):
                f = pick(i, blocks)
                wq_load(f, i).wait()
                left = a1_ref[:, pl.ds(pl.multiple_of(f * shard, shard), shard)]
                acc[...] += matmul(left, wbuf[i])
                return 0

            if first:
                acc[...] = jnp.zeros_like(acc)
            lax.fori_loop(0, len(blocks), one, 0)

        for own in owns[1:]:
            own.wait()
        wq_gather.all_from_partner(0)
        add_queries(wq_gather.blocks(0), True)
        for s in range(1, far + 1):
            wq_gather.advance(s)
            if s == max(far - 1, 1):
                wout_gather.begin()
            wq_gather.settle(s)
            wq_gather.complete(s)
            wq_gather.all_from_partner(s)
            add_queries(wq_gather.blocks(s), False)

        def turn_tile(j, _):
            at = pl.ds(pl.multiple_of(j * LANES, LANES), LANES)
            part = acc[:, at]
            q_ref[:, at] = (part * turn_ref[0] + turned(part) * turn_ref[1]).astype(BF16)
            return 0

        lax.fori_loop(0, width // LANES, turn_tile, 0)
        a1_store.wait()
        q_store = pltpu.make_async_copy(q_ref, q_in, ssem.at[0])
        q_store.start()
        for step in range(1, ctx_n):
            kv_copy(ctx, lax.rem(ctx + step, ctx_n), step).wait_send()
            sender = lax.rem(ctx - step + ctx_n, ctx_n)
            kv_copy(sender, sender, step).wait_recv()

        lse_ref[...] = jnp.zeros_like(lse_ref)

        def groups(lo, hi):
            def body(group, _):
                spread_heads(kv, 0, kz, group)
                spread_heads(kv, 1, vz, group)
                attend_group(group, q_ref, kz, vz, mask_ref, o_ref, lse_ref)
                return 0

            lax.fori_loop(lo, hi, body, 0)

        groups(0, 2)
        for s in range(1, far):
            wout_gather.advance(s)
            if s < far - 1:
                wout_gather.settle(s)
        cot_gather.begin()
        groups(2, KV)
        q_store.wait()
        stores = [
            pltpu.make_async_copy(o_ref, o_in, isem.at[0]),
            pltpu.make_async_copy(lse_ref, lse_in, isem.at[1]),
        ]
        for store in stores:
            store.start()
        def wout_load(f, slot):
            return pltpu.make_async_copy(wout_ref.at[f], obuf.at[slot], wsem.at[slot])

        for s in range(0, far + 1):
            if s == 0:
                for late in range(max(far - 1, 1), far + 1):
                    if late == far:
                        wout_gather.advance(late)
                    wout_gather.settle(late)
            if s:
                wout_gather.complete(s)
            wout_gather.all_from_partner(s)
            blocks = wout_gather.blocks(s)
            for i in range(len(blocks)):
                wout_load(blocks[i], i).start()

            def project(i, _, blocks=blocks):
                f = pick(i, blocks)
                wout_load(f, i).wait()
                at = pl.ds(pl.multiple_of(f * shard, shard), shard)
                dh1[:, at] = x_ref[:, at].astype(F32) + matmul(o_ref[...], obuf[i])
                return 0

            lax.fori_loop(0, len(blocks), project, 0)
        gain = gain2_ref[...]

        def norm_two(i, _):
            rows = pl.ds(pl.multiple_of(i * step_rows, step_rows), step_rows)
            a1_ref[rows] = normed(dh1[rows], gain)[2]
            return 0

        lax.fori_loop(0, 4, norm_two, 0)
        a2_store = pltpu.make_async_copy(a1_ref, rows_all.at[fsdp], ssem.at[0])
        a2_store.start()
        h1_store = pltpu.make_async_copy(dh1, h1_ref, ssem.at[1])
        h1_store.start()
        a2_store.wait()
        gather.begin()
        h1_store.wait()
        for store in stores:
            store.wait()
        wkv_gather.end()
        wq_gather.end()
        wout_gather.end()

    rows_type = pltpu.VMEM((count, width), BF16)
    pl.run_scoped(
        forward,
        rows_type,
        rows_type,
        pltpu.VMEM(wkv_ref.shape, BF16),
        pltpu.VMEM((count, width), F32),
        pltpu.VMEM((4,) + wq_ref.shape[1:], BF16),
        rows_type,
        rows_type,
        pltpu.VMEM((2, 2 * keys, LANES), BF16),
        pltpu.VMEM((2, 2 * keys, LANES), BF16),
        pltpu.VMEM(mask_in.shape, F32),
        pltpu.VMEM(turn_in.shape, F32),
        pltpu.VMEM(lse_in.shape, F32),
        pltpu.VMEM((4,) + wout_ref.shape[1:], BF16),
    )

    def ring_sum(partial, rows, wide, sems, first=0):
        return RingSum(ring, partial, arena, rows, wide, sems, first)

    def feed_forward(wgate, wup, wdown, hb, abuf, cbuf, stage):
        loads = [
            pltpu.make_async_copy(wdown_ref, wdown, isem.at[4]),
            pltpu.make_async_copy(wgate_ref, wgate, isem.at[5]),
            pltpu.make_async_copy(wup_ref, wup, isem.at[6]),
        ]
        for load in loads:
            load.start()

        def each(source, blocks, body):
            def fetch(f, slot):
                return pltpu.make_async_copy(source.at[f], abuf.at[slot], isem.at[slot])

            for i, f in enumerate(blocks):
                fetch(f, i).start()

            def step(i, _):
                f = pick(i, blocks)
                fetch(f, i).wait()
                body(f, i)
                return 0

            lax.fori_loop(0, len(blocks), step, 0)

        def dhid(f, slot):
            hb[2, f] = through(abuf[slot], wdown[...]).astype(BF16)

        def gates(f, slot):
            rows = abuf[slot]
            hidden, dgate, dup = gate_back(
                hb[2, f].astype(F32), through(rows, wgate[...]), through(rows, wup[...])
            )
            hb[0, f] = dgate
            hb[1, f] = dup
            hb[2, f] = hidden

        for load in loads:
            load.wait()
        for s in range(far + 1):
            if s == 1:
                cot_gather.advance(s)
            if s:
                cot_gather.settle(s)
            cot_gather.all_from_partner(s)
            each(cot_ref, cot_gather.blocks(s), dhid)
            if s:
                gather.advance(s)
                if s < far:
                    cot_gather.advance(s + 1)
                gather.settle(s)
            gather.all_from_partner(s)
            each(rows_all, gather.blocks(s), gates)
        cot_gather.end()
        gather.end()

        wide = 2 * LANES
        per_kind = width // wide
        total = 3 * per_kind

        def chunk_load(m, start):
            slot = lax.rem(m, 2)
            at = pl.multiple_of(lax.rem(m, per_kind) * wide, wide)
            for source, use in ((rows_all, m < 2 * per_kind), (cot_ref, m >= 2 * per_kind)):
                copy = pltpu.make_async_copy(
                    source.at[:, :, pl.ds(at, wide)], cbuf.at[slot], wsem.at[slot]
                )
                pl.when(use)(copy.start if start else copy.wait)

        def chunk_store(m):
            slot = lax.rem(m, 2)
            return pltpu.make_async_copy(
                stage.at[slot], gz_ref.at[pl.ds(2 * m, 2)], ssem.at[slot]
            )

        def gradients(m, lo):
            slot = lax.rem(m, 2)
            pl.when(m + 1 < total)(lambda: chunk_load(jnp.minimum(m + 1, total - 1), True))
            chunk_load(m, False)
            right = cbuf[slot].reshape(fsdp_n * count, wide)
            left = hb[m // per_kind].reshape(fsdp_n * count, local)
            out = across(left, right).astype(BF16)
            pl.when(m >= lo + 2)(lambda: chunk_store(jnp.maximum(m - 2, 0)).wait())
            stage[slot, 0] = out[:, :LANES]
            stage[slot, 1] = out[:, LANES:]
            chunk_store(m).start()

        def run(lo, hi, every=0):
            start = clock[0]

            def body(m, _):
                gradients(m, lo)
                if every:
                    pl.when(lax.rem(m - lo, every) == every - 1)(
                        lambda: line.tick(start + (m - lo) // every)
                    )
                return 0

            lax.fori_loop(lo, hi, body, 0)
            for m in (hi - 2, hi - 1):
                chunk_store(jnp.int32(m)).wait()
            if every:
                clock[0] = start + (hi - lo) // every

        chunk_load(jnp.int32(0), True)
        head = 4
        run(0, head)
        cap[0] = 2 * head - 1
        ticks(3)

        def da2_partial(f, at):
            return matmul(hb[0, f], wgate[:, at]) + matmul(hb[1, f], wup[:, at])

        da2 = ring_sum(da2_partial, count, width, da2_sems)
        da2.pair_all(lambda i: ticks(1))
        middle = head + (total - head) // 2
        run(head, middle, 2)
        da2.launch()
        run(middle, total, 3)
        cap[0] = line.first
        ticks(2)
        own_cot = pltpu.make_async_copy(cot_ref.at[fsdp], abuf.at[0], isem.at[0])
        own_cot.start()
        da2.finish()
        own_cot.wait()
        gain = gain2_ref[...]
        piece = count // 4

        def norm_back(i, acc):
            rows = pl.ds(pl.multiple_of(i * piece, piece), piece)
            hidden = dh1[rows]
            grad = da2.value(rows)
            factor = lax.rsqrt(jnp.mean(hidden * hidden, -1, keepdims=True) + EPSILON)
            unit = hidden * factor
            dh1[rows] = abuf[0, rows].astype(F32) + normed_back(unit, factor, grad, gain)
            return acc + jnp.sum(grad * unit, 0, keepdims=True)

        gain2_sum = lax.fori_loop(0, 4, norm_back, jnp.zeros((1, width), F32))
        gslot[fsdp, 1:2] = gain2_sum
        settle()

        def out_partial(f, at):
            return matmul(hb[2, f], wdown[:, at])

        mlp_out = ring_sum(out_partial, count, width, out_sems)
        mlp_out.pair_all(lambda i: ticks(1))
        holder.append(mlp_out)

    holder = []
    pl.run_scoped(
        feed_forward,
        pltpu.VMEM((local, width), BF16),
        pltpu.VMEM((local, width), BF16),
        pltpu.VMEM((local, width), BF16),
        pltpu.VMEM((3, fsdp_n, count, local), BF16),
        pltpu.VMEM((4, count, width), BF16),
        pltpu.VMEM((2, fsdp_n, count, 2 * LANES), BF16),
        pltpu.VMEM((2, 2, local, LANES), BF16),
    )
    mlp_out = holder[0]

    def attention_back(
        q_ref, o_ref, do_ref, a1_ref, dhb_ref, lse_ref, mask_ref, turn_ref,
        h1_buf, obuf, wbuf, wkv, kz, vz, dk_acc, dv_acc, gqkv, dkv,
    ):
        loads = [
            pltpu.make_async_copy(src, dst, isem.at[i])
            for i, (src, dst) in enumerate(
                [
                    (q_in, q_ref),
                    (o_in, o_ref),
                    (a1_in, a1_ref),
                    (lse_in, lse_ref),
                    (mask_in, mask_ref),
                    (turn_in, turn_ref),
                ]
            )
        ]

        def wout_load(f):
            return pltpu.make_async_copy(wout_ref.at[f], obuf.at[f % 2], wsem.at[f % 2])

        wout_load(0).start()
        for load in loads:
            load.start()
        dhb_ref[...] = dh1[...].astype(BF16)
        for f in range(fsdp_n):
            if f + 1 < fsdp_n:
                wout_load(f + 1).start()
            wout_load(f).wait()
            term = through(dhb_ref[:, f * shard : (f + 1) * shard], obuf[f % 2])
            h1_buf[...] = term if f == 0 else h1_buf[...] + term
        do_ref[...] = h1_buf[...].astype(BF16)
        h1_load = pltpu.make_async_copy(h1_ref, h1_buf, ssem.at[0])
        h1_load.start()
        ticks(2)
        mlp_out.launch()
        for load in loads:
            load.wait()

        step_keys = min(keys, 4 * LANES)

        def piece(par, q4, do4, lse, delta, at, mask, grad_q):
            span = pl.ds(at, step_keys)
            k_part = kz[par, span]
            v_part = vz[par, span]
            scores = through(q4, k_part)
            if mask is not None:
                scores = scores + mask
            probs = jnp.exp(scores - lse)
            dprob = through(do4, v_part)
            dscore = (probs * (dprob - delta)).astype(BF16)
            dk_acc[par, span] += across(dscore, q4)
            dv_acc[par, span] += across(probs.astype(BF16), do4)
            return grad_q + matmul(dscore, k_part)

        def group_step(group, rb):
            rows = pl.ds(rb * block, block)
            q4 = stacked(q_ref, rows, group) * jnp.asarray(scale, BF16)
            do4 = stacked(do_ref, rows, group)
            prod = do4.astype(F32) * stacked(o_ref, rows, group).astype(F32)
            lse_all = lse_ref[rb]
            grad_q = jnp.zeros((PAIRS * block, LANES), F32)
            for par in range(2):
                lse = jnp.sum(
                    jnp.where(lanes_of(lse_all.shape) == 2 * group + par, lse_all, 0.0),
                    -1,
                    keepdims=True,
                )
                delta = jnp.sum(
                    jnp.where(lanes_of(prod.shape) // HD == par, prod, 0.0), -1, keepdims=True
                )
                for at in range(0, (rb + 1) * keys, step_keys):
                    mask = None
                    if at >= rb * keys:
                        mask = mask_ref[rb, :, pl.ds(at - rb * keys, step_keys)]
                        mask = jnp.concatenate([mask] * PAIRS, 0)
                    grad_q = piece(par, q4, do4, lse, delta, at, mask, grad_q)
            grad_q = grad_q * scale
            cosine, sine = turn_ref[0, rows], turn_ref[1, rows]
            for j in range(PAIRS):
                part = grad_q[j * block : (j + 1) * block]
                at = pl.multiple_of((group * PAIRS + j) * LANES, LANES)
                gqkv[rows, pl.ds(at, LANES)] = (part * cosine - turned(part) * sine).astype(BF16)

        def dkv_copy(owner, tile, step):
            return pltpu.make_async_remote_copy(
                src_ref=dkv.at[owner, tile],
                dst_ref=dkv_in.at[ctx, tile],
                send_sem=dkv_send.at[step, tile],
                recv_sem=dkv_recv.at[step, tile],
                device_id={"ctx": owner},
                device_id_type=MESH,
            )

        def attention(lo, hi):
            start = clock[0]

            def body(group, _):
                spread_heads(kv, 0, kz, group)
                spread_heads(kv, 1, vz, group)
                dk_acc[...] = jnp.zeros_like(dk_acc)
                dv_acc[...] = jnp.zeros_like(dv_acc)
                for rb in range(2):
                    group_step(group, rb)
                    line.tick(start + (group - lo) * 2 + rb)
                tile = group // 2
                for which, acc in enumerate((dk_acc, dv_acc)):
                    for part in range(ctx_n):
                        for rb in range(2):
                            span = pl.ds(rb * keys + part * block, block)
                            both = jnp.where(
                                lanes_of((block, LANES)) < HD, acc[0, span], acc[1, span]
                            )
                            both = both + roll_lanes(both, HD)
                            there = (part, tile, which, pl.ds(rb * block, block))
                            mine = lanes_of((block, LANES)) // HD == lax.rem(group, 2)
                            dkv[there] = jnp.where(mine, both.astype(BF16), dkv[there])
                return 0

            lax.fori_loop(lo, hi, body, 0)
            clock[0] = start + (hi - lo) * 2

        def send_dkv(tile):
            for step in range(1, ctx_n):
                dkv_copy(lax.rem(ctx + step, ctx_n), tile, step - 1).start()

        attention(0, 2)
        send_dkv(0)
        mlp_out.finish()
        h1_load.wait()

        def add_out(rows):
            h1_buf[rows] = h1_buf[rows] + mlp_out.value(rows)

        mlp_out.by_rows(add_out)
        settle()

        def output_partial(f, at):
            return across(dhb_ref[:, pl.ds(pl.multiple_of(f * shard, shard), shard)], o_ref[:, at])

        ysum = ring_sum(output_partial, shard, width, ysems)
        ysum.pair_all(lambda i: ticks(1) if i else None)
        attention(2, 3)
        ysum.launch()
        attention(3, 4)
        send_dkv(1)
        ticks(3)
        do_ref[...] = h1_buf[...].astype(BF16)
        result_copy = pltpu.make_async_copy(do_ref, result_out, isem.at[0])
        result_copy.start()
        ysum.finish()

        def keep_output(rows):
            az[rows, :width] = ysum.value(rows).astype(BF16)

        ysum.by_rows(keep_output)
        cap[0] = line.first + width // (2 * LANES)
        settle()
        x_load = pltpu.make_async_copy(x_in, q_ref, isem.at[1])
        x_load.start()

        def query_partial(f, at):
            return across(a1_ref[:, pl.ds(pl.multiple_of(f * shard, shard), shard)], gqkv[:, at])

        def pair_partial(f, at):
            return across(
                a1_ref[:, pl.ds(pl.multiple_of(f * shard, shard), shard)],
                gqkv[:, pl.ds(width, 2 * key_cols)],
            )

        xsum = ring_sum(query_partial, shard, width, xsems)
        xsum.pair_all(lambda i: ticks(1))
        for step in range(1, ctx_n):
            for tile in range(KV // 2):
                dkv_copy(lax.rem(ctx + step, ctx_n), tile, step - 1).wait_send()
                sender = lax.rem(ctx - step + ctx_n, ctx_n)
                pltpu.make_async_remote_copy(
                    src_ref=dkv.at[sender, tile],
                    dst_ref=dkv_in.at[sender, tile],
                    send_sem=dkv_send.at[step - 1, tile],
                    recv_sem=dkv_recv.at[step - 1, tile],
                    device_id={"ctx": sender},
                    device_id_type=MESH,
                ).wait_recv()
        cosine, sine = turn_ref[0], turn_ref[1]
        for tile in range(KV // 2):
            for which in range(2):
                part = dkv[ctx, tile, which].astype(F32)
                for step in range(1, ctx_n):
                    part = part + dkv_in[lax.rem(ctx + step, ctx_n), tile, which].astype(F32)
                if which == 0:
                    part = part * cosine - turned(part) * sine
                at = width + which * key_cols + tile * LANES
                gqkv[:, at : at + LANES] = part.astype(BF16)

        kvsum = ring_sum(pair_partial, shard, 2 * key_cols, kvsems, width)
        kvsum.pair_all()
        ticks(2)
        xsum.launch()
        kvsum.launch()
        ticks(2)

        def weight_copies(f):
            slot = f % 2
            return (
                pltpu.make_async_copy(wq_ref.at[f], wbuf.at[slot], wsem.at[slot]),
                pltpu.make_async_copy(wkv_ref.at[f], wkv.at[slot], wsem.at[2 + slot]),
            )

        for copy in weight_copies(0):
            copy.start()
        for f in range(fsdp_n):
            if f + 1 < fsdp_n:
                for copy in weight_copies(f + 1):
                    copy.start()
            for copy in weight_copies(f):
                copy.wait()
            h1_buf[:, f * shard : (f + 1) * shard] = through(
                gqkv[:, :width], wbuf[f % 2]
            ) + through(gqkv[:, width:], wkv[f % 2])
            if f % (fsdp_n // 4) == 0:
                ticks(1)
        ticks(1)
        x_load.wait()
        gain = gain1_ref[...]
        piece_rows = count // 4

        def norm_back(i, acc):
            rows = pl.ds(pl.multiple_of(i * piece_rows, piece_rows), piece_rows)
            x = q_ref[rows].astype(F32)
            grad = h1_buf[rows]
            factor = lax.rsqrt(jnp.mean(x * x, -1, keepdims=True) + EPSILON)
            unit = x * factor
            o_ref[rows] = (dh1[rows] + normed_back(unit, factor, grad, gain)).astype(BF16)
            return acc + jnp.sum(grad * unit, 0, keepdims=True)

        gslot[fsdp, 0:1] = lax.fori_loop(0, 4, norm_back, jnp.zeros((1, width), F32))
        gtok_copy = pltpu.make_async_copy(o_ref, gtok_out, isem.at[2])
        gtok_copy.start()

        def gain_copy(slots, axis, here, step, sems):
            n = fsdp_n if axis == "fsdp" else ctx_n
            return pltpu.make_async_remote_copy(
                src_ref=slots.at[here],
                dst_ref=slots.at[here],
                send_sem=sems[0].at[step - 1],
                recv_sem=sems[1].at[step - 1],
                device_id={axis: lax.rem((fsdp if axis == "fsdp" else ctx) + step, n)},
                device_id_type=MESH,
            )

        def exchange(slots, axis, n, me, sems):
            for step in range(1, n):
                gain_copy(slots, axis, me, step, sems).start()
            for step in range(1, n):
                gain_copy(slots, axis, me, step, sems).wait_send()
                gain_copy(slots, axis, lax.rem(me - step + n, n), step, sems).wait_recv()
            total = slots[0]
            for i in range(1, n):
                total = total + slots[i]
            return total

        ticks(1)
        cslot[ctx] = exchange(gslot, "fsdp", fsdp_n, fsdp, (gain_send, gain_recv))
        ticks(2)
        gains_ref[...] = exchange(cslot, "ctx", ctx_n, ctx, (cgain_send, cgain_recv))

        ticks(2)
        xsum.finish()
        kvsum.finish()

        def keep_query(rows):
            az[rows, width : 2 * width] = xsum.value(rows).astype(BF16)
            az[rows, 2 * width :] = kvsum.value(rows).astype(BF16)

        xsum.by_rows(keep_query)
        result_copy.wait()
        gtok_copy.wait()

    pl.run_scoped(
        attention_back,
        rows_type,
        rows_type,
        rows_type,
        rows_type,
        rows_type,
        pltpu.VMEM(lse_in.shape, F32),
        pltpu.VMEM(mask_in.shape, F32),
        pltpu.VMEM(turn_in.shape, F32),
        pltpu.VMEM((count, width), F32),
        pltpu.VMEM((2,) + wout_ref.shape[1:], BF16),
        pltpu.VMEM((2,) + wq_ref.shape[1:], BF16),
        pltpu.VMEM((2,) + wkv_ref.shape[1:], BF16),
        pltpu.VMEM((2, 2 * keys, LANES), BF16),
        pltpu.VMEM((2, 2 * keys, LANES), BF16),
        pltpu.VMEM((2, 2 * keys, LANES), F32),
        pltpu.VMEM((2, 2 * keys, LANES), F32),
        pltpu.VMEM((count, cols), BF16),
        pltpu.VMEM(dkv_in.shape, BF16),
    )
    cap[0] = line.ticks
    ticks(line.ticks - clock[0])


def layer(x, cot, wq, wkv, w_out, w_gate, w_up, w_down, mask, turn, gain_one, gain_two):
    ctx_n = lax.axis_size("ctx")
    fsdp_n = lax.axis_size("fsdp")
    count, width = x.shape
    local = w_gate.shape[0]
    shard = wq.shape[0]
    cols = wq.shape[1] + wkv.shape[1]
    chips = fsdp_n // 2
    far = chips // 2
    vmem = pl.BlockSpec(memory_space=pltpu.VMEM)
    hbm = pl.BlockSpec(memory_space=pl.ANY)
    dma = pltpu.SemaphoreType.DMA
    regular = pltpu.SemaphoreType.REGULAR
    zbuf = pltpu.VMEM((SLOTS, local, LANES), BF16)
    scratch = (
        [zbuf] * 5
        + [
            pltpu.VMEM((shard, cols + width), BF16),
            pltpu.VMEM((2 + chips + 2 * far, max(count, shard), cols), BF16),
            pltpu.VMEM((count, width), F32),
            pltpu.VMEM((ctx_n, KV // 2, 2, count, LANES), BF16),
            pltpu.VMEM((ctx_n, 2, count, KV * HD), BF16),
            pltpu.VMEM((fsdp_n, 2, width), F32),
            pltpu.VMEM((ctx_n, 2, width), F32),
        ]
        + [dma((SLOTS,))] * 5
        + [dma((SLOTS, 2)), regular, regular]
        + gather_sems(chips) * 5
        + sum_sems(chips) * 5
        + [
            dma((ctx_n - 1, KV // 2)),
            dma((ctx_n - 1, KV // 2)),
            dma((ctx_n - 1,)),
            dma((ctx_n - 1,)),
            dma((fsdp_n - 1,)),
            dma((fsdp_n - 1,)),
            dma((ctx_n - 1,)),
            dma((ctx_n - 1,)),
            dma((4,)),
            dma((9,)),
            dma((2,)),
            regular((4,)),
        ]
    )

    def bf16(*shape):
        return jax.ShapeDtypeStruct(shape, BF16)

    return pl.pallas_call(
        functools.partial(layer_kernel, (ctx_n, fsdp_n)),
        out_shape=(
            bf16(count, width),
            bf16(count, width),
            jax.ShapeDtypeStruct((2, width), F32),
            bf16(local, width),
            bf16(local, width),
            bf16(local, width),
            bf16(shard, cols),
            bf16(shard, width),
            bf16(fsdp_n, count, width),
            bf16(3 * width // LANES, local, LANES),
            bf16(fsdp_n, *wq.shape),
            bf16(fsdp_n, *wkv.shape),
            bf16(fsdp_n, *w_out.shape),
            bf16(fsdp_n, count, width),
            bf16(count, width),
            bf16(count, width),
            bf16(count, width),
            jax.ShapeDtypeStruct((count, width), F32),
            jax.ShapeDtypeStruct((2, PAIRS * count // 2, LANES), F32),
        ),
        in_specs=[hbm] * 10 + [vmem] * 2,
        out_specs=(hbm, hbm, vmem) + (hbm,) * 16,
        scratch_shapes=scratch,
        compiler_params=pltpu.CompilerParams(
            collective_id=1, has_side_effects=True, vmem_limit_bytes=VMEM_LIMIT
        ),
        name="layer",
    )(x, cot, wq, wkv, w_out, w_gate, w_up, w_down, mask, turn, gain_one, gain_two)[:8]


def widen_kernel(
    swap_ref,
    gate_in,
    up_in,
    down_in,
    query_in,
    pair_in,
    output_in,
    result_in,
    gtok_in,
    gate_out,
    up_out,
    down_out,
    query_out,
    key_out,
    value_out,
    output_out,
    result_out,
    gtok_out,
):
    gate_out[...] = gate_in[...].astype(F32)
    up_out[...] = up_in[...].astype(F32)
    down_out[...] = down_in[...].astype(F32)
    query_out[...] = query_in[...].astype(F32)
    output_out[...] = output_in[...].astype(F32).T

    @pl.when(pl.program_id(0) == 0)
    def _():
        half = key_out.shape[1]
        key_out[...] = pair_in[:, :half].astype(F32)
        value_out[...] = pair_in[:, half:].astype(F32)

    @pl.when(pl.program_id(0) < 2)
    def _():
        result_out[...] = result_in[...]
        gtok_out[...] = gtok_in[...]


def widen(swap, gate, up, down, query, output, result, gtok):
    local, width = gate.shape
    shard = query.shape[0]
    count = result.shape[0]
    key_cols = KV * HD
    wide = 2 * LANES

    def columns(rows):
        return pl.BlockSpec((rows, wide), lambda i, swap: (0, i))

    def whole(*shape, at=0):
        return pl.BlockSpec(shape, lambda i, swap: (0, at))

    rows_in = pl.BlockSpec(
        (count // 2, width), lambda i, swap: (lax.rem(jnp.minimum(i, 1) + swap[0], 2), 0)
    )
    rows_out = pl.BlockSpec((count // 2, width), lambda i, swap: (jnp.minimum(i, 1), 0))

    def f32(*shape):
        return jax.ShapeDtypeStruct(shape, F32)

    return pl.pallas_call(
        widen_kernel,
        grid_spec=pltpu.PrefetchScalarGridSpec(
            num_scalar_prefetch=1,
            grid=(width // wide,),
            in_specs=[columns(local)] * 3
            + [
                columns(shard),
                whole(shard, 2 * key_cols, at=width // (2 * key_cols)),
                columns(shard),
                rows_in,
                rows_in,
            ],
            out_specs=[columns(local)] * 3
            + [
                columns(shard),
                whole(shard, key_cols),
                whole(shard, key_cols),
                pl.BlockSpec((wide, shard), lambda i, swap: (i, 0)),
                rows_out,
                rows_out,
            ],
        ),
        out_shape=[f32(local, width)] * 3
        + [
            f32(shard, width),
            f32(shard, key_cols),
            f32(shard, key_cols),
            f32(width, shard),
            jax.ShapeDtypeStruct((count, width), BF16),
            jax.ShapeDtypeStruct((count, width), BF16),
        ],
        compiler_params=pltpu.CompilerParams(vmem_limit_bytes=VMEM_LIMIT),
        name="widen",
    )(swap, gate, up, down, query, query, output, result, gtok)


def shards(
    tokens,
    cotangent,
    block_table,
    gain_attn,
    w_query,
    w_key,
    w_value,
    w_output,
    gain_mlp,
    w_gate,
    w_up,
    w_down,
):
    ctx_n = lax.axis_size("ctx")
    ctx = lax.axis_index("ctx")
    count, width = tokens.shape[1:]
    block = count // 2

    table = block_table.reshape(ctx_n, 2)
    lower, upper = jnp.min(table, 1), jnp.max(table, 1)
    owned = table[ctx]
    swap = owned[0] > owned[1]

    def ordered(rows):
        return jnp.where(swap, jnp.concatenate([rows[block:], rows[:block]], 0), rows)

    offsets = jnp.arange(block, dtype=jnp.int32)
    spots = jnp.stack([lower, upper])[:, :, None] * block + offsets
    own_spots = spots[:, ctx]
    key_spots = spots.reshape(2, -1)
    mask = jnp.where(own_spots[:, :, None] >= key_spots[:, None, :], 0.0, NEGATIVE).astype(F32)
    freqs = 10000.0 ** (-jnp.arange(HD // 2, dtype=F32) / (HD // 2))
    angle = own_spots.reshape(-1).astype(F32)[:, None] * freqs[None, :]
    angle = jnp.concatenate([angle] * (LANES * 2 // HD), -1)
    turn = jnp.stack([jnp.cos(angle), jnp.sin(angle)])

    rows_in = ordered(tokens[0])
    grad_out = ordered(cotangent[0])

    result, grad_tokens, gains, gate_sum, up_sum, down_sum, query_sum, output_sum = layer(
        rows_in,
        grad_out,
        w_query,
        jnp.concatenate([w_key, w_value], 1),
        w_output,
        w_gate.T,
        w_up.T,
        w_down,
        mask,
        turn,
        gain_attn[None],
        gain_mlp[None],
    )
    grad_gate, grad_up, grad_down, grad_query, grad_key, grad_value, grad_output, result, grad_tokens = (
        widen(
            swap.astype(jnp.int32)[None],
            gate_sum,
            up_sum,
            down_sum,
            query_sum,
            output_sum,
            result,
            grad_tokens,
        )
    )
    return (
        result[None],
        grad_tokens[None],
        grad_query,
        grad_key,
        grad_value,
        grad_output,
        grad_gate.T,
        grad_up.T,
        grad_down,
        gains[0],
        gains[1],
    )


def solution(mesh):
    in_specs = (
        P("fsdp", "ctx", None),
        P("fsdp", "ctx", None),
        P(),
        P(),
        P("fsdp", None),
        P("fsdp", None),
        P("fsdp", None),
        P(None, "fsdp"),
        P(),
        P(None, "fsdp"),
        P(None, "fsdp"),
        P("fsdp", None),
    )
    out_specs = (
        P("fsdp", "ctx", None),
        P("fsdp", "ctx", None),
        P("fsdp", None),
        P("fsdp", None),
        P("fsdp", None),
        P(None, "fsdp"),
        P(None, "fsdp"),
        P(None, "fsdp"),
        P("fsdp", None),
        P(),
        P(),
    )
    return jax.shard_map(shards, mesh=mesh, in_specs=in_specs, out_specs=out_specs, check_vma=False)
```

```python
import functools

import jax
import jax.numpy as jnp
from jax import lax
from jax.experimental import pallas as pl
from jax.experimental.pallas import tpu as pltpu
from jax.sharding import PartitionSpec as P

H = 32
KV = 4
HD = 64
GROUP = H // KV
PAIRS = GROUP // 2
LANES = 128

EPSILON = 1e-05
NEGATIVE = -1e30
SLOTS = 8
GAP = 3
VMEM_LIMIT = 61 * 1024 * 1024
MESH = pl.DeviceIdType.MESH
F32 = jnp.float32
BF16 = jnp.bfloat16


def dot(left, right, left_dim, right_dim):
    return lax.dot_general(
        left, right, (((left_dim,), (right_dim,)), ((), ())), preferred_element_type=F32
    )


def matmul(left, right):
    return dot(left, right, 1, 0)


def across(left, right):
    return dot(left, right, 0, 0)


def through(left, right):
    return dot(left, right, 1, 1)


def normed(hidden, gain):
    factor = lax.rsqrt(jnp.mean(hidden * hidden, -1, keepdims=True) + EPSILON)
    unit = hidden * factor
    return (unit, factor, (unit * gain).astype(BF16))


def normed_back(unit, factor, grad_in, gain):
    scaled = grad_in * gain
    return factor * (scaled - unit * jnp.mean(scaled * unit, -1, keepdims=True))


def gate_back(grad_hidden, gate, up):
    sigma = jax.nn.sigmoid(gate)
    activated = gate * sigma
    grad_gate_in = (grad_hidden * up * sigma * (1.0 + gate * (1.0 - sigma))).astype(BF16)
    grad_up_in = (grad_hidden * activated).astype(BF16)
    return ((activated * up).astype(BF16), grad_gate_in, grad_up_in)


def lanes_of(shape):
    return lax.broadcasted_iota(jnp.int32, shape, len(shape) - 1)


def roll_lanes(value, amount):
    return pltpu.roll(value, amount, 1)


def turned(value):
    first = lax.rem(lanes_of(value.shape), HD) < HD // 2
    return jnp.where(first, -roll_lanes(value, LANES - HD // 2), roll_lanes(value, HD // 2))


def stacked(ref, rows, group):
    wide = PAIRS * LANES
    block = ref[rows, pl.ds(pl.multiple_of(group * wide, wide), wide)]
    return jnp.concatenate([block[:, j * LANES : (j + 1) * LANES] for j in range(PAIRS)], 0)


def spread_heads(kv_ref, which, out_ref, group):
    devices, _, count, _ = kv_ref.shape
    block = count // 2
    at = pl.multiple_of((group // 2) * LANES, LANES)
    here = lax.rem(group, 2)
    for part in range(devices):
        tile = kv_ref[part, which, :, pl.ds(at, LANES)].astype(F32)
        other = roll_lanes(tile, HD)
        half = lanes_of(tile.shape) // HD
        for par in range(2):
            picked = jnp.where(here == par, tile, other)
            picked = jnp.where(half == par, picked, 0.0).astype(BF16)
            for rb in range(2):
                rows = pl.ds((rb * devices + part) * block, block)
                out_ref[par, rows] = picked[rb * block : (rb + 1) * block]


def attend_group(group, q_ref, kz, vz, mask_ref, o_ref, lse_ref):
    block = q_ref.shape[0] // 2
    keys = kz.shape[1] // 2
    together = PAIRS if keys <= 4 * LANES else PAIRS // 2
    for rb in range(2):
        rows = pl.ds(rb * block, block)
        every = stacked(q_ref, rows, group) * jnp.asarray(HD ** (-0.5), BF16)
        mask = jnp.concatenate([mask_ref[rb]] * together, 0)
        for first in range(0, PAIRS, together):
            some = slice(first * block, (first + together) * block)
            q4 = every[some]
            total = 0.0
            lse = lse_ref[rb, some]
            for par in range(2):
                scores = []
                for part in range(rb + 1):
                    score = through(q4, kz[par, pl.ds(part * keys, keys)])
                    scores.append(score + mask if part == rb else score)
                peak = functools.reduce(
                    jnp.maximum, [jnp.max(s, -1, keepdims=True) for s in scores]
                )
                probs = [jnp.exp(s - peak) for s in scores]
                norm = sum(jnp.sum(p, -1, keepdims=True) for p in probs)
                mixed = sum(
                    matmul(p.astype(BF16), vz[par, pl.ds(i * keys, keys)])
                    for i, p in enumerate(probs)
                )
                total = total + mixed / norm
                here = lanes_of(lse.shape) == 2 * group + par
                lse = jnp.where(here, peak + jnp.log(norm), lse)
            lse_ref[rb, some] = lse
            for j in range(together):
                at = pl.multiple_of((group * PAIRS + first + j) * LANES, LANES)
                o_ref[rows, pl.ds(at, LANES)] = total[j * block : (j + 1) * block].astype(BF16)


class LineSum:
    def __init__(self, count, index, first, second, sources, targets, bufs, sems):
        self.n = count
        self.first, self.second = first, second
        self.total = first + second
        self.mlp_src, self.att_src = sources
        self.gate_dst, self.up_dst, self.down_dst, self.query_dst, self.output_dst = targets
        self.own, self.rout, self.sums, self.rin, self.done = bufs
        (
            self.load_sem,
            self.in_send,
            self.rout_sem,
            self.rin_sem,
            self.out_send,
            self.store_sem,
            self.credit_in,
            self.credit_out,
        ) = sems
        half = count // 2
        left = index < half
        self.depth = jnp.where(left, index, count - 1 - index)
        step = jnp.where(left, 1, -1)
        self.inward = index + step
        outward = index - step
        self.has_out = self.depth > 0
        self.outward = jnp.where(self.has_out, outward, index + step)
        self.is_mid = self.depth == half - 1
        deepest = half - 1
        self.lag_sum = 1 + GAP * self.depth
        self.lag_sent = self.lag_sum + GAP
        self.lag_total = 1 + GAP * deepest + GAP + GAP * (deepest - self.depth)
        self.lag_end = self.lag_total + GAP
        self.ticks = self.total + 1 + 3 * GAP * deepest + 3 * GAP
        self.att_rows = 2 * self.att_src.shape[0]
        self.blocks = self.down_dst.shape[1] // LANES

    def view(self, buf, slot, att):
        return buf.at[slot, pl.ds(0, self.att_rows)] if att else buf.at[slot]

    def each(self, chunk, body):
        slot = lax.rem(jnp.maximum(chunk, 0), SLOTS)
        pl.when((chunk >= 0) & (chunk < self.first))(lambda: body(chunk, slot, False))
        if self.second:
            pl.when((chunk >= self.first) & (chunk < self.total))(lambda: body(chunk, slot, True))

    def send(self, src, dst, sems, target, slot, att):
        return pltpu.make_async_remote_copy(
            src_ref=self.view(src, slot, att),
            dst_ref=self.view(dst, slot, att),
            send_sem=sems[0].at[slot],
            recv_sem=sems[1].at[slot],
            device_id={"ctx": target},
            device_id_type=MESH,
        )

    def to_total(self, slot, att):
        return self.send(self.sums, self.rin, (self.in_send, self.rin_sem), self.inward, slot, att)

    def to_partial(self, slot, att):
        return self.send(
            self.sums, self.rout, (self.in_send, self.rout_sem), self.inward, slot, att
        )

    def to_outward(self, slot, att):
        return self.send(
            self.done, self.rin, (self.out_send, self.rin_sem), self.outward, slot, att
        )

    def load(self, chunk, slot):
        return pltpu.make_async_copy(
            self.mlp_src.at[chunk], self.own.at[slot], self.load_sem.at[slot]
        )

    def stores(self, chunk, slot, att):
        if att:
            rows = self.att_rows // 2
            wide = self.output_dst.shape[1] // LANES
            pairs = []
            for i in range(2):
                at = 2 * (chunk - self.first) + i
                src = self.done.at[slot, pl.ds(i * rows, rows)]
                sem = self.store_sem.at[slot, i]
                o_at = pl.multiple_of(jnp.minimum(at, wide - 1) * LANES, LANES)
                q_at = pl.multiple_of(jnp.maximum(at - wide, 0) * LANES, LANES)
                pairs.append(
                    (
                        at < wide,
                        pltpu.make_async_copy(src, self.output_dst.at[:, pl.ds(o_at, LANES)], sem),
                    )
                )
                pairs.append(
                    (
                        at >= wide,
                        pltpu.make_async_copy(src, self.query_dst.at[:, pl.ds(q_at, LANES)], sem),
                    )
                )
            return pairs
        kind = chunk // self.blocks
        at = pl.multiple_of(lax.rem(chunk, self.blocks) * LANES, LANES)
        sem = self.store_sem.at[slot, 0]
        return [
            (kind == i, pltpu.make_async_copy(self.done.at[slot], dst.at[:, pl.ds(at, LANES)], sem))
            for i, dst in enumerate((self.gate_dst, self.up_dst, self.down_dst))
        ]

    def tick(self, i):
        self.each(i - self.lag_sum + 1, self.stage_load)
        self.each(i - self.lag_sum, self.stage_sum)
        self.each(i - self.lag_sent, self.stage_sent)
        self.each(i - self.lag_total, self.stage_total)
        self.each(i - self.lag_end, self.stage_end)

    def stage_load(self, chunk, slot, att):
        if not att:
            self.load(chunk, slot).start()

    def stage_sum(self, chunk, slot, att):
        if not att:
            self.load(chunk, slot).wait()

        def own():
            if not att:
                return self.own[slot]
            at = (chunk - self.first) * 2 * LANES
            return jnp.concatenate(
                [
                    self.att_src[:, pl.ds(pl.multiple_of(at + i * LANES, LANES), LANES)]
                    for i in range(2)
                ],
                0,
            )

        @pl.when(self.has_out)
        def _():
            self.to_partial(slot, att).wait_recv()
            arrived = self.view(self.rout, slot, att)[...].astype(F32)
            self.view(self.sums, slot, att)[...] = (own().astype(F32) + arrived).astype(BF16)

            @pl.when(chunk < self.total - SLOTS)
            def _():
                pl.semaphore_signal(
                    self.credit_in, 1, device_id={"ctx": self.outward}, device_id_type=MESH
                )

        @pl.when(jnp.logical_not(self.has_out))
        def _():
            self.view(self.sums, slot, att)[...] = own()

        @pl.when(chunk >= SLOTS)
        def _():
            pl.semaphore_wait(self.credit_in, 1)

        pl.when(self.is_mid)(lambda: self.to_total(slot, att).start())
        pl.when(jnp.logical_not(self.is_mid))(lambda: self.to_partial(slot, att).start())

    def stage_sent(self, chunk, slot, att):
        self.to_total(slot, att).wait_send()

    def stage_total(self, chunk, slot, att):
        self.to_total(slot, att).wait_recv()
        arrived = self.view(self.rin, slot, att)
        done = self.view(self.done, slot, att)

        @pl.when(self.is_mid)
        def _():
            mine = self.view(self.sums, slot, att)[...].astype(F32)
            done[...] = (mine + arrived[...].astype(F32)).astype(BF16)

            @pl.when(chunk < self.total - SLOTS)
            def _():
                pl.semaphore_signal(
                    self.credit_in, 1, device_id={"ctx": self.inward}, device_id_type=MESH
                )

        @pl.when(jnp.logical_not(self.is_mid))
        def _():
            done[...] = arrived[...]

            @pl.when(chunk < self.total - SLOTS)
            def _():
                pl.semaphore_signal(
                    self.credit_out, 1, device_id={"ctx": self.inward}, device_id_type=MESH
                )

        @pl.when(self.has_out)
        def _():
            @pl.when(chunk >= SLOTS)
            def _():
                pl.semaphore_wait(self.credit_out, 1)

            self.to_outward(slot, att).start()

        for condition, copy in self.stores(chunk, slot, att):
            pl.when(condition)(copy.start)

    def stage_end(self, chunk, slot, att):
        pl.when(self.has_out)(lambda: self.to_outward(slot, att).wait_send())
        for condition, copy in self.stores(chunk, slot, att):
            pl.when(condition)(copy.wait)


def chip_at(place):
    return 2 * (place // 2) + lax.rem(place + place // 2, 2)


class Ring:
    def __init__(self, count, index):
        self.chips = count // 2
        chip = index // 2
        self.core = lax.rem(index, 2)
        self.place = chip_at(chip)
        self.partner = 2 * chip + 1 - self.core
        self.right = self.device(1)
        self.left = self.device(-1)

    def device(self, offset, core=None):
        place = lax.rem(self.place + offset + self.chips, self.chips)
        return 2 * chip_at(place) + (self.core if core is None else core)


class RingGather:
    def __init__(self, ring, source, slots, sems, mate=None, odd=None):
        self.ring, self.source, self.slots = ring, source, slots
        self.sems, self.mate = sems, mate
        self.far = ring.chips // 2
        rows = slots.shape[1]
        self.share = rows // 4 if mate is not None else 0
        self.rows = rows - self.share
        if mate is None:
            self.start, self.give, self.take = 0, 0, 0
        else:
            self.start = pl.multiple_of(odd * self.share, 16)
            self.give = pl.multiple_of(odd * self.rows, 16)
            self.take = pl.multiple_of((1 - odd) * self.rows, 16)

    def span(self, half=None):
        if half is None:
            return pl.ds(self.start, self.rows)
        size = self.rows // 2
        return pl.ds(self.start + half * size, size)

    def move(self, src, dst, kind, index, target):
        return pltpu.make_async_remote_copy(
            src_ref=src,
            dst_ref=dst,
            send_sem=self.sems[2 * kind].at[index],
            recv_sem=self.sems[2 * kind + 1].at[index],
            device_id=target,
            device_id_type=MESH,
        )

    def copy(self, offset, target, kind, index, rows):
        block = self.ring.device(offset)
        src = self.source if offset == 0 else self.slots.at[block]
        return self.move(
            src.at[rows], self.slots.at[block, rows], kind, index, {"fsdp": target}
        )

    def rightward(self, s, half):
        return self.copy(-s, self.ring.right, 0, (s, half), self.span(half))

    def leftward(self, s, half):
        return self.copy(s, self.ring.left, 1, (s, half), self.span(half))

    def firsts(self, s):
        return [self.rightward(s, 0), self.leftward(s, 1)]

    def seconds(self, s):
        return [self.rightward(s, 1), self.leftward(s, 0)] if s + 1 < self.far else []

    def coming(self, s, half_left, half_right):
        return [
            self.copy(-s, self.ring.right, 0, (s - 1, half_left), self.span(half_left)),
            self.copy(s, self.ring.left, 1, (s - 1, half_right), self.span(half_right)),
        ]

    def index(self, offset):
        return 0 if offset == 0 else 2 * abs(offset) - (1 if offset < 0 else 0)

    def across(self, offset):
        rows = pl.ds(0, self.rows + self.share) if offset == 0 else self.span()
        return self.copy(offset, self.ring.partner, 2, self.index(offset), rows)

    def across_share(self, offset):
        rows = pl.ds(self.take, self.share)
        return self.copy(offset, self.ring.partner, 3, self.index(offset), rows)

    def to_mate(self, offset, core=None):
        block = self.ring.device(offset)
        rows = pl.ds(self.give, self.share)
        place = self.slots.at[block, rows]
        return self.move(place, place, 4, self.index(offset), {"ctx": self.mate})

    def offsets(self, s):
        return [s] if s == self.far else [-s, s]

    def begin(self):
        for message in self.firsts(0) + self.seconds(0):
            message.start()
        self.across(0).start()

    def advance(self, s):
        for message in self.coming(s, 0, 1):
            message.wait_recv()
        if s < self.far:
            for message in self.firsts(s):
                message.start()

    def settle(self, s):
        if s < self.far:
            for message in self.coming(s, 1, 0):
                message.wait_recv()
            for message in self.seconds(s):
                message.start()
        for offset in self.offsets(s):
            self.across(offset).start()
            if self.share:
                self.to_mate(offset).start()

    def complete(self, s):
        if self.share:
            for offset in self.offsets(s):
                block = self.ring.device(offset)
                place = self.slots.at[block, pl.ds(self.take, self.share)]
                self.move(
                    place, place, 4, self.index(offset), {"ctx": self.mate}
                ).wait_recv()
                self.across_share(offset).start()

    def from_partner(self, offset):
        block = self.ring.device(offset, 1 - self.ring.core)
        rows = pl.ds(0, self.rows + self.share) if offset == 0 else self.span()
        index = self.index(offset)
        target = {"fsdp": self.ring.partner}
        place = self.slots.at[block, rows]
        self.move(place, place, 2, index, target).wait_recv()
        if self.share and offset != 0:
            place = self.slots.at[block, pl.ds(self.take, self.share)]
            self.move(place, place, 3, index, target).wait_recv()

    def blocks(self, s):
        offsets = [0] if s == 0 else self.offsets(s)
        return [self.ring.device(o) for o in offsets] + [
            self.ring.device(o, 1 - self.ring.core) for o in offsets
        ]

    def all_from_partner(self, s):
        for offset in [0] if s == 0 else self.offsets(s):
            self.from_partner(offset)

    def end(self):
        for s in range(self.far):
            for message in self.firsts(s) + self.seconds(s):
                message.wait_send()
        self.across(0).wait_send()
        for s in range(1, self.far + 1):
            for offset in self.offsets(s):
                self.across(offset).wait_send()
                if self.share:
                    self.across_share(offset).wait_send()
                    self.to_mate(offset).wait_send()


def gather_sems(chips):
    far = chips // 2
    dma = pltpu.SemaphoreType.DMA
    return [dma((far, 2))] * 4 + [dma((2 * far + 1,))] * 6


def pick(index, choices):
    out = choices[0]
    for i, choice in enumerate(choices[1:]):
        out = jnp.where(index == i + 1, choice, out)
    return out


class RingSum:
    def __init__(self, ring, partial, arena, rows, cols, sems, first=0):
        self.ring, self.partial, self.first = ring, partial, first
        self.arena, self.rows, self.cols = arena, rows, cols
        (
            self.stage_send,
            self.pair_recv,
            self.right_send,
            self.right_recv,
            self.left_send,
            self.left_recv,
        ) = sems
        far = ring.chips // 2
        self.far = far
        offsets = [far]
        for s in range(far - 1, 0, -1):
            offsets += [s, -s]
        self.offsets = offsets + [0]
        self.at = {offset: i for i, offset in enumerate(self.offsets)}

    def view(self, slot, rows=None):
        rows = pl.ds(0, self.rows) if rows is None else rows
        return self.arena.at[slot, rows, pl.ds(self.first, self.cols)]

    def stage(self, i):
        return self.view(i % 2)

    def pair(self, i, rows=None):
        return self.view(2 + i, rows)

    def side(self, right, s, rows=None):
        return self.view(2 + self.ring.chips + (0 if right else self.far) + s - 1, rows)

    def half(self, which):
        return pl.ds(which * (self.rows // 2), self.rows // 2)

    def pair_copy(self, i):
        return pltpu.make_async_remote_copy(
            src_ref=self.stage(i),
            dst_ref=self.pair(i),
            send_sem=self.stage_send.at[i],
            recv_sem=self.pair_recv.at[i],
            device_id={"fsdp": self.ring.partner},
            device_id_type=MESH,
        )

    def by_columns(self, piece):
        wide = 4 * LANES

        def body(j, _):
            at = pl.multiple_of(j * wide, wide)
            piece(pl.ds(at, wide), pl.ds(pl.multiple_of(self.first + at, wide), wide))
            return 0

        lax.fori_loop(0, self.cols // wide, body, 0)

    def pair_step(self, i):
        offset = self.offsets[i]
        if i >= 2:
            self.pair_copy(i - 2).wait_send()
        owner = self.ring.device(offset, 1 - self.ring.core)
        rows = pl.ds(0, self.rows)

        def piece(at, place):
            self.arena[i % 2, rows, place] = self.partial(owner, at).astype(BF16)

        self.by_columns(piece)
        self.pair_copy(i).start()

    def pair_add(self, i):
        owner = self.ring.device(self.offsets[i])
        self.pair_copy(i).wait_recv()
        rows = pl.ds(0, self.rows)

        def piece(at, place):
            mine = self.partial(owner, at)
            there = (2 + i, rows, place)
            self.arena[there] = (mine + self.arena[there].astype(F32)).astype(BF16)

        self.by_columns(piece)

    def pair_all(self, between=None):
        last = len(self.offsets)
        for i in range(last):
            self.pair_step(i)
            if i >= 1:
                self.pair_add(i - 1)
                self.launch_free(i - 1)
            if between is not None:
                between(i)
        self.pair_add(last - 1)
        for i in range(max(last - 2, 0), last):
            self.pair_copy(i).wait_send()

    def hop(self, s, right, which):
        owner = self.at[s if right or s == self.far else -s]
        rows = self.half(which)
        return pltpu.make_async_remote_copy(
            src_ref=self.pair(owner, rows),
            dst_ref=self.side(right, s, rows),
            send_sem=(self.right_send if right else self.left_send).at[s - 1, which],
            recv_sem=(self.right_recv if right else self.left_recv).at[s - 1, which],
            device_id={"fsdp": self.ring.right if right else self.ring.left},
            device_id_type=MESH,
        )

    def hops(self):
        far = self.far
        moves = [(far, True, 0), (far, False, 1)]
        if far > 1:
            moves += [(far - 1, True, 1), (far - 1, False, 0)]
            moves += [(far - 1, True, 0), (far - 1, False, 1)]
        for s in range(far - 2, 0, -1):
            for which in range(2):
                moves += [(s, True, which), (s, False, which)]
        return moves

    def free(self, s, right, which):
        return s == self.far or (s == self.far - 1 and which == (1 if right else 0))

    def launch_free(self, i):
        offset = self.offsets[i]
        for s, right, which in self.hops():
            owner = s if right or s == self.far else -s
            if self.free(s, right, which) and owner == offset:
                self.hop(s, right, which).start()

    def launch(self):
        for s, right, which in self.hops():
            if not self.free(s, right, which):
                self.hop(s + 1, right, which).wait_recv()
                owner = self.at[s if right else -s]
                rows = self.half(which)
                arrived = self.side(right, s + 1, rows)
                mine = self.pair(owner, rows)
                mine[...] = (mine[...].astype(F32) + arrived[...].astype(F32)).astype(BF16)
                self.hop(s, right, which).start()

    def finish(self):
        for s, right, which in self.hops():
            if s == 1:
                self.hop(s, right, which).wait_recv()
            self.hop(s, right, which).wait_send()

    def by_rows(self, piece):
        step = self.rows // 4

        def body(i, _):
            piece(pl.ds(pl.multiple_of(i * step, step), step))
            return 0

        lax.fori_loop(0, 4, body, 0)

    def value(self, rows):
        own = self.pair(self.at[0], rows)[...].astype(F32)
        left = self.side(True, 1, rows)[...].astype(F32)
        return own + left + self.side(False, 1, rows)[...].astype(F32)


def sum_sems(chips):
    far = chips // 2
    dma = pltpu.SemaphoreType.DMA
    return [dma((chips,))] * 2 + [dma((far, 2))] * 4


def layer_kernel(
    sizes,
    x_in,
    cot_in,
    wq_in,
    wkv_in,
    wout_in,
    wgate_ref,
    wup_ref,
    wdown_ref,
    mask_in,
    turn_in,
    gain1_ref,
    gain2_ref,
    result_out,
    gtok_out,
    gains_ref,
    gate_out,
    up_out,
    down_out,
    query_out,
    output_out,
    rows_all,
    gz_ref,
    wq_ref,
    wkv_ref,
    wout_ref,
    cot_ref,
    q_in,
    o_in,
    a1_in,
    h1_ref,
    lse_in,
    *scratch,
):
    ctx_n, fsdp_n = sizes
    (
        zown,
        zrout,
        zsums,
        zrin,
        zdone,
        az,
        arena,
        dh1,
        dkv_in,
        kv,
        gslot,
        cslot,
    ) = scratch[:12]
    scratch = scratch[12:]
    zsems, scratch = scratch[:8], scratch[8:]
    gathers, scratch = [scratch[10 * i : 10 * i + 10] for i in range(5)], scratch[50:]
    da2_sems, scratch = scratch[:6], scratch[6:]
    out_sems, scratch = scratch[:6], scratch[6:]
    ysems, scratch = scratch[:6], scratch[6:]
    xsems, scratch = scratch[:6], scratch[6:]
    kvsems, scratch = scratch[:6], scratch[6:]
    (
        dkv_send,
        dkv_recv,
        kv_send,
        kv_recv,
        gain_send,
        gain_recv,
        cgain_send,
        cgain_recv,
        wsem,
        isem,
        ssem,
        ready,
    ) = scratch
    ctx = lax.axis_index("ctx")
    fsdp = lax.axis_index("fsdp")
    ring = Ring(fsdp_n, fsdp)
    count, width = x_in.shape
    block = count // 2
    keys = ctx_n * block
    scale = HD ** (-0.5)
    shard = query_out.shape[0]
    cols = query_out.shape[1]
    local = wgate_ref.shape[0]
    key_cols = KV * HD

    barrier = pltpu.get_barrier_semaphore()
    for axis, me, n in (("ctx", ctx, ctx_n), ("fsdp", fsdp, fsdp_n)):
        for step in range(1, n):
            pl.semaphore_signal(
                barrier, 1, device_id={axis: lax.rem(me + step, n)}, device_id_type=MESH
            )
    pl.semaphore_wait(barrier, ctx_n + fsdp_n - 2)

    rounds = [0]

    def settle():
        sem = ready.at[rounds[0]]
        rounds[0] += 1
        for target in (ring.partner, ring.left, ring.right):
            pl.semaphore_signal(sem, 1, device_id={"fsdp": target}, device_id_type=MESH)
        pl.semaphore_wait(sem, 3)

    line = LineSum(
        ctx_n,
        ctx,
        gz_ref.shape[0],
        az.shape[1] // (2 * LANES),
        (gz_ref, az),
        (gate_out, up_out, down_out, query_out, output_out),
        (zown, zrout, zsums, zrin, zdone),
        zsems,
    )
    clock = [0]
    cap = [0]

    def ticks(number):
        start = clock[0]
        number = max(min(number, cap[0] - start), 0)
        clock[0] = start + number

        def body(i, _):
            line.tick(i)
            return 0

        lax.fori_loop(start, start + number, body, 0)

    odd = lax.rem(ctx, 2)
    mate = ctx + 1 - 2 * odd
    help_along = ()
    wkv_gather = RingGather(ring, wkv_in, wkv_ref, gathers[0], *help_along)
    wq_gather = RingGather(ring, wq_in, wq_ref, gathers[1], *help_along)
    wout_gather = RingGather(ring, wout_in, wout_ref, gathers[2], mate, odd)
    cot_gather = RingGather(ring, cot_in, cot_ref, gathers[3])
    gather = RingGather(ring, rows_all.at[fsdp], rows_all, gathers[4])
    far = gather.far

    def forward(x_ref, a1_ref, wkv, acc, wbuf, q_ref, o_ref, kz, vz, mask_ref, turn_ref, lse_ref, obuf):
        wkv_gather.begin()
        loads = [
            pltpu.make_async_copy(src, dst, isem.at[i])
            for i, (src, dst) in enumerate(
                [
                    (x_in, x_ref),
                    (mask_in, mask_ref),
                    (turn_in, turn_ref),
                    (wkv_in, wkv.at[fsdp]),
                    (wq_in, wbuf.at[0]),
                    (wout_in, obuf.at[0]),
                    (cot_in, o_ref),
                ]
            )
        ]
        owns = [
            pltpu.make_async_copy(src, dst, isem.at[3 + i])
            for i, (src, dst) in enumerate(
                [
                    (wkv.at[fsdp], wkv_ref.at[fsdp]),
                    (wbuf.at[0], wq_ref.at[fsdp]),
                    (obuf.at[0], wout_ref.at[fsdp]),
                    (o_ref, cot_ref.at[fsdp]),
                ]
            )
        ]
        for load in loads:
            load.start()
        wkv_gather.advance(1)
        wq_gather.begin()
        loads[0].wait()
        gain = gain1_ref[...]
        step_rows = count // 4

        def norm_one(i, _):
            rows = pl.ds(pl.multiple_of(i * step_rows, step_rows), step_rows)
            a1_ref[rows] = normed(x_ref[rows].astype(F32), gain)[2]
            return 0

        lax.fori_loop(0, 4, norm_one, 0)
        a1_store = pltpu.make_async_copy(a1_ref, a1_in, ssem.at[0])
        a1_store.start()
        for load in loads[1:]:
            load.wait()
        for own in owns:
            own.start()

        wkv_gather.settle(1)
        for s in range(2, far + 1):
            wkv_gather.advance(s)
            wkv_gather.settle(s)
        for s in range(1, far + 1):
            wkv_gather.complete(s)
        for s in range(0, far + 1):
            wkv_gather.all_from_partner(s)
        owns[0].wait()
        wkv_load = pltpu.make_async_copy(wkv_ref, wkv, wsem.at[0])
        wkv_load.start()
        wkv_load.wait()
        pairs = matmul(a1_ref[...], wkv[...].reshape(width, 2 * key_cols))
        cosine, sine = turn_ref[0], turn_ref[1]
        for tile in range(2 * key_cols // LANES):
            part = pairs[:, tile * LANES : (tile + 1) * LANES]
            which, at = tile * LANES // key_cols, tile * LANES % key_cols
            if which == 0:
                part = part * cosine + turned(part) * sine
            kv[ctx, which, :, at : at + LANES] = part.astype(BF16)

        def kv_copy(source, target, step):
            return pltpu.make_async_remote_copy(
                src_ref=kv.at[source],
                dst_ref=kv.at[source],
                send_sem=kv_send.at[step - 1],
                recv_sem=kv_recv.at[step - 1],
                device_id={"ctx": target},
                device_id_type=MESH,
            )

        for step in range(1, ctx_n):
            kv_copy(ctx, lax.rem(ctx + step, ctx_n), step).start()

        def wq_load(f, slot):
            return pltpu.make_async_copy(wq_ref.at[f], wbuf.at[slot], wsem.at[slot])

        def add_queries(blocks, first):
            for i, f in enumerate(blocks):
                wq_load(f, i).start()

            def one(i, _):
                f = pick(i, blocks)
                wq_load(f, i).wait()
                left = a1_ref[:, pl.ds(pl.multiple_of(f * shard, shard), shard)]
                acc[...] += matmul(left, wbuf[i])
                return 0

            if first:
                acc[...] = jnp.zeros_like(acc)
            lax.fori_loop(0, len(blocks), one, 0)

        for own in owns[1:]:
            own.wait()
        wq_gather.all_from_partner(0)
        add_queries(wq_gather.blocks(0), True)
        for s in range(1, far + 1):
            wq_gather.advance(s)
            if s == max(far - 1, 1):
                wout_gather.begin()
            wq_gather.settle(s)
            wq_gather.complete(s)
            wq_gather.all_from_partner(s)
            add_queries(wq_gather.blocks(s), False)

        def turn_tile(j, _):
            at = pl.ds(pl.multiple_of(j * LANES, LANES), LANES)
            part = acc[:, at]
            q_ref[:, at] = (part * turn_ref[0] + turned(part) * turn_ref[1]).astype(BF16)
            return 0

        lax.fori_loop(0, width // LANES, turn_tile, 0)
        a1_store.wait()
        q_store = pltpu.make_async_copy(q_ref, q_in, ssem.at[0])
        q_store.start()
        for step in range(1, ctx_n):
            kv_copy(ctx, lax.rem(ctx + step, ctx_n), step).wait_send()
            sender = lax.rem(ctx - step + ctx_n, ctx_n)
            kv_copy(sender, sender, step).wait_recv()

        lse_ref[...] = jnp.zeros_like(lse_ref)

        def groups(lo, hi):
            def body(group, _):
                spread_heads(kv, 0, kz, group)
                spread_heads(kv, 1, vz, group)
                attend_group(group, q_ref, kz, vz, mask_ref, o_ref, lse_ref)
                return 0

            lax.fori_loop(lo, hi, body, 0)

        groups(0, 2)
        for s in range(1, far):
            wout_gather.advance(s)
            if s < far - 1:
                wout_gather.settle(s)
        cot_gather.begin()
        groups(2, KV)
        q_store.wait()
        stores = [
            pltpu.make_async_copy(o_ref, o_in, isem.at[0]),
            pltpu.make_async_copy(lse_ref, lse_in, isem.at[1]),
        ]
        for store in stores:
            store.start()
        def wout_load(f, slot):
            return pltpu.make_async_copy(wout_ref.at[f], obuf.at[slot], wsem.at[slot])

        for s in range(0, far + 1):
            if s == 0:
                for late in range(max(far - 1, 1), far + 1):
                    if late == far:
                        wout_gather.advance(late)
                    wout_gather.settle(late)
            if s:
                wout_gather.complete(s)
            wout_gather.all_from_partner(s)
            blocks = wout_gather.blocks(s)
            for i in range(len(blocks)):
                wout_load(blocks[i], i).start()

            def project(i, _, blocks=blocks):
                f = pick(i, blocks)
                wout_load(f, i).wait()
                at = pl.ds(pl.multiple_of(f * shard, shard), shard)
                dh1[:, at] = x_ref[:, at].astype(F32) + matmul(o_ref[...], obuf[i])
                return 0

            lax.fori_loop(0, len(blocks), project, 0)
        gain = gain2_ref[...]

        def norm_two(i, _):
            rows = pl.ds(pl.multiple_of(i * step_rows, step_rows), step_rows)
            a1_ref[rows] = normed(dh1[rows], gain)[2]
            return 0

        lax.fori_loop(0, 4, norm_two, 0)
        a2_store = pltpu.make_async_copy(a1_ref, rows_all.at[fsdp], ssem.at[0])
        a2_store.start()
        h1_store = pltpu.make_async_copy(dh1, h1_ref, ssem.at[1])
        h1_store.start()
        a2_store.wait()
        gather.begin()
        h1_store.wait()
        for store in stores:
            store.wait()
        wkv_gather.end()
        wq_gather.end()
        wout_gather.end()

    rows_type = pltpu.VMEM((count, width), BF16)
    pl.run_scoped(
        forward,
        rows_type,
        rows_type,
        pltpu.VMEM(wkv_ref.shape, BF16),
        pltpu.VMEM((count, width), F32),
        pltpu.VMEM((4,) + wq_ref.shape[1:], BF16),
        rows_type,
        rows_type,
        pltpu.VMEM((2, 2 * keys, LANES), BF16),
        pltpu.VMEM((2, 2 * keys, LANES), BF16),
        pltpu.VMEM(mask_in.shape, F32),
        pltpu.VMEM(turn_in.shape, F32),
        pltpu.VMEM(lse_in.shape, F32),
        pltpu.VMEM((4,) + wout_ref.shape[1:], BF16),
    )

    def ring_sum(partial, rows, wide, sems, first=0):
        return RingSum(ring, partial, arena, rows, wide, sems, first)

    def feed_forward(wgate, wup, wdown, hb, abuf, cbuf, stage):
        loads = [
            pltpu.make_async_copy(wdown_ref, wdown, isem.at[4]),
            pltpu.make_async_copy(wgate_ref, wgate, isem.at[5]),
            pltpu.make_async_copy(wup_ref, wup, isem.at[6]),
        ]
        for load in loads:
            load.start()

        def each(source, blocks, body):
            def fetch(f, slot):
                return pltpu.make_async_copy(source.at[f], abuf.at[slot], isem.at[slot])

            for i, f in enumerate(blocks):
                fetch(f, i).start()

            def step(i, _):
                f = pick(i, blocks)
                fetch(f, i).wait()
                body(f, i)
                return 0

            lax.fori_loop(0, len(blocks), step, 0)

        def dhid(f, slot):
            hb[2, f] = through(abuf[slot], wdown[...]).astype(BF16)

        def gates(f, slot):
            rows = abuf[slot]
            hidden, dgate, dup = gate_back(
                hb[2, f].astype(F32), through(rows, wgate[...]), through(rows, wup[...])
            )
            hb[0, f] = dgate
            hb[1, f] = dup
            hb[2, f] = hidden

        for load in loads:
            load.wait()
        for s in range(far + 1):
            if s == 1:
                cot_gather.advance(s)
            if s:
                cot_gather.settle(s)
            cot_gather.all_from_partner(s)
            each(cot_ref, cot_gather.blocks(s), dhid)
            if s:
                gather.advance(s)
                if s < far:
                    cot_gather.advance(s + 1)
                gather.settle(s)
            gather.all_from_partner(s)
            each(rows_all, gather.blocks(s), gates)
        cot_gather.end()
        gather.end()

        wide = 2 * LANES
        per_kind = width // wide
        total = 3 * per_kind

        def chunk_load(m, start):
            slot = lax.rem(m, 2)
            at = pl.multiple_of(lax.rem(m, per_kind) * wide, wide)
            for source, use in ((rows_all, m < 2 * per_kind), (cot_ref, m >= 2 * per_kind)):
                copy = pltpu.make_async_copy(
                    source.at[:, :, pl.ds(at, wide)], cbuf.at[slot], wsem.at[slot]
                )
                pl.when(use)(copy.start if start else copy.wait)

        def chunk_store(m):
            slot = lax.rem(m, 2)
            return pltpu.make_async_copy(
                stage.at[slot], gz_ref.at[pl.ds(2 * m, 2)], ssem.at[slot]
            )

        def gradients(m, lo):
            slot = lax.rem(m, 2)
            pl.when(m + 1 < total)(lambda: chunk_load(jnp.minimum(m + 1, total - 1), True))
            chunk_load(m, False)
            right = cbuf[slot].reshape(fsdp_n * count, wide)
            left = hb[m // per_kind].reshape(fsdp_n * count, local)
            out = across(left, right).astype(BF16)
            pl.when(m >= lo + 2)(lambda: chunk_store(jnp.maximum(m - 2, 0)).wait())
            stage[slot, 0] = out[:, :LANES]
            stage[slot, 1] = out[:, LANES:]
            chunk_store(m).start()

        def run(lo, hi, every=0):
            start = clock[0]

            def body(m, _):
                gradients(m, lo)
                if every:
                    pl.when(lax.rem(m - lo, every) == every - 1)(
                        lambda: line.tick(start + (m - lo) // every)
                    )
                return 0

            lax.fori_loop(lo, hi, body, 0)
            for m in (hi - 2, hi - 1):
                chunk_store(jnp.int32(m)).wait()
            if every:
                clock[0] = start + (hi - lo) // every

        chunk_load(jnp.int32(0), True)
        head = 4
        run(0, head)
        cap[0] = 2 * head - 1
        ticks(3)

        def da2_partial(f, at):
            return matmul(hb[0, f], wgate[:, at]) + matmul(hb[1, f], wup[:, at])

        da2 = ring_sum(da2_partial, count, width, da2_sems)
        da2.pair_all(lambda i: ticks(1))
        middle = head + (total - head) // 2
        run(head, middle, 2)
        da2.launch()
        run(middle, total, 2)
        cap[0] = line.first
        ticks(2)
        own_cot = pltpu.make_async_copy(cot_ref.at[fsdp], abuf.at[0], isem.at[0])
        own_cot.start()
        da2.finish()
        own_cot.wait()
        gain = gain2_ref[...]
        piece = count // 4

        def norm_back(i, acc):
            rows = pl.ds(pl.multiple_of(i * piece, piece), piece)
            hidden = dh1[rows]
            grad = da2.value(rows)
            factor = lax.rsqrt(jnp.mean(hidden * hidden, -1, keepdims=True) + EPSILON)
            unit = hidden * factor
            dh1[rows] = abuf[0, rows].astype(F32) + normed_back(unit, factor, grad, gain)
            return acc + jnp.sum(grad * unit, 0, keepdims=True)

        gain2_sum = lax.fori_loop(0, 4, norm_back, jnp.zeros((1, width), F32))
        gslot[fsdp, 1:2] = gain2_sum
        settle()

        def out_partial(f, at):
            return matmul(hb[2, f], wdown[:, at])

        mlp_out = ring_sum(out_partial, count, width, out_sems)
        mlp_out.pair_all(lambda i: ticks(1))
        holder.append(mlp_out)

    holder = []
    pl.run_scoped(
        feed_forward,
        pltpu.VMEM((local, width), BF16),
        pltpu.VMEM((local, width), BF16),
        pltpu.VMEM((local, width), BF16),
        pltpu.VMEM((3, fsdp_n, count, local), BF16),
        pltpu.VMEM((4, count, width), BF16),
        pltpu.VMEM((2, fsdp_n, count, 2 * LANES), BF16),
        pltpu.VMEM((2, 2, local, LANES), BF16),
    )
    mlp_out = holder[0]

    def attention_back(
        q_ref, o_ref, do_ref, a1_ref, dhb_ref, lse_ref, mask_ref, turn_ref,
        h1_buf, obuf, wbuf, wkv, kz, vz, dk_acc, dv_acc, gqkv, dkv,
    ):
        loads = [
            pltpu.make_async_copy(src, dst, isem.at[i])
            for i, (src, dst) in enumerate(
                [
                    (q_in, q_ref),
                    (o_in, o_ref),
                    (a1_in, a1_ref),
                    (lse_in, lse_ref),
                    (mask_in, mask_ref),
                    (turn_in, turn_ref),
                ]
            )
        ]

        def wout_load(f):
            return pltpu.make_async_copy(wout_ref.at[f], obuf.at[f % 2], wsem.at[f % 2])

        wout_load(0).start()
        for load in loads:
            load.start()
        dhb_ref[...] = dh1[...].astype(BF16)
        for f in range(fsdp_n):
            if f + 1 < fsdp_n:
                wout_load(f + 1).start()
            wout_load(f).wait()
            term = through(dhb_ref[:, f * shard : (f + 1) * shard], obuf[f % 2])
            h1_buf[...] = term if f == 0 else h1_buf[...] + term
        do_ref[...] = h1_buf[...].astype(BF16)
        h1_load = pltpu.make_async_copy(h1_ref, h1_buf, ssem.at[0])
        h1_load.start()
        ticks(2)
        mlp_out.launch()
        for load in loads:
            load.wait()

        step_keys = min(keys, 4 * LANES)

        def piece(par, q4, do4, lse, delta, at, mask, grad_q):
            span = pl.ds(at, step_keys)
            k_part = kz[par, span]
            v_part = vz[par, span]
            scores = through(q4, k_part)
            if mask is not None:
                scores = scores + mask
            probs = jnp.exp(scores - lse)
            dprob = through(do4, v_part)
            dscore = (probs * (dprob - delta)).astype(BF16)
            dk_acc[par, span] += across(dscore, q4)
            dv_acc[par, span] += across(probs.astype(BF16), do4)
            return grad_q + matmul(dscore, k_part)

        def group_step(group, rb):
            rows = pl.ds(rb * block, block)
            q4 = stacked(q_ref, rows, group) * jnp.asarray(scale, BF16)
            do4 = stacked(do_ref, rows, group)
            prod = do4.astype(F32) * stacked(o_ref, rows, group).astype(F32)
            lse_all = lse_ref[rb]
            grad_q = jnp.zeros((PAIRS * block, LANES), F32)
            for par in range(2):
                lse = jnp.sum(
                    jnp.where(lanes_of(lse_all.shape) == 2 * group + par, lse_all, 0.0),
                    -1,
                    keepdims=True,
                )
                delta = jnp.sum(
                    jnp.where(lanes_of(prod.shape) // HD == par, prod, 0.0), -1, keepdims=True
                )
                for at in range(0, (rb + 1) * keys, step_keys):
                    mask = None
                    if at >= rb * keys:
                        mask = mask_ref[rb, :, pl.ds(at - rb * keys, step_keys)]
                        mask = jnp.concatenate([mask] * PAIRS, 0)
                    grad_q = piece(par, q4, do4, lse, delta, at, mask, grad_q)
            grad_q = grad_q * scale
            cosine, sine = turn_ref[0, rows], turn_ref[1, rows]
            for j in range(PAIRS):
                part = grad_q[j * block : (j + 1) * block]
                at = pl.multiple_of((group * PAIRS + j) * LANES, LANES)
                gqkv[rows, pl.ds(at, LANES)] = (part * cosine - turned(part) * sine).astype(BF16)

        def dkv_copy(owner, tile, step):
            return pltpu.make_async_remote_copy(
                src_ref=dkv.at[owner, tile],
                dst_ref=dkv_in.at[ctx, tile],
                send_sem=dkv_send.at[step, tile],
                recv_sem=dkv_recv.at[step, tile],
                device_id={"ctx": owner},
                device_id_type=MESH,
            )

        def attention(lo, hi):
            start = clock[0]

            def body(group, _):
                spread_heads(kv, 0, kz, group)
                spread_heads(kv, 1, vz, group)
                dk_acc[...] = jnp.zeros_like(dk_acc)
                dv_acc[...] = jnp.zeros_like(dv_acc)
                for rb in range(2):
                    group_step(group, rb)
                    line.tick(start + (group - lo) * 2 + rb)
                tile = group // 2
                for which, acc in enumerate((dk_acc, dv_acc)):
                    for part in range(ctx_n):
                        for rb in range(2):
                            span = pl.ds(rb * keys + part * block, block)
                            both = jnp.where(
                                lanes_of((block, LANES)) < HD, acc[0, span], acc[1, span]
                            )
                            both = both + roll_lanes(both, HD)
                            there = (part, tile, which, pl.ds(rb * block, block))
                            mine = lanes_of((block, LANES)) // HD == lax.rem(group, 2)
                            dkv[there] = jnp.where(mine, both.astype(BF16), dkv[there])
                return 0

            lax.fori_loop(lo, hi, body, 0)
            clock[0] = start + (hi - lo) * 2

        def send_dkv(tile):
            for step in range(1, ctx_n):
                dkv_copy(lax.rem(ctx + step, ctx_n), tile, step - 1).start()

        attention(0, 2)
        send_dkv(0)
        mlp_out.finish()
        h1_load.wait()

        def add_out(rows):
            h1_buf[rows] = h1_buf[rows] + mlp_out.value(rows)

        mlp_out.by_rows(add_out)
        settle()

        def output_partial(f, at):
            return across(dhb_ref[:, pl.ds(pl.multiple_of(f * shard, shard), shard)], o_ref[:, at])

        ysum = ring_sum(output_partial, shard, width, ysems)
        ysum.pair_all(lambda i: ticks(1) if i else None)
        attention(2, 3)
        ysum.launch()
        attention(3, 4)
        send_dkv(1)
        ticks(3)
        do_ref[...] = h1_buf[...].astype(BF16)
        result_copy = pltpu.make_async_copy(do_ref, result_out, isem.at[0])
        result_copy.start()
        ysum.finish()

        def keep_output(rows):
            az[rows, :width] = ysum.value(rows).astype(BF16)

        ysum.by_rows(keep_output)
        cap[0] = line.first + width // (2 * LANES)
        settle()
        x_load = pltpu.make_async_copy(x_in, q_ref, isem.at[1])
        x_load.start()

        def query_partial(f, at):
            return across(a1_ref[:, pl.ds(pl.multiple_of(f * shard, shard), shard)], gqkv[:, at])

        def pair_partial(f, at):
            return across(
                a1_ref[:, pl.ds(pl.multiple_of(f * shard, shard), shard)],
                gqkv[:, pl.ds(width, 2 * key_cols)],
            )

        xsum = ring_sum(query_partial, shard, width, xsems)
        xsum.pair_all(lambda i: ticks(1))
        for step in range(1, ctx_n):
            for tile in range(KV // 2):
                dkv_copy(lax.rem(ctx + step, ctx_n), tile, step - 1).wait_send()
                sender = lax.rem(ctx - step + ctx_n, ctx_n)
                pltpu.make_async_remote_copy(
                    src_ref=dkv.at[sender, tile],
                    dst_ref=dkv_in.at[sender, tile],
                    send_sem=dkv_send.at[step - 1, tile],
                    recv_sem=dkv_recv.at[step - 1, tile],
                    device_id={"ctx": sender},
                    device_id_type=MESH,
                ).wait_recv()
        cosine, sine = turn_ref[0], turn_ref[1]
        for tile in range(KV // 2):
            for which in range(2):
                part = dkv[ctx, tile, which].astype(F32)
                for step in range(1, ctx_n):
                    part = part + dkv_in[lax.rem(ctx + step, ctx_n), tile, which].astype(F32)
                if which == 0:
                    part = part * cosine - turned(part) * sine
                at = width + which * key_cols + tile * LANES
                gqkv[:, at : at + LANES] = part.astype(BF16)

        kvsum = ring_sum(pair_partial, shard, 2 * key_cols, kvsems, width)
        kvsum.pair_all()
        ticks(2)
        xsum.launch()
        kvsum.launch()
        ticks(2)

        def weight_copies(f):
            slot = f % 2
            return (
                pltpu.make_async_copy(wq_ref.at[f], wbuf.at[slot], wsem.at[slot]),
                pltpu.make_async_copy(wkv_ref.at[f], wkv.at[slot], wsem.at[2 + slot]),
            )

        for copy in weight_copies(0):
            copy.start()
        for f in range(fsdp_n):
            if f + 1 < fsdp_n:
                for copy in weight_copies(f + 1):
                    copy.start()
            for copy in weight_copies(f):
                copy.wait()
            h1_buf[:, f * shard : (f + 1) * shard] = through(
                gqkv[:, :width], wbuf[f % 2]
            ) + through(gqkv[:, width:], wkv[f % 2])
            if f % (fsdp_n // 4) == 0:
                ticks(1)
        ticks(1)
        x_load.wait()
        gain = gain1_ref[...]
        piece_rows = count // 4

        def norm_back(i, acc):
            rows = pl.ds(pl.multiple_of(i * piece_rows, piece_rows), piece_rows)
            x = q_ref[rows].astype(F32)
            grad = h1_buf[rows]
            factor = lax.rsqrt(jnp.mean(x * x, -1, keepdims=True) + EPSILON)
            unit = x * factor
            o_ref[rows] = (dh1[rows] + normed_back(unit, factor, grad, gain)).astype(BF16)
            return acc + jnp.sum(grad * unit, 0, keepdims=True)

        gslot[fsdp, 0:1] = lax.fori_loop(0, 4, norm_back, jnp.zeros((1, width), F32))
        gtok_copy = pltpu.make_async_copy(o_ref, gtok_out, isem.at[2])
        gtok_copy.start()

        def gain_copy(slots, axis, here, step, sems):
            n = fsdp_n if axis == "fsdp" else ctx_n
            return pltpu.make_async_remote_copy(
                src_ref=slots.at[here],
                dst_ref=slots.at[here],
                send_sem=sems[0].at[step - 1],
                recv_sem=sems[1].at[step - 1],
                device_id={axis: lax.rem((fsdp if axis == "fsdp" else ctx) + step, n)},
                device_id_type=MESH,
            )

        def exchange(slots, axis, n, me, sems):
            for step in range(1, n):
                gain_copy(slots, axis, me, step, sems).start()
            for step in range(1, n):
                gain_copy(slots, axis, me, step, sems).wait_send()
                gain_copy(slots, axis, lax.rem(me - step + n, n), step, sems).wait_recv()
            total = slots[0]
            for i in range(1, n):
                total = total + slots[i]
            return total

        ticks(1)
        cslot[ctx] = exchange(gslot, "fsdp", fsdp_n, fsdp, (gain_send, gain_recv))
        ticks(2)
        gains_ref[...] = exchange(cslot, "ctx", ctx_n, ctx, (cgain_send, cgain_recv))

        ticks(2)
        xsum.finish()
        kvsum.finish()

        def keep_query(rows):
            az[rows, width : 2 * width] = xsum.value(rows).astype(BF16)
            az[rows, 2 * width :] = kvsum.value(rows).astype(BF16)

        xsum.by_rows(keep_query)
        result_copy.wait()
        gtok_copy.wait()

    pl.run_scoped(
        attention_back,
        rows_type,
        rows_type,
        rows_type,
        rows_type,
        rows_type,
        pltpu.VMEM(lse_in.shape, F32),
        pltpu.VMEM(mask_in.shape, F32),
        pltpu.VMEM(turn_in.shape, F32),
        pltpu.VMEM((count, width), F32),
        pltpu.VMEM((2,) + wout_ref.shape[1:], BF16),
        pltpu.VMEM((2,) + wq_ref.shape[1:], BF16),
        pltpu.VMEM((2,) + wkv_ref.shape[1:], BF16),
        pltpu.VMEM((2, 2 * keys, LANES), BF16),
        pltpu.VMEM((2, 2 * keys, LANES), BF16),
        pltpu.VMEM((2, 2 * keys, LANES), F32),
        pltpu.VMEM((2, 2 * keys, LANES), F32),
        pltpu.VMEM((count, cols), BF16),
        pltpu.VMEM(dkv_in.shape, BF16),
    )
    cap[0] = line.ticks
    ticks(line.ticks - clock[0])


def layer(x, cot, wq, wkv, w_out, w_gate, w_up, w_down, mask, turn, gain_one, gain_two):
    ctx_n = lax.axis_size("ctx")
    fsdp_n = lax.axis_size("fsdp")
    count, width = x.shape
    local = w_gate.shape[0]
    shard = wq.shape[0]
    cols = wq.shape[1] + wkv.shape[1]
    chips = fsdp_n // 2
    far = chips // 2
    vmem = pl.BlockSpec(memory_space=pltpu.VMEM)
    hbm = pl.BlockSpec(memory_space=pl.ANY)
    dma = pltpu.SemaphoreType.DMA
    regular = pltpu.SemaphoreType.REGULAR
    zbuf = pltpu.VMEM((SLOTS, local, LANES), BF16)
    scratch = (
        [zbuf] * 5
        + [
            pltpu.VMEM((shard, cols + width), BF16),
            pltpu.VMEM((2 + chips + 2 * far, max(count, shard), cols), BF16),
            pltpu.VMEM((count, width), F32),
            pltpu.VMEM((ctx_n, KV // 2, 2, count, LANES), BF16),
            pltpu.VMEM((ctx_n, 2, count, KV * HD), BF16),
            pltpu.VMEM((fsdp_n, 2, width), F32),
            pltpu.VMEM((ctx_n, 2, width), F32),
        ]
        + [dma((SLOTS,))] * 5
        + [dma((SLOTS, 2)), regular, regular]
        + gather_sems(chips) * 5
        + sum_sems(chips) * 5
        + [
            dma((ctx_n - 1, KV // 2)),
            dma((ctx_n - 1, KV // 2)),
            dma((ctx_n - 1,)),
            dma((ctx_n - 1,)),
            dma((fsdp_n - 1,)),
            dma((fsdp_n - 1,)),
            dma((ctx_n - 1,)),
            dma((ctx_n - 1,)),
            dma((4,)),
            dma((9,)),
            dma((2,)),
            regular((4,)),
        ]
    )

    def bf16(*shape):
        return jax.ShapeDtypeStruct(shape, BF16)

    return pl.pallas_call(
        functools.partial(layer_kernel, (ctx_n, fsdp_n)),
        out_shape=(
            bf16(count, width),
            bf16(count, width),
            jax.ShapeDtypeStruct((2, width), F32),
            bf16(local, width),
            bf16(local, width),
            bf16(local, width),
            bf16(shard, cols),
            bf16(shard, width),
            bf16(fsdp_n, count, width),
            bf16(3 * width // LANES, local, LANES),
            bf16(fsdp_n, *wq.shape),
            bf16(fsdp_n, *wkv.shape),
            bf16(fsdp_n, *w_out.shape),
            bf16(fsdp_n, count, width),
            bf16(count, width),
            bf16(count, width),
            bf16(count, width),
            jax.ShapeDtypeStruct((count, width), F32),
            jax.ShapeDtypeStruct((2, PAIRS * count // 2, LANES), F32),
        ),
        in_specs=[hbm] * 10 + [vmem] * 2,
        out_specs=(hbm, hbm, vmem) + (hbm,) * 16,
        scratch_shapes=scratch,
        compiler_params=pltpu.CompilerParams(
            collective_id=1, has_side_effects=True, vmem_limit_bytes=VMEM_LIMIT
        ),
        name="layer",
    )(x, cot, wq, wkv, w_out, w_gate, w_up, w_down, mask, turn, gain_one, gain_two)[:8]


def widen_kernel(
    swap_ref,
    gate_in,
    up_in,
    down_in,
    query_in,
    pair_in,
    output_in,
    result_in,
    gtok_in,
    gate_out,
    up_out,
    down_out,
    query_out,
    key_out,
    value_out,
    output_out,
    result_out,
    gtok_out,
):
    gate_out[...] = gate_in[...].astype(F32)
    up_out[...] = up_in[...].astype(F32)
    down_out[...] = down_in[...].astype(F32)
    query_out[...] = query_in[...].astype(F32)
    output_out[...] = output_in[...].astype(F32).T

    @pl.when(pl.program_id(0) == 0)
    def _():
        half = key_out.shape[1]
        key_out[...] = pair_in[:, :half].astype(F32)
        value_out[...] = pair_in[:, half:].astype(F32)

    @pl.when(pl.program_id(0) < 2)
    def _():
        result_out[...] = result_in[...]
        gtok_out[...] = gtok_in[...]


def widen(swap, gate, up, down, query, output, result, gtok):
    local, width = gate.shape
    shard = query.shape[0]
    count = result.shape[0]
    key_cols = KV * HD
    wide = 2 * LANES

    def columns(rows):
        return pl.BlockSpec((rows, wide), lambda i, swap: (0, i))

    def whole(*shape, at=0):
        return pl.BlockSpec(shape, lambda i, swap: (0, at))

    rows_in = pl.BlockSpec(
        (count // 2, width), lambda i, swap: (lax.rem(jnp.minimum(i, 1) + swap[0], 2), 0)
    )
    rows_out = pl.BlockSpec((count // 2, width), lambda i, swap: (jnp.minimum(i, 1), 0))

    def f32(*shape):
        return jax.ShapeDtypeStruct(shape, F32)

    return pl.pallas_call(
        widen_kernel,
        grid_spec=pltpu.PrefetchScalarGridSpec(
            num_scalar_prefetch=1,
            grid=(width // wide,),
            in_specs=[columns(local)] * 3
            + [
                columns(shard),
                whole(shard, 2 * key_cols, at=width // (2 * key_cols)),
                columns(shard),
                rows_in,
                rows_in,
            ],
            out_specs=[columns(local)] * 3
            + [
                columns(shard),
                whole(shard, key_cols),
                whole(shard, key_cols),
                pl.BlockSpec((wide, shard), lambda i, swap: (i, 0)),
                rows_out,
                rows_out,
            ],
        ),
        out_shape=[f32(local, width)] * 3
        + [
            f32(shard, width),
            f32(shard, key_cols),
            f32(shard, key_cols),
            f32(width, shard),
            jax.ShapeDtypeStruct((count, width), BF16),
            jax.ShapeDtypeStruct((count, width), BF16),
        ],
        compiler_params=pltpu.CompilerParams(vmem_limit_bytes=VMEM_LIMIT),
        name="widen",
    )(swap, gate, up, down, query, query, output, result, gtok)


def shards(
    tokens,
    cotangent,
    block_table,
    gain_attn,
    w_query,
    w_key,
    w_value,
    w_output,
    gain_mlp,
    w_gate,
    w_up,
    w_down,
):
    ctx_n = lax.axis_size("ctx")
    ctx = lax.axis_index("ctx")
    count, width = tokens.shape[1:]
    block = count // 2

    table = block_table.reshape(ctx_n, 2)
    lower, upper = jnp.min(table, 1), jnp.max(table, 1)
    owned = table[ctx]
    swap = owned[0] > owned[1]

    def ordered(rows):
        return jnp.where(swap, jnp.concatenate([rows[block:], rows[:block]], 0), rows)

    offsets = jnp.arange(block, dtype=jnp.int32)
    spots = jnp.stack([lower, upper])[:, :, None] * block + offsets
    own_spots = spots[:, ctx]
    key_spots = spots.reshape(2, -1)
    mask = jnp.where(own_spots[:, :, None] >= key_spots[:, None, :], 0.0, NEGATIVE).astype(F32)
    freqs = 10000.0 ** (-jnp.arange(HD // 2, dtype=F32) / (HD // 2))
    angle = own_spots.reshape(-1).astype(F32)[:, None] * freqs[None, :]
    angle = jnp.concatenate([angle] * (LANES * 2 // HD), -1)
    turn = jnp.stack([jnp.cos(angle), jnp.sin(angle)])

    rows_in = ordered(tokens[0])
    grad_out = ordered(cotangent[0])

    result, grad_tokens, gains, gate_sum, up_sum, down_sum, query_sum, output_sum = layer(
        rows_in,
        grad_out,
        w_query,
        jnp.concatenate([w_key, w_value], 1),
        w_output,
        w_gate.T,
        w_up.T,
        w_down,
        mask,
        turn,
        gain_attn[None],
        gain_mlp[None],
    )
    grad_gate, grad_up, grad_down, grad_query, grad_key, grad_value, grad_output, result, grad_tokens = (
        widen(
            swap.astype(jnp.int32)[None],
            gate_sum,
            up_sum,
            down_sum,
            query_sum,
            output_sum,
            result,
            grad_tokens,
        )
    )
    return (
        result[None],
        grad_tokens[None],
        grad_query,
        grad_key,
        grad_value,
        grad_output,
        grad_gate.T,
        grad_up.T,
        grad_down,
        gains[0],
        gains[1],
    )


def solution(mesh):
    in_specs = (
        P("fsdp", "ctx", None),
        P("fsdp", "ctx", None),
        P(),
        P(),
        P("fsdp", None),
        P("fsdp", None),
        P("fsdp", None),
        P(None, "fsdp"),
        P(),
        P(None, "fsdp"),
        P(None, "fsdp"),
        P("fsdp", None),
    )
    out_specs = (
        P("fsdp", "ctx", None),
        P("fsdp", "ctx", None),
        P("fsdp", None),
        P("fsdp", None),
        P("fsdp", None),
        P(None, "fsdp"),
        P(None, "fsdp"),
        P(None, "fsdp"),
        P("fsdp", None),
        P(),
        P(),
    )
    return jax.shard_map(shards, mesh=mesh, in_specs=in_specs, out_specs=out_specs, check_vma=False)
```
